32 devices in a mesh: grp: 4 (over y, core), wide: 8 (over z, x).
Axes of the slice: x: 2, y: 2, z: 4, core: 2. Of those that a mesh axis runs over, the one named last changes fastest.
Arguments:
- features: bfloat16 [6144, 2304], P(('grp', 'wide')), may hold values from -6 to 6
- labels: int32 [6144], P(('grp', 'wide')), may hold values from 0 to 9
- counts: int32 [32], P(('grp', 'wide')), may hold values from 64 to 192, as said below
- weight6: float32 [2304, 384], P('wide'), may hold values from -0.125 to 0.125
- weight7: float32 [384, 192], P('wide'), may hold values from -0.3125 to 0.3125
- weight8: float32 [192, 10], P('wide'), may hold values from -1.25 to 1.25
- moment6: float32 [2304, 384], P('wide'), may hold values from -0.00390625 to 0.00390625
- moment7: float32 [384, 192], P('wide'), may hold values from -0.0068359375 to 0.0068359375
- moment8: float32 [192, 10], P('wide'), may hold values from -0.01171875 to 0.01171875
- resid6: float32 [73728, 384], P(('grp', 'wide')), may hold values from -4 to 4
- resid7: float32 [12288, 192], P(('grp', 'wide')), may hold values from -8 to 8
- resid8: float32 [6144, 10], P(('grp', 'wide')), may hold values from -12 to 12
- noise6: int32 [73728, 384], P(('grp', 'wide')), may hold values from 0 to 1023
- noise7: int32 [12288, 192], P(('grp', 'wide')), may hold values from 0 to 1023
- noise8: int32 [6144, 10], P(('grp', 'wide')), may hold values from 0 to 1023
- biases: float32 [586], replicated, may hold values from -1.75 to 1.75
- bias_first: float32 [586], replicated
- bias_second: float32 [586], replicated
Outputs:
- new_weight6: float32 [2304, 384], P('wide')
- new_weight7: float32 [384, 192], P('wide')
- new_weight8: float32 [192, 10], P('wide')
- low_weight6: bfloat16 [2304, 384], P('wide')
- low_weight7: bfloat16 [384, 192], P('wide')
- low_weight8: bfloat16 [192, 10], P('wide')
- new_moment6: float32 [2304, 384], P('wide')
- new_moment7: float32 [384, 192], P('wide')
- new_moment8: float32 [192, 10], P('wide')
- new_resid6: float32 [73728, 384], P(('grp', 'wide'))
- new_resid7: float32 [12288, 192], P(('grp', 'wide'))
- new_resid8: float32 [6144, 10], P(('grp', 'wide'))
- new_biases: float32 [586], replicated
- new_bias_first: float32 [586], replicated
- new_bias_second: float32 [586], replicated
- loss_sum: float32 [], replicated
- image_count: float32 [], replicated
The draws below stay inside these ranges and needn't reach their ends.
Inputs may be any that keep to these rules, and one draw needn't show every extreme that they name: `counts`: varies from worker to worker; some worker holds exactly 192 images and some exactly 64.
All inputs are finite; a program needn't handle non-finite values. Where the reference program divides by a largest or mean magnitude, that divisor is 1e-20 or more.
Results may differ from the reference program's by a relative error of at most 0.011.
Values may be sent and summed in bfloat16 or wider, within the bound.
No kernel may reach another device: no remote copies, remote signals or barrier semaphores. Data moves between devices by JAX's collectives and lax.ppermute only.
A program may use at most 128 MiB of HBM per device.

```python
import jax
import jax.numpy as jnp
from jax import lax

IN = 2304
H1 = 384
H2 = 192
C = 10
ROWS_DEV = 192
NS_STEPS = 5
ADAM_STEP = 10
WORKERS = 32
N_GRP = 4
N_WIDE = 8


def draw_counts(key, part):
    key = jax.random.fold_in(key, 3)
    position = jnp.arange(WORKERS, dtype=jnp.int32)
    grp_pos = position // N_WIDE
    wide_pos = position % N_WIDE
    low_count = ROWS_DEV // 3
    spread = ROWS_DEV - low_count
    linear = low_count + spread * (wide_pos * (N_GRP - 1) + grp_pos * (N_WIDE - 1)) // (2 * (N_WIDE - 1) * (N_GRP - 1))
    jitter = jax.random.randint(key, (WORKERS,), -(ROWS_DEV // 24), ROWS_DEV // 24 + 1)
    result = jnp.clip(linear + jitter, low_count, ROWS_DEV)
    return result.at[0].set(low_count).at[WORKERS - 1].set(ROWS_DEV).astype(jnp.int32)


def bias_scales():
    image_guess = 0.67 * ROWS_DEV * WORKERS
    pieces = [jnp.full((H1,), 0.066, jnp.float32), jnp.full((H2,), 0.19, jnp.float32), jnp.full((C,), 0.3, jnp.float32)]
    return jnp.concatenate(pieces) / jnp.sqrt(jnp.float32(image_guess))


def draw_bias_first(key, part):
    key = jax.random.fold_in(key, 7)
    return 0.11 * bias_scales() * jax.random.normal(key, (H1 + H2 + C,), jnp.float32)


def draw_bias_second(key, part):
    key = jax.random.fold_in(key, 5)
    factor = jax.random.uniform(key, (H1 + H2 + C,), jnp.float32, 1.0, 4.0)
    return 0.001 * factor * bias_scales() ** 2


def set_ends(values, rng, low, top_value):
    longest = values.shape.index(max(values.shape))
    spots = []
    for shift in (0, 1):
        where = [jax.random.randint(jax.random.fold_in(rng, axis), (), 0, length) for axis, length in enumerate(values.shape)]
        where[longest] = (where[longest] + shift) % values.shape[longest]
        spots.append(tuple(where))
    return values.at[spots[0]].set(low).at[spots[1]].set(top_value)


def level_of(rng, shape, cuts, low, top_value):
    def one(dim, blocks):
        heights = jax.random.uniform(jax.random.fold_in(jax.random.fold_in(rng, 6), dim), (blocks,), jnp.float32, low / len(cuts), top_value / len(cuts))
        return jnp.repeat(jnp.exp(heights), shape[dim] // blocks).reshape((-1,) + (1,) * (len(shape) - dim - 1))

    factor_of = one(*cuts[0])
    for cut in cuts[1:]:
        factor_of = factor_of * one(*cut)
    return factor_of


def centred(stream_key, extent, scale, limit, split=(), kind=jnp.bfloat16):
    gain = level_of(stream_key, extent, split, -0.22, 0.18) if split else 1.0
    entries = jax.random.normal(stream_key, extent, jnp.float32) * scale * gain
    return jnp.minimum(jnp.maximum(entries, -limit), limit).astype(kind)


def setup_inputs(seed: int = 0) -> dict:
    streams_of = jax.random.split(jax.random.key(seed), 19)
    return {
        "features": centred(streams_of[0], (WORKERS * ROWS_DEV, IN), 1.0, 6.0, ((0, 32),)),
        "labels": set_ends(jax.random.randint(streams_of[1], (WORKERS * ROWS_DEV,), 0, C), jax.random.fold_in(streams_of[1], 1), 0, C - 1).astype(jnp.int32),
        "counts": draw_counts(jax.random.fold_in(streams_of[18], 71), 0),
        "weight6": centred(streams_of[3], (IN, H1), IN ** -0.5, 0.125, ((0, 8),), jnp.float32),
        "weight7": centred(streams_of[4], (H1, H2), H1 ** -0.5, 0.3125, ((0, 8),), jnp.float32),
        "weight8": centred(streams_of[5], (H2, C), (H2 // 8) ** -0.5, 1.25, ((0, 8),), jnp.float32),
        "moment6": centred(streams_of[6], (IN, H1), (0.7 / (ROWS_DEV * WORKERS ** 0.5)), 0.00390625, ((0, 8),), jnp.float32),
        "moment7": centred(streams_of[7], (H1, H2), (1.3 / (ROWS_DEV * WORKERS ** 0.5)), 0.0068359375, ((0, 8),), jnp.float32),
        "moment8": centred(streams_of[8], (H2, C), (2.0 / (ROWS_DEV * WORKERS ** 0.5)), 0.01171875, ((0, 8),), jnp.float32),
        "resid6": centred(streams_of[9], (WORKERS * IN, H1), 0.7, 4.0, ((0, 32),), jnp.float32),
        "resid7": centred(streams_of[10], (WORKERS * H1, H2), 1.3, 8.0, ((0, 32),), jnp.float32),
        "resid8": centred(streams_of[11], (WORKERS * H2, C), 2.0, 12.0, ((0, 32),), jnp.float32),
        "noise6": set_ends(jax.random.randint(streams_of[12], (WORKERS * IN, H1), 0, 1024), jax.random.fold_in(streams_of[12], 1), 0, 1023).astype(jnp.int32),
        "noise7": set_ends(jax.random.randint(streams_of[13], (WORKERS * H1, H2), 0, 1024), jax.random.fold_in(streams_of[13], 1), 0, 1023).astype(jnp.int32),
        "noise8": set_ends(jax.random.randint(streams_of[14], (WORKERS * H2, C), 0, 1024), jax.random.fold_in(streams_of[14], 1), 0, 1023).astype(jnp.int32),
        "biases": centred(streams_of[15], (H1 + H2 + C,), 0.3, 1.75, (), jnp.float32),
        "bias_first": draw_bias_first(jax.random.fold_in(streams_of[18], 71), 0),
        "bias_second": draw_bias_second(jax.random.fold_in(streams_of[18], 71), 0),
    }


highest = lax.Precision.HIGHEST
smoothing = 0.1
clip_width = 2.5
noise_levels = 1024.0
ramp_slope = 2.0
momentum_decay = 0.95
muon_rate = 0.6
decay_rate = 0.01
coef_a = 3.4445
coef_b = -4.775
coef_c = 2.0315
beta_first = 0.9
beta_second = 0.999
bias_rate = 0.05
adam_eps = 1e-08

@jax.custom_vjp
def low(v):
    return lax.optimization_barrier(v.astype(jnp.bfloat16)).astype(jnp.float32)

@jax.custom_vjp
def low_back(v):
    return v

def low_keep(v):
    return (low(v), None)

def low_pass(kept, grad):
    return (grad,)

def back_keep(v):
    return (v, None)

def back_low(kept, grad):
    return (low(grad),)
low.defvjp(low_keep, low_pass)
low_back.defvjp(back_keep, back_low)

def worker_loss(params, feats, labs, row_mask):
    weight6, weight7, weight8, biases = params
    bias6 = biases[:H1]
    bias7 = biases[H1:H1 + H2]
    bias8 = biases[H1 + H2:]
    hidden = feats.astype(jnp.float32)
    pre6 = low_back(jnp.dot(hidden, low(weight6), precision=highest) + bias6)
    act6 = low(jax.nn.gelu(pre6))
    pre7 = low_back(jnp.dot(act6, low(weight7), precision=highest) + bias7)
    act7 = low(jax.nn.gelu(pre7))
    logits = low_back(jnp.dot(act7, low(weight8), precision=highest) + bias8)
    logp = jax.nn.log_softmax(logits, axis=-1)
    onehot = (labs[:, None] == jnp.arange(C)[None, :]).astype(jnp.float32)
    target = (1.0 - smoothing) * onehot + smoothing / C
    row_loss = -lax.optimization_barrier(jnp.sum(target * logp, axis=-1))
    return jnp.sum(row_loss * row_mask)

def dithered_code(clipped, peak, noise):
    ratio = jnp.abs(clipped) / peak
    dither = (noise.astype(jnp.float32) + 0.5) / noise_levels
    return jnp.sign(clipped) * jnp.clip(ramp_slope * (ratio - dither) + ratio, 0.0, 1.0)

def gram_of(iterate):
    return jnp.dot(iterate.T, iterate, precision=highest)

def schulz_step(iterate, gram_matrix):
    mixed = coef_b * gram_matrix + coef_c * jnp.dot(gram_matrix, gram_matrix, precision=highest)
    return coef_a * iterate + jnp.dot(iterate, mixed, precision=highest)

def reference(features, labels, counts, weight6, weight7, weight8, moment6, moment7, moment8, resid6, resid7, resid8, noise6, noise7, noise8, biases, bias_first, bias_second):
    image_total = jnp.sum(counts).astype(jnp.float32)
    params = (weight6, weight7, weight8, biases)
    feats = features.reshape(WORKERS, ROWS_DEV, IN)
    labs = labels.reshape(WORKERS, ROWS_DEV)

    def one_worker(inputs):
        feat_rows, lab_rows, count = inputs
        row_mask = (jnp.arange(ROWS_DEV) < count).astype(jnp.float32)
        loss_val, backward = jax.vjp(lambda p: worker_loss(p, feat_rows, lab_rows, row_mask), params)
        return (backward(jnp.ones((), jnp.float32))[0], loss_val)
    grads, losses = lax.map(one_worker, (feats, labs, counts))
    shapes = ((IN, H1), (H1, H2), (H2, C))
    resids = (resid6, resid7, resid8)
    noises = (noise6, noise7, noise8)
    masters = (weight6, weight7, weight8)
    moments = (moment6, moment7, moment8)
    new_weights, low_weights, new_moments, new_resids = ([], [], [], [])
    for which_layer in range(3):
        rows_in, cols_out = shapes[which_layer]
        acc = grads[which_layer] + resids[which_layer].reshape(WORKERS, rows_in, cols_out)
        bound = clip_width * jnp.sqrt(lax.optimization_barrier(jnp.mean(acc * acc, axis=(1, 2), keepdims=True)))
        clipped = jnp.clip(acc, -bound, bound)
        peak = jnp.max(jnp.abs(clipped)) + 1e-06
        code = dithered_code(clipped, peak, noises[which_layer].reshape(WORKERS, rows_in, cols_out))
        new_resids.append((acc - peak * code).reshape(WORKERS * rows_in, cols_out))
        reduced = peak * lax.optimization_barrier(jnp.sum(code, axis=0)) / image_total
        moment_new = momentum_decay * moments[which_layer] + reduced
        iterate = moment_new / (jnp.sqrt(jnp.sum(moment_new * moment_new)) + 1e-07)
        for step_num in range(NS_STEPS):
            iterate = schulz_step(iterate, gram_of(iterate))
        weight_new = masters[which_layer] - muon_rate * (iterate + decay_rate * masters[which_layer])
        new_weights.append(weight_new)
        low_weights.append(weight_new.astype(jnp.bfloat16))
        new_moments.append(moment_new)
    bias_grad = lax.optimization_barrier(jnp.sum(grads[3], axis=0)) / image_total
    first_new = beta_first * bias_first + (1.0 - beta_first) * bias_grad
    second_new = beta_second * bias_second + (1.0 - beta_second) * bias_grad * bias_grad
    first_hat = first_new / (1.0 - beta_first ** ADAM_STEP)
    second_hat = second_new / (1.0 - beta_second ** ADAM_STEP)
    biases_new = biases - bias_rate * (first_hat / (jnp.sqrt(second_hat) + adam_eps) + decay_rate * biases)
    return (new_weights[0], new_weights[1], new_weights[2], low_weights[0], low_weights[1], low_weights[2], new_moments[0], new_moments[1], new_moments[2], new_resids[0], new_resids[1], new_resids[2], biases_new, first_new, second_new, jnp.sum(losses), image_total)
```

```python
import functools

import jax
import jax.numpy as jnp
from jax import lax
from jax.experimental import pallas as pl
from jax.experimental.pallas import tpu as pltpu
from jax.sharding import PartitionSpec as P

NS_STEPS = 5
ADAM_STEP = 10


highest = lax.Precision.HIGHEST
smoothing = 0.1
clip_width = 2.5
noise_levels = 1024.0
ramp_slope = 2.0
momentum_decay = 0.95
muon_rate = 0.6
decay_rate = 0.01
coef_a = 3.4445
coef_b = -4.775
coef_c = 2.0315
beta_first = 0.9
beta_second = 0.999
bias_rate = 0.05
adam_eps = 1e-08

F32 = jnp.float32
BF16 = jnp.bfloat16
LANE = 128
BOTH = ("grp", "wide")
VMEM_LIMIT = 48 * 1024 * 1024


def dithered_code(clipped, peak, noise):
    ratio = jnp.abs(clipped) / peak
    dither = (noise.astype(jnp.float32) + 0.5) / noise_levels
    return jnp.sign(clipped) * jnp.clip(ramp_slope * (ratio - dither) + ratio, 0.0, 1.0)


def gram_of(iterate):
    return jnp.dot(iterate.T, iterate, precision=highest)


def schulz_step(iterate, gram_matrix):
    mixed = coef_b * gram_matrix + coef_c * jnp.dot(gram_matrix, gram_matrix, precision=highest)
    return coef_a * iterate + jnp.dot(iterate, mixed, precision=highest)


def layer_forward(inputs_b, weight_b, bias_part):
    return jnp.dot(inputs_b, weight_b, preferred_element_type=jnp.float32) + bias_part


def layer_backward(inputs_b, weight_b, grad_pre):
    grad_low = grad_pre.astype(jnp.bfloat16)
    weight_grad = jnp.einsum("ri,ro->io", inputs_b, grad_low, preferred_element_type=jnp.float32)
    bias_grad = jnp.sum(grad_low.astype(jnp.float32), axis=0)
    grad_inputs = jnp.einsum("ro,io->ri", grad_low, weight_b, preferred_element_type=jnp.float32)
    return (weight_grad, bias_grad, grad_inputs)


def adam_biases(biases, bias_first, bias_second, bias_grad):
    first_new = beta_first * bias_first + (1.0 - beta_first) * bias_grad
    second_new = beta_second * bias_second + (1.0 - beta_second) * bias_grad * bias_grad
    first_hat = first_new / (1.0 - beta_first**ADAM_STEP)
    second_hat = second_new / (1.0 - beta_second**ADAM_STEP)
    biases_new = biases - bias_rate * (
        first_hat / (jnp.sqrt(second_hat) + adam_eps) + decay_rate * biases
    )
    return biases_new, first_new, second_new


def general_plan(
    features,
    labels,
    counts,
    weight6,
    weight7,
    weight8,
    moment6,
    moment7,
    moment8,
    resid6,
    resid7,
    resid8,
    noise6,
    noise7,
    noise8,
    biases,
    bias_first,
    bias_second,
):
    masters = (weight6, weight7, weight8)
    weights_b = [
        lax.all_gather(weight.astype(jnp.bfloat16), "wide", axis=0, tiled=True)
        for weight in masters
    ]
    widths = [weights_b[0].shape[1], weights_b[1].shape[1], weights_b[2].shape[1]]
    bias_parts = [
        biases[: widths[0]],
        biases[widths[0] : widths[0] + widths[1]],
        biases[widths[0] + widths[1] :],
    ]
    row_mask = (jnp.arange(features.shape[0]) < counts[0]).astype(jnp.float32)
    inputs_list = [features]
    gelu_backs = []
    logits = None
    for which_layer in range(3):
        pre_act = layer_forward(
            inputs_list[which_layer], weights_b[which_layer], bias_parts[which_layer]
        )
        if which_layer < 2:
            activ, gelu_back = jax.vjp(jax.nn.gelu, pre_act)
            inputs_list.append(activ.astype(jnp.bfloat16))
            gelu_backs.append(gelu_back)
        else:
            logits = pre_act
    logp = jax.nn.log_softmax(logits, axis=-1)
    onehot = (labels[:, None] == jnp.arange(widths[2])[None, :]).astype(jnp.float32)
    target = (1.0 - smoothing) * onehot + smoothing / widths[2]
    worker_loss = jnp.sum(-jnp.sum(target * logp, axis=-1) * row_mask)
    upstream = -target * row_mask[:, None]
    grad_pre = upstream - jnp.exp(logp) * jnp.sum(upstream, axis=-1, keepdims=True)
    weight_grads = [None, None, None]
    bias_grads = [None, None, None]
    for which_layer in (2, 1, 0):
        weight_grads[which_layer], bias_grads[which_layer], grad_inputs = layer_backward(
            inputs_list[which_layer], weights_b[which_layer], grad_pre
        )
        if which_layer > 0:
            grad_pre = gelu_backs[which_layer - 1](grad_inputs)[0]
    resids = (resid6, resid7, resid8)
    noises = (noise6, noise7, noise8)
    accs = [weight_grads[k] + resids[k] for k in range(3)]
    clipped_list = []
    for acc in accs:
        bound = clip_width * jnp.sqrt(jnp.mean(acc * acc))
        clipped_list.append(jnp.clip(acc, -bound, bound))
    peak_list = lax.pmax(tuple(jnp.max(jnp.abs(clipped)) for clipped in clipped_list), BOTH)
    peak_list = [p + 1e-06 for p in peak_list]
    code_list = [dithered_code(clipped_list[k], peak_list[k], noises[k]) for k in range(3)]
    new_resids = [accs[k] - peak_list[k] * code_list[k] for k in range(3)]
    loss_total, image_total, bias_total = lax.psum(
        (worker_loss, jnp.sum(row_mask), jnp.concatenate(bias_grads)), BOTH
    )
    code_rows = [
        lax.psum_scatter(code, "wide", scatter_dimension=0, tiled=True) for code in code_list
    ]
    code_sums = lax.psum(tuple(code_rows), "grp")
    moments = (moment6, moment7, moment8)
    new_moments = [
        momentum_decay * moments[k] + peak_list[k] * code_sums[k] / image_total for k in range(3)
    ]
    full_moments = [
        lax.all_gather(moment, "wide", axis=0, tiled=True) for moment in new_moments
    ]
    row_block = lax.axis_index("wide")
    iterates = []
    for k in range(3):
        whole = full_moments[k]
        iterate = whole / (jnp.sqrt(jnp.sum(whole * whole)) + 1e-07)
        for step_num in range(NS_STEPS):
            iterate = schulz_step(iterate, gram_of(iterate))
        row_count = new_moments[k].shape[0]
        iterates.append(lax.dynamic_slice_in_dim(iterate, row_block * row_count, row_count, 0))
    new_weights = [
        masters[k] - muon_rate * (iterates[k] + decay_rate * masters[k]) for k in range(3)
    ]
    new_biases = adam_biases(biases, bias_first, bias_second, bias_total / image_total)
    return (
        *new_weights,
        *[weight.astype(jnp.bfloat16) for weight in new_weights],
        *new_moments,
        *new_resids,
        *new_biases,
        loss_total,
        image_total,
    )


ORDERS = ((1, 2, 4), (2, 1, 4))


def wide_perm(phase):
    return [
        (g * 8 + w, g * 8 + (w ^ ORDERS[g % 2][phase])) for g in range(4) for w in range(8)
    ]


def grp_perm(bit):
    return [(g * 8 + w, (g ^ bit) * 8 + w) for g in range(4) for w in range(8)]


def places(wide, core):
    result = []
    for place in range(8):
        masks = []
        for order in ORDERS:
            mask = 0
            for phase in range(3):
                if place & (4 >> phase):
                    mask |= order[phase]
            masks.append(mask)
        result.append(wide ^ jnp.where(core == 0, masks[0], masks[1]))
    return result


def gather_halves(own):
    first = lax.ppermute(own, BOTH, wide_perm(2))
    two = jnp.concatenate([own, first], axis=0)
    second = lax.ppermute(two, BOTH, wide_perm(1))
    four = jnp.concatenate([two, second], axis=0)
    third = lax.ppermute(four, BOTH, wide_perm(0))
    other_low = lax.ppermute(four, BOTH, grp_perm(1))
    other_high = lax.ppermute(third, BOTH, grp_perm(1))
    return four, third, other_low, other_high


def dims(contract_left, contract_right):
    return (((contract_left,), (contract_right,)), ((), ()))


def mxu(left, right, contract_left=1, contract_right=0):
    return lax.dot_general(
        left, right, dims(contract_left, contract_right), preferred_element_type=F32
    )


def split(value):
    high = value.astype(BF16)
    return high, (value - high.astype(F32)).astype(BF16)


def left_parts(value):
    high, rest = split(value)
    return jnp.concatenate([high, high, rest], axis=1)


def right_parts(value):
    high, rest = split(value)
    return jnp.concatenate([high, rest, high], axis=0)


def eye(size, dtype):
    rows = lax.broadcasted_iota(jnp.int32, (size, size), 0)
    cols = lax.broadcasted_iota(jnp.int32, (size, size), 1)
    return (rows == cols).astype(dtype)


def call(kernel, **options):
    limit = options.pop("vmem_limit_bytes", VMEM_LIMIT)
    return pl.pallas_call(
        kernel, compiler_params=pltpu.CompilerParams(vmem_limit_bytes=limit), **options
    )


def full_spec(shape):
    return pl.BlockSpec(shape, lambda *_: (0,) * len(shape))


def pack_kernel(rows6, h2, classes, tail, core_ref, w6_ref, w7_ref, w8t_ref, out_ref):
    out_ref[0, :rows6, :] = w6_ref[...].astype(BF16)
    rows7 = w7_ref.shape[0]
    out_ref[0, rows6:, :] = jnp.zeros((rows7, out_ref.shape[2]), BF16)
    out_ref[0, rows6:, :h2] = w7_ref[...].astype(BF16)
    rows8 = w8t_ref.shape[1]
    tall = mxu(eye(rows8, BF16), w8t_ref[...].astype(BF16), 1, 1)
    out_ref[0, rows6 : rows6 + rows8, tail : tail + classes] = tall.astype(BF16)


def pack_weights(core, weight6, weight7, weight8):
    h1 = weight6.shape[1]
    h2 = weight7.shape[1]
    classes = weight8.shape[1]
    rows6 = weight6.shape[0] // 2
    rows7 = weight7.shape[0] // 2
    tail = h1 - LANE
    return call(
        functools.partial(pack_kernel, rows6, h2, classes, tail),
        grid_spec=pltpu.PrefetchScalarGridSpec(
            num_scalar_prefetch=1,
            grid=(1,),
            in_specs=[
                pl.BlockSpec((rows6, h1), lambda i, c: (c[0], 0)),
                pl.BlockSpec((rows7, h2), lambda i, c: (c[0], 0)),
                full_spec((classes, weight8.shape[0])),
            ],
            out_specs=full_spec((1, rows6 + rows7, h1)),
        ),
        out_shape=jax.ShapeDtypeStruct((1, rows6 + rows7, h1), BF16),
        name="pack_weights",
    )(core[None], weight6, weight7, weight8.T)


def gelu_pair(pre):
    slope = 0.7978845608028654
    inner = slope * (pre + 0.044715 * pre * pre * pre)
    t = jnp.tanh(inner)
    value = 0.5 * pre * (1.0 + t)
    back = 0.5 * (1.0 + t) + 0.5 * pre * (1.0 - t * t) * slope * (1.0 + 3 * 0.044715 * pre * pre)
    return value, back


def worker_kernel(
    sizes,
    tile,
    table_ref,
    count_ref,
    own_low,
    own_high,
    other_low,
    other_high,
    feat_ref,
    label_ref,
    b6_ref,
    b7_ref,
    b8_ref,
    resid6_ref,
    resid7_ref,
    resid8_ref,
    acc6_ref,
    acc7_ref,
    acc8_ref,
    stats_ref,
    w6,
    w7,
    w8,
    hold,
    in_sem,
    out_sem,
):
    ins, h1, h2, classes, rows6, rows7, rows8, tail = sizes
    tiles = ins // tile

    def resid_copy(t):
        part = pl.ds(t * tile, tile)
        return pltpu.make_async_copy(resid6_ref.at[part], hold.at[part], in_sem.at[t])

    def acc_copy(t):
        part = pl.ds(t * tile, tile)
        return pltpu.make_async_copy(hold.at[part], acc6_ref.at[part], out_sem.at[t])

    for t in range(tiles):
        resid_copy(t).start()

    w8[...] = jnp.zeros(w8.shape, F32)
    for at, ref in enumerate((own_low, own_high, other_low, other_high)):
        for q in range(4):
            half = table_ref[at * 4 + q]
            position = half // 2
            w6[pl.ds(pl.multiple_of(half * rows6, 16), rows6), :] = ref[q, :rows6, :]
            w7[pl.ds(pl.multiple_of(half * rows7, 8), rows7), :] = ref[
                q, rows6 : rows6 + rows7, :h2
            ].astype(F32)
            w8[pl.ds(pl.multiple_of(position * rows8, 8), rows8), :] = ref[
                q, rows6 : rows6 + rows8, tail : tail + LANE
            ].astype(F32)
    w7_low = w7[...].astype(BF16)
    w8_low = w8[...].astype(BF16)

    rows = feat_ref.shape[0]
    row_mask = (lax.broadcasted_iota(jnp.int32, (rows, 1), 0) < count_ref[0]).astype(F32)
    lanes = lax.broadcasted_iota(jnp.int32, (rows, LANE), 1)
    valid = lanes < classes

    pre6 = mxu(feat_ref[...], w6[...]) + b6_ref[...]
    act6, back6 = gelu_pair(pre6)
    act6 = act6.astype(BF16)
    pre7 = mxu(act6, w7_low) + b7_ref[...]
    act7, back7 = gelu_pair(pre7)
    act7 = act7.astype(BF16)
    logits = jnp.where(valid, mxu(act7, w8_low) + b8_ref[...], -1e30)
    top = jnp.max(logits, axis=1, keepdims=True)
    shifted = logits - top
    logp = shifted - jnp.log(jnp.sum(jnp.exp(shifted), axis=1, keepdims=True))
    onehot = (label_ref[...] == lanes).astype(F32)
    target = jnp.where(valid, (1.0 - smoothing) * onehot + smoothing / classes, 0.0)
    loss = jnp.sum(-jnp.sum(target * jnp.where(valid, logp, 0.0), axis=1, keepdims=True) * row_mask)
    weight = jnp.sum(target, axis=1, keepdims=True)
    dlogits = (row_mask * (jnp.exp(logp) * weight - target)).astype(BF16)
    dpre7 = (mxu(dlogits, w8_low, 1, 1) * back7).astype(BF16)
    dpre6 = (mxu(dpre7, w7_low, 1, 1) * back6).astype(BF16)

    square6 = jnp.zeros((8, h1), F32)
    most6 = jnp.zeros((8, h1), F32)
    for t in range(tiles):
        part = slice(t * tile, (t + 1) * tile)
        grad = mxu(feat_ref[:, part], dpre6, 0, 0)
        resid_copy(t).wait()
        acc = hold[part, :] + grad
        hold[part, :] = acc
        acc_copy(t).start()
        square6 = square6 + jnp.sum((acc * acc).reshape(tile // 8, 8, h1), axis=0)
        most6 = jnp.maximum(most6, jnp.max(jnp.abs(acc).reshape(tile // 8, 8, h1), axis=0))
    acc7 = mxu(dpre7, act6, 0, 0) + resid7_ref[...]
    acc7_ref[...] = acc7
    acc8 = mxu(dlogits, act7, 0, 0)[:classes, :] + resid8_ref[...]
    acc8_ref[...] = acc8

    bound6 = clip_width * jnp.sqrt(jnp.sum(square6) * (1.0 / (ins * h1)))
    bound7 = clip_width * jnp.sqrt(jnp.sum(acc7 * acc7) * (1.0 / (h1 * h2)))
    bound8 = clip_width * jnp.sqrt(jnp.sum(acc8 * acc8) * (1.0 / (h2 * classes)))
    peak6 = jnp.minimum(jnp.max(most6), bound6)
    peak7 = jnp.minimum(jnp.max(jnp.abs(acc7)), bound7)
    peak8 = jnp.minimum(jnp.max(jnp.abs(acc8)), bound8)
    lane = lax.broadcasted_iota(jnp.int32, (1, LANE), 1)
    head = jnp.zeros((1, LANE), F32)
    count = count_ref[0].astype(F32)
    for k, value in enumerate((peak6, peak7, peak8, loss, count, bound6, bound7, bound8)):
        head = jnp.where(lane == k, value, head)
    db6 = jnp.sum(dpre6.astype(F32), axis=0, keepdims=True)
    db7 = jnp.sum(dpre7.astype(F32), axis=0, keepdims=True)
    db8 = jnp.sum(dlogits.astype(F32), axis=0, keepdims=True)
    db7 = jnp.concatenate([db7, jnp.zeros((1, 2 * LANE - h2), F32)], axis=1)
    tiled = jnp.concatenate(
        [head]
        + [db6[:, k * LANE : (k + 1) * LANE] for k in range(h1 // LANE)]
        + [db7[:, :LANE], db7[:, LANE:], db8, jnp.zeros((1, LANE), F32)],
        axis=0,
    )
    stats_ref[...] = jnp.broadcast_to(tiled[None], stats_ref.shape)
    for t in range(tiles):
        acc_copy(t).wait()


def code_of(acc, bound, scale, noise):
    ramp = jnp.minimum(jnp.abs(acc), bound) * scale - (
        noise.astype(F32) * (ramp_slope / noise_levels) + 0.5 * ramp_slope / noise_levels
    )
    ramp = jnp.clip(ramp, 0.0, 1.0)
    return jnp.where(acc < 0, -ramp, ramp)


def code_kernel(
    sizes,
    small,
    table_ref,
    stats_ref,
    mine_ref,
    acc6_ref,
    noise6_ref,
    acc7_ref,
    noise7_ref,
    acc8_ref,
    noise8_ref,
    *refs,
):
    ins, h1, h2, classes, rows6, rows7, rows8, tail = sizes
    if small:
        code_ref, resid6_ref, resid7_ref, resid8_ref, code7, code8, peaks = refs
    else:
        code_ref, resid6_ref, code7, code8, peaks = refs
    step = pl.program_id(0)

    @pl.when(step == 0)
    def _():
        most = jnp.max(stats_ref[:, 0, :], axis=0, keepdims=True)
        lane = lax.broadcasted_iota(jnp.int32, (1, LANE), 1)
        for k in range(3):
            peaks[k] = jnp.max(jnp.where(lane == k, most, 0.0)) + 1e-06
            peaks[3 + k] = jnp.max(jnp.where(lane == 5 + k, mine_ref[0, :1, :], 0.0))
        acc7 = acc7_ref[...]
        small7 = code_of(acc7, peaks[4], (1.0 + ramp_slope) / peaks[1], noise7_ref[...])
        acc8 = acc8_ref[...]
        small8 = code_of(acc8, peaks[5], (1.0 + ramp_slope) / peaks[2], noise8_ref[...])
        if small:
            resid7_ref[...] = acc7 - peaks[1] * small7
            resid8_ref[...] = acc8 - peaks[2] * small8
        code7[...] = mxu(eye(h1, BF16), small7.astype(BF16), 1, 1)
        code8[...] = jnp.zeros(code8.shape, F32)
        code8[:, :classes] = mxu(eye(h2, BF16), small8.astype(BF16), 1, 1)

    acc = acc6_ref[...]
    code = code_of(acc, peaks[3], (1.0 + ramp_slope) / peaks[0], noise6_ref[...])
    resid6_ref[...] = acc - peaks[0] * code
    code_ref[0, :rows6, :] = code.astype(BF16)
    half = table_ref[step]
    code_ref[0, rows6:, :] = jnp.zeros((rows7, h1), BF16)
    code_ref[0, rows6:, :h2] = code7[
        pl.ds(pl.multiple_of(half * rows7, 8), rows7), :
    ].astype(BF16)
    lead = (half % 2 == 0).astype(F32)
    code_ref[0, rows6 : rows6 + rows8, tail : tail + LANE] = (
        lead * code8[pl.ds(pl.multiple_of((half // 2) * rows8, 8), rows8), :]
    ).astype(BF16)


def code_call(sizes, small, table, stats, mine, acc6, noise6, acc7, noise7, acc8, noise8):
    ins, h1, h2, classes, rows6, rows7, rows8, tail = sizes
    block6 = pl.BlockSpec((rows6, h1), lambda i, t: (t[i], 0))
    out_shape = [
        jax.ShapeDtypeStruct((8, rows6 + rows7, h1), BF16),
        jax.ShapeDtypeStruct(acc6.shape, F32),
    ]
    out_specs = [pl.BlockSpec((1, rows6 + rows7, h1), lambda i, t: (i, 0, 0)), block6]
    if small:
        for acc in (acc7, acc8):
            out_shape.append(jax.ShapeDtypeStruct(acc.shape, F32))
            out_specs.append(full_spec(acc.shape))
    return call(
        functools.partial(code_kernel, sizes, small),
        grid_spec=pltpu.PrefetchScalarGridSpec(
            num_scalar_prefetch=1,
            grid=(8,),
            in_specs=[
                full_spec(stats.shape),
                pl.BlockSpec((1,) + mine.shape[1:], lambda i, t: (0, 0, 0)),
                block6,
                block6,
                full_spec(acc7.shape),
                full_spec(noise7.shape),
                full_spec(acc8.shape),
                full_spec(noise8.shape),
            ],
            out_specs=out_specs,
            scratch_shapes=[
                pltpu.VMEM((h1, h2), F32),
                pltpu.VMEM((h2, LANE), F32),
                pltpu.SMEM((6,), F32),
            ],
        ),
        out_shape=out_shape,
        input_output_aliases={3: 1},
        name="codes_sent" if small else "codes_kept",
    )(table, stats, mine, acc6, noise6, acc7, noise7, acc8, noise8)


def schulz_chain(gram, iterate):
    size = gram.shape[0]
    diagonal = eye(size, F32)
    norm = jnp.sqrt(jnp.sum(gram * diagonal)) + 1e-07
    inverse = 1.0 / norm
    gram = gram * (inverse * inverse)
    iterate = iterate * inverse

    def step(carry, last):
        gram, iterate = carry
        left = left_parts(gram)
        square = mxu(left, right_parts(gram))
        mixed = right_parts(coef_a * diagonal + coef_b * gram + coef_c * square)
        iterate = mxu(left_parts(iterate), mixed)
        if not last:
            gram = mxu(left_parts(mxu(left, mixed)), mixed)
        return gram, iterate

    return step, (gram, iterate)


def update_kernel(
    sizes,
    table_ref,
    core_ref,
    own_low,
    own_high,
    other_low,
    other_high,
    mine_ref,
    theirs_ref,
    w6_ref,
    w7_ref,
    w8_ref,
    new6_ref,
    new7_ref,
    new8_ref,
    low6_ref,
    low7_ref,
    low8_ref,
    mom6_ref,
    mom7_ref,
    mom8_ref,
    all6,
    all78,
):
    ins, h1, h2, classes, rows6, rows7, rows8, tail = sizes
    core = core_ref[0]

    for at, ref in enumerate((own_low, own_high, other_low, other_high)):
        for q in range(4):
            half = table_ref[at * 4 + q]
            all6[pl.ds(pl.multiple_of(half * rows6, 16), rows6), :] = ref[q, :rows6, :]
            all78[pl.ds(pl.multiple_of(half * rows7, 8), rows7), :] = ref[q, rows6:, :].astype(F32)
    gram6 = mxu(all6[...], all6[...], 0, 0)
    regions = all78[...].astype(BF16)
    gram78 = mxu(regions, regions, 0, 0)
    gram7 = gram78[:h2, :h2]
    gram8 = gram78[tail:, tail:]

    for at, ref in ((core, mine_ref), (1 - core, theirs_ref)):
        mom6_ref[pl.ds(pl.multiple_of(at * rows6, 8), rows6), :] = ref[0, :rows6, :]
        mom7_ref[pl.ds(pl.multiple_of(at * rows7, 8), rows7), :] = ref[
            0, rows6 : rows6 + rows7, :h2
        ]
    mom8 = jnp.where(
        core == 0,
        mine_ref[0, rows6 : rows6 + rows8, tail:],
        theirs_ref[0, rows6 : rows6 + rows8, tail:],
    )
    mom8_ref[...] = mom8[:, :classes]

    step6, carry6 = schulz_chain(gram6, mom6_ref[...])
    step7, carry7 = schulz_chain(gram7, mom7_ref[...])
    step8, carry8 = schulz_chain(gram8, mom8)

    for _ in range(NS_STEPS - 1):
        carry6 = step6(carry6, False)
        carry7 = step7(carry7, False)
        carry8 = step8(carry8, False)
    iterate6 = step6(carry6, True)[1]
    iterate7 = step7(carry7, True)[1]
    iterate8 = step8(carry8, True)[1][:, :classes]
    for iterate, w_ref, new_ref, low_ref in (
        (iterate6, w6_ref, new6_ref, low6_ref),
        (iterate7, w7_ref, new7_ref, low7_ref),
        (iterate8, w8_ref, new8_ref, low8_ref),
    ):
        master = w_ref[...]
        value = master - muon_rate * (iterate + decay_rate * master)
        new_ref[...] = value
        low_ref[...] = value.astype(BF16)


def paired_plan(
    features,
    labels,
    counts,
    weight6,
    weight7,
    weight8,
    moment6,
    moment7,
    moment8,
    resid6,
    resid7,
    resid8,
    noise6,
    noise7,
    noise8,
    biases,
    bias_first,
    bias_second,
):
    ins, h1 = resid6.shape
    h2, classes = resid8.shape
    rows6 = weight6.shape[0] // 2
    rows7 = weight7.shape[0] // 2
    rows8 = weight8.shape[0]
    tail = h1 - LANE
    sizes = (ins, h1, h2, classes, rows6, rows7, rows8, tail)
    devices = 32

    core = lax.axis_index("grp").astype(jnp.int32) % 2
    wide = lax.axis_index("wide").astype(jnp.int32)
    own = [position * 2 + core for position in places(wide, core)]
    other = [position * 2 + 1 - core for position in places(wide, 1 - core)]
    own_table = jnp.stack(own)
    other_table = jnp.stack(other)
    all_table = jnp.concatenate([own_table, other_table])

    halves = gather_halves(pack_weights(core, weight6, weight7, weight8))

    bias6 = biases[:h1].reshape(1, h1)
    bias7 = biases[h1 : h1 + h2].reshape(1, h2)
    bias8 = jnp.pad(biases[h1 + h2 :], (0, LANE - classes)).reshape(1, LANE)
    tile = 2 * LANE
    any_spec = pl.BlockSpec(memory_space=pl.ANY)
    smem_spec = pl.BlockSpec(memory_space=pltpu.SMEM)
    vmem_spec = pl.BlockSpec(memory_space=pltpu.VMEM)
    acc6, acc7, acc8, stats = call(
        functools.partial(worker_kernel, sizes, tile),
        in_specs=[smem_spec, smem_spec] + [vmem_spec] * 9 + [any_spec] + [vmem_spec] * 2,
        out_specs=[any_spec] + [vmem_spec] * 3,
        out_shape=[
            jax.ShapeDtypeStruct((ins, h1), F32),
            jax.ShapeDtypeStruct((h2, h1), F32),
            jax.ShapeDtypeStruct((classes, h2), F32),
            jax.ShapeDtypeStruct((devices, 8, LANE), F32),
        ],
        scratch_shapes=[
            pltpu.VMEM((ins, h1), BF16),
            pltpu.VMEM((h1, h2), F32),
            pltpu.VMEM((h2, LANE), F32),
            pltpu.VMEM((ins, h1), F32),
            pltpu.SemaphoreType.DMA((ins // tile,)),
            pltpu.SemaphoreType.DMA((ins // tile,)),
        ],
        name="worker",
    )(
        all_table,
        counts,
        *halves,
        features,
        labels.reshape(-1, 1),
        bias6,
        bias7,
        bias8,
        resid6,
        resid7.T,
        resid8.T,
    )

    all_stats = lax.all_to_all(stats, BOTH, 0, 0, tiled=True)

    sent, resid6_part, new_resid7, new_resid8 = code_call(
        sizes, True, other_table, all_stats, stats, acc6, noise6, acc7, noise7.T, acc8, noise8.T
    )
    kept, new_resid6 = code_call(
        sizes,
        False,
        own_table,
        all_stats,
        stats,
        resid6_part,
        noise6,
        acc7,
        noise7.T,
        acc8,
        noise8.T,
    )

    total = jnp.sum(all_stats, axis=0)
    peaks = jnp.max(all_stats[:, 0, :3], axis=0) + 1e-06
    loss_total = total[0, 3]
    image_total = total[0, 4]
    lanes6 = h1 // LANE
    bias_total = jnp.concatenate(
        [
            total[1 : 1 + lanes6].reshape(-1),
            total[1 + lanes6 : 3 + lanes6].reshape(-1)[:h2],
            total[3 + lanes6, :classes],
        ]
    )
    new_biases = adam_biases(biases, bias_first, bias_second, bias_total / image_total)

    got = lax.ppermute(sent, BOTH, grp_perm(1))
    part = kept.astype(F32)
    count = 8
    for phase in range(3):
        count = count // 2
        out = (part[count:] + got[count : 2 * count].astype(F32)).astype(BF16)
        next_got = lax.ppermute(out, BOTH, wide_perm(phase))
        part = part[:count] + got[:count].astype(F32)
        got = next_got
    mine = lax.optimization_barrier((part + got.astype(F32)).astype(BF16))
    theirs = lax.ppermute(mine, BOTH, grp_perm(2))
    code_sum = mine.astype(F32) + theirs.astype(F32)

    half6 = lax.dynamic_slice_in_dim(moment6, core * rows6, rows6, 0)
    half7 = lax.dynamic_slice_in_dim(moment7, core * rows7, rows7, 0)
    half8 = jnp.where(core == 0, moment8, 0.0)
    region = jnp.concatenate(
        [
            half7,
            jnp.zeros((rows7, tail - h2), F32),
            jnp.pad(half8, ((0, rows7 - rows8), (0, LANE - classes))),
        ],
        axis=1,
    )
    held = momentum_decay * jnp.concatenate([half6, region], axis=0)[None]
    rates = peaks / image_total
    row = lax.broadcasted_iota(jnp.int32, (1, rows6 + rows7, h1), 1)
    column = lax.broadcasted_iota(jnp.int32, (1, rows6 + rows7, h1), 2)
    rate = jnp.where(row < rows6, rates[0], jnp.where(column < h2, rates[1], rates[2]))
    moment = held + rate * code_sum
    moment_other = lax.ppermute(moment, BOTH, grp_perm(1))
    moments = gather_halves(moment.astype(BF16))

    updated = call(
        functools.partial(update_kernel, sizes),
        in_specs=[smem_spec] * 2 + [vmem_spec] * 9,
        out_specs=[vmem_spec] * 9,
        out_shape=[
            jax.ShapeDtypeStruct(weight6.shape, F32),
            jax.ShapeDtypeStruct(weight7.shape, F32),
            jax.ShapeDtypeStruct(weight8.shape, F32),
            jax.ShapeDtypeStruct(weight6.shape, BF16),
            jax.ShapeDtypeStruct(weight7.shape, BF16),
            jax.ShapeDtypeStruct(weight8.shape, BF16),
            jax.ShapeDtypeStruct(weight6.shape, F32),
            jax.ShapeDtypeStruct(weight7.shape, F32),
            jax.ShapeDtypeStruct(weight8.shape, F32),
        ],
        scratch_shapes=[pltpu.VMEM((ins, h1), BF16), pltpu.VMEM((16 * rows7, h1), F32)],
        name="update",
    )(all_table, core[None], *moments, moment, moment_other, weight6, weight7, weight8)

    return (
        *updated,
        new_resid6,
        new_resid7.T,
        new_resid8.T,
        *new_biases,
        loss_total,
        image_total,
    )


def on_device(*arrays):
    (ins, h1), (_, h2), (_, classes) = [array.shape for array in arrays[9:12]]
    rows6, rows7, rows8 = [array.shape[0] for array in arrays[3:6]]
    paired = (
        (lax.axis_size("grp"), lax.axis_size("wide")) == (4, 8)
        and rows6 % 32 == 0
        and rows7 % 16 == 0
        and rows8 % 8 == 0
        and rows8 <= rows7 // 2
        and h1 == 3 * LANE
        and h2 <= 2 * LANE
        and classes <= LANE
        and ins % (2 * LANE) == 0
    )
    return (paired_plan if paired else general_plan)(*arrays)


def solution(mesh):
    split_both = P(BOTH, None)
    split_wide = P("wide", None)
    return jax.shard_map(
        on_device,
        mesh=mesh,
        in_specs=(
            split_both,
            P(BOTH),
            P(BOTH),
            *[split_wide] * 6,
            *[split_both] * 6,
            P(),
            P(),
            P(),
        ),
        out_specs=(*[split_wide] * 9, *[split_both] * 3, P(), P(), P(), P(), P()),
        check_vma=False,
    )
```

```python
import functools

import jax
import jax.numpy as jnp
from jax import lax
from jax.experimental import pallas as pl
from jax.experimental.pallas import tpu as pltpu
from jax.sharding import PartitionSpec as P

NS_STEPS = 5
ADAM_STEP = 10


highest = lax.Precision.HIGHEST
smoothing = 0.1
clip_width = 2.5
noise_levels = 1024.0
ramp_slope = 2.0
momentum_decay = 0.95
muon_rate = 0.6
decay_rate = 0.01
coef_a = 3.4445
coef_b = -4.775
coef_c = 2.0315
beta_first = 0.9
beta_second = 0.999
bias_rate = 0.05
adam_eps = 1e-08

F32 = jnp.float32
BF16 = jnp.bfloat16
LANE = 128
BOTH = ("grp", "wide")


def dithered_code(clipped, peak, noise):
    ratio = jnp.abs(clipped) / peak
    dither = (noise.astype(jnp.float32) + 0.5) / noise_levels
    return jnp.sign(clipped) * jnp.clip(ramp_slope * (ratio - dither) + ratio, 0.0, 1.0)


def gram_of(iterate):
    return jnp.dot(iterate.T, iterate, precision=highest)


def schulz_step(iterate, gram_matrix):
    mixed = coef_b * gram_matrix + coef_c * jnp.dot(gram_matrix, gram_matrix, precision=highest)
    return coef_a * iterate + jnp.dot(iterate, mixed, precision=highest)


def layer_forward(inputs_b, weight_b, bias_part):
    return jnp.dot(inputs_b, weight_b, preferred_element_type=jnp.float32) + bias_part


def layer_backward(inputs_b, weight_b, grad_pre):
    grad_low = grad_pre.astype(jnp.bfloat16)
    weight_grad = jnp.einsum("ri,ro->io", inputs_b, grad_low, preferred_element_type=jnp.float32)
    bias_grad = jnp.sum(grad_low.astype(jnp.float32), axis=0)
    grad_inputs = jnp.einsum("ro,io->ri", grad_low, weight_b, preferred_element_type=jnp.float32)
    return (weight_grad, bias_grad, grad_inputs)


def adam_biases(biases, bias_first, bias_second, bias_grad):
    first_new = beta_first * bias_first + (1.0 - beta_first) * bias_grad
    second_new = beta_second * bias_second + (1.0 - beta_second) * bias_grad * bias_grad
    first_hat = first_new / (1.0 - beta_first**ADAM_STEP)
    second_hat = second_new / (1.0 - beta_second**ADAM_STEP)
    biases_new = biases - bias_rate * (
        first_hat / (jnp.sqrt(second_hat) + adam_eps) + decay_rate * biases
    )
    return biases_new, first_new, second_new


def general_plan(
    features,
    labels,
    counts,
    weight6,
    weight7,
    weight8,
    moment6,
    moment7,
    moment8,
    resid6,
    resid7,
    resid8,
    noise6,
    noise7,
    noise8,
    biases,
    bias_first,
    bias_second,
):
    masters = (weight6, weight7, weight8)
    weights_b = [
        lax.all_gather(weight.astype(jnp.bfloat16), "wide", axis=0, tiled=True)
        for weight in masters
    ]
    widths = [weights_b[0].shape[1], weights_b[1].shape[1], weights_b[2].shape[1]]
    bias_parts = [
        biases[: widths[0]],
        biases[widths[0] : widths[0] + widths[1]],
        biases[widths[0] + widths[1] :],
    ]
    row_mask = (jnp.arange(features.shape[0]) < counts[0]).astype(jnp.float32)
    inputs_list = [features]
    gelu_backs = []
    logits = None
    for which_layer in range(3):
        pre_act = layer_forward(
            inputs_list[which_layer], weights_b[which_layer], bias_parts[which_layer]
        )
        if which_layer < 2:
            activ, gelu_back = jax.vjp(jax.nn.gelu, pre_act)
            inputs_list.append(activ.astype(jnp.bfloat16))
            gelu_backs.append(gelu_back)
        else:
            logits = pre_act
    logp = jax.nn.log_softmax(logits, axis=-1)
    onehot = (labels[:, None] == jnp.arange(widths[2])[None, :]).astype(jnp.float32)
    target = (1.0 - smoothing) * onehot + smoothing / widths[2]
    worker_loss = jnp.sum(-jnp.sum(target * logp, axis=-1) * row_mask)
    upstream = -target * row_mask[:, None]
    grad_pre = upstream - jnp.exp(logp) * jnp.sum(upstream, axis=-1, keepdims=True)
    weight_grads = [None, None, None]
    bias_grads = [None, None, None]
    for which_layer in (2, 1, 0):
        weight_grads[which_layer], bias_grads[which_layer], grad_inputs = layer_backward(
            inputs_list[which_layer], weights_b[which_layer], grad_pre
        )
        if which_layer > 0:
            grad_pre = gelu_backs[which_layer - 1](grad_inputs)[0]
    resids = (resid6, resid7, resid8)
    noises = (noise6, noise7, noise8)
    accs = [weight_grads[k] + resids[k] for k in range(3)]
    clipped_list = []
    for acc in accs:
        bound = clip_width * jnp.sqrt(jnp.mean(acc * acc))
        clipped_list.append(jnp.clip(acc, -bound, bound))
    peak_list = lax.pmax(tuple(jnp.max(jnp.abs(clipped)) for clipped in clipped_list), BOTH)
    peak_list = [p + 1e-06 for p in peak_list]
    code_list = [dithered_code(clipped_list[k], peak_list[k], noises[k]) for k in range(3)]
    new_resids = [accs[k] - peak_list[k] * code_list[k] for k in range(3)]
    loss_total, image_total, bias_total = lax.psum(
        (worker_loss, jnp.sum(row_mask), jnp.concatenate(bias_grads)), BOTH
    )
    code_rows = [
        lax.psum_scatter(code, "wide", scatter_dimension=0, tiled=True) for code in code_list
    ]
    code_sums = lax.psum(tuple(code_rows), "grp")
    moments = (moment6, moment7, moment8)
    new_moments = [
        momentum_decay * moments[k] + peak_list[k] * code_sums[k] / image_total for k in range(3)
    ]
    full_moments = [
        lax.all_gather(moment, "wide", axis=0, tiled=True) for moment in new_moments
    ]
    row_block = lax.axis_index("wide")
    iterates = []
    for k in range(3):
        whole = full_moments[k]
        iterate = whole / (jnp.sqrt(jnp.sum(whole * whole)) + 1e-07)
        for step_num in range(NS_STEPS):
            iterate = schulz_step(iterate, gram_of(iterate))
        row_count = new_moments[k].shape[0]
        iterates.append(lax.dynamic_slice_in_dim(iterate, row_block * row_count, row_count, 0))
    new_weights = [
        masters[k] - muon_rate * (iterates[k] + decay_rate * masters[k]) for k in range(3)
    ]
    new_biases = adam_biases(biases, bias_first, bias_second, bias_total / image_total)
    return (
        *new_weights,
        *[weight.astype(jnp.bfloat16) for weight in new_weights],
        *new_moments,
        *new_resids,
        *new_biases,
        loss_total,
        image_total,
    )


ORDERS = ((2, 1, 4), (1, 2, 4))


def wide_perm(phase):
    return [
        (g * 8 + w, g * 8 + (w ^ ORDERS[g % 2][phase])) for g in range(4) for w in range(8)
    ]


def grp_perm(bit):
    return [(g * 8 + w, (g ^ bit) * 8 + w) for g in range(4) for w in range(8)]


def swap(array, perm):
    return lax.ppermute(array, BOTH, perm)


def own_core():
    return lax.rem(lax.axis_index("grp"), 2)


def half_at(place, same_core):
    core = own_core() if same_core else 1 - own_core()
    masks = [
        sum(order[phase] for phase in range(3) if place & (4 >> phase)) for order in ORDERS
    ]
    return 2 * (lax.axis_index("wide") ^ jnp.where(core == 0, masks[0], masks[1])) + core


def dims(contract_left, contract_right):
    return (((contract_left,), (contract_right,)), ((), ()))


def mxu(left, right, contract_left=1, contract_right=0):
    return lax.dot_general(
        left, right, dims(contract_left, contract_right), preferred_element_type=F32
    )


def split(value):
    high = value.astype(BF16)
    return high, (value - high.astype(F32)).astype(BF16)


def left_parts(value):
    high, rest = split(value)
    return jnp.concatenate([high, high, rest], axis=1)


def right_parts(value):
    high, rest = split(value)
    return jnp.concatenate([high, rest, high], axis=0)


def shifted_eye(rows, cols, shift, dtype):
    at = lax.broadcasted_iota(jnp.int32, (rows, cols), 0) + shift
    return (at == lax.broadcasted_iota(jnp.int32, (rows, cols), 1)).astype(dtype)


def upright(flat, shift, dtype=BF16):
    return mxu(flat.astype(BF16), shifted_eye(flat.shape[0], 2 * LANE, shift, BF16), 0, 0)


def fold(region):
    n = region.shape[0] // 3
    third = jnp.concatenate([region[2 * n :, :LANE], region[2 * n :, LANE:]], axis=0)
    return jnp.concatenate([region[: 2 * n], third], axis=1)


def unfold(folded):
    n = folded.shape[0] // 2
    last = jnp.concatenate([folded[:n, 2 * LANE :], folded[n:, 2 * LANE :]], axis=1)
    return jnp.concatenate([folded[:, : 2 * LANE], last], axis=0)


HBM = pl.BlockSpec(memory_space=pltpu.HBM)
SMEM = pl.BlockSpec(memory_space=pltpu.SMEM)
VMEM = pl.BlockSpec(memory_space=pltpu.VMEM)
RESULT = pl.BlockSpec(memory_space=pltpu.VMEM)


def shape_of(shape, dtype=F32):
    return jax.ShapeDtypeStruct(shape, dtype)


MICROS = {"passed_near": 0.6, "passed_last": 20.0}


def placed(shape, spec):
    if spec is HBM:
        return pltpu.HBM(shape.shape, shape.dtype)
    return pltpu.VMEM(shape.shape, shape.dtype) if spec is VMEM else shape


def call(kernel, name, in_specs, out_specs, out_shape, scratch=(), megabytes=4, aliases=None):
    many = isinstance(out_shape, list)
    shapes = [
        placed(shape, spec)
        for shape, spec in zip(
            out_shape if many else [out_shape], out_specs if many else [out_specs]
        )
    ]
    kernel_call = pl.pallas_call(
        kernel,
        in_specs=in_specs,
        out_specs=out_specs,
        out_shape=shapes if many else shapes[0],
        scratch_shapes=list(scratch),
        compiler_params=pltpu.CompilerParams(vmem_limit_bytes=megabytes * 1024 * 1024),
        cost_estimate=pl.CostEstimate(
            flops=int(MICROS.get(name, 0.0) * 1.15e9), bytes_accessed=0, transcendentals=0
        ),
        input_output_aliases=aliases or {},
        name=name,
    )

    def run(*arrays):
        return kernel_call(
            *[
                pltpu.with_memory_space_constraint(array, pltpu.HBM) if spec is HBM else array
                for array, spec in zip(arrays, in_specs)
            ]
        )

    return run


def pack_kernel(w6_ref, w7_ref, w8_ref, out_ref, half6, half7, all8, sems):
    core = own_core()
    rows6, rows7 = half6.shape[0], half7.shape[0]
    copies = [
        pltpu.make_async_copy(
            w6_ref.at[pl.ds(pl.multiple_of(core * rows6, 8), rows6)], half6, sems.at[0]
        ),
        pltpu.make_async_copy(
            w7_ref.at[pl.ds(pl.multiple_of(core * rows7, 8), rows7)], half7, sems.at[1]
        ),
        pltpu.make_async_copy(w8_ref, all8, sems.at[2]),
    ]
    for copy in copies:
        copy.start()
    for copy in copies:
        copy.wait()
    out_ref[0, :rows6, :] = half6[...].astype(BF16)
    h2 = half7.shape[1]
    lead = (core == 0).astype(F32)
    region = upright(all8[...], h2) * lead + jnp.concatenate(
        [half7[...], jnp.zeros((rows7, 2 * LANE - h2), F32)], axis=1
    )
    out_ref[0, rows6:, :] = fold(region).astype(BF16)


def pack_weights(weight6, weight7, weight8):
    rows6, h1 = weight6.shape[0] // 2, weight6.shape[1]
    rows7, h2 = weight7.shape[0] // 2, weight7.shape[1]
    return call(
        pack_kernel,
        "pack_weights",
        [HBM] * 3,
        VMEM,
        shape_of((1, rows6 + rows7 * 2 // 3, h1), BF16),
        [
            pltpu.VMEM((rows6, h1), F32),
            pltpu.VMEM((rows7, h2), F32),
            pltpu.VMEM(weight8.shape[::-1], F32),
            pltpu.SemaphoreType.DMA((3,)),
        ],
    )(weight6, weight7, weight8.T)


def stage_kernel(count, after_ref, images_ref, *refs):
    ins, outs, token_ref, sems = refs[:count], refs[count:-2], refs[-2], refs[-1]
    copies = [
        pltpu.make_async_copy(
            source, target if len(source.shape) == len(target.shape) else target.at[0], sems.at[k]
        )
        for k, (source, target) in enumerate(zip(ins, outs))
    ]
    for copy in copies:
        copy.start()
    token_ref[...] = jnp.full(token_ref.shape, images_ref[0], jnp.int32)
    for copy in copies:
        copy.wait()


def stage(after, counts, *arrays):
    count = len(arrays)
    shapes = [(1,) * (2 - array.ndim) + array.shape for array in arrays]
    return call(
        functools.partial(stage_kernel, count),
        "stage",
        [VMEM, SMEM] + [HBM] * count,
        [VMEM] * (count + 1),
        [shape_of(shape, array.dtype) for shape, array in zip(shapes, arrays)]
        + [shape_of((1, LANE), jnp.int32)],
        [pltpu.SemaphoreType.DMA((count,))],
    )(after, counts, *arrays)


def add_kernel(picks, size, *refs):
    for k in range(size):
        total = None
        for ref, pick in zip(refs, picks):
            part = ref[pick + k].astype(F32)
            total = part if total is None else total + part
        refs[-1][k] = total.astype(BF16)


def add(picks, arrays, size, after=(), name="add"):
    shape = shape_of((size,) + arrays[0].shape[1:], BF16)
    specs = [VMEM] * len(arrays) + [spec for spec, _ in after]
    return call(functools.partial(add_kernel, picks, size), name, specs, VMEM, shape)(
        *arrays, *[array for _, array in after]
    )


def pass_kernel(in_ref, *refs):
    refs[-1][...] = in_ref[...]


def passed(array, after, name="passed"):
    specs = [VMEM] * (1 + len(after))
    shape = shape_of(array.shape, array.dtype)
    return call(pass_kernel, name, specs, VMEM, shape)(array, *after)


def first_join_kernel(own_ref, far_ref, mid_ref, *refs):
    trio_ref, again_ref = refs[-2:]
    for k, ref in enumerate((own_ref, far_ref, mid_ref)):
        trio_ref[k] = ref[0]
    again_ref[...] = far_ref[...]


def relay_kernel(trio_ref, one_ref, out_ref):
    count = trio_ref.shape[0]
    out_ref[:count] = trio_ref[...]
    out_ref[count:] = one_ref[...]


def relay(trio, one):
    shape = shape_of((trio.shape[0] + one.shape[0],) + one.shape[1:], one.dtype)
    return call(relay_kernel, "relay", [VMEM] * 2, VMEM, shape)(trio, one)


def gather_halves(own, after=(), work=None):
    far = swap(own, wide_perm(2))
    mid = swap(own, wide_perm(1))
    trio, far = call(
        first_join_kernel,
        "first_join",
        [VMEM] * 3 + [spec for spec, _ in after],
        [VMEM] * 2,
        [shape_of((3,) + own.shape[1:], BF16), shape_of(own.shape, BF16)],
    )(own, far, mid, *[array for _, array in after])
    one3 = swap(far, wide_perm(1))
    trio4 = swap(trio, wide_perm(0))
    one7 = swap(one3, wide_perm(0))
    four, done = (relay(trio, one3), None) if work is None else work(trio, one3)
    trio4 = passed(trio4, (four,))
    one7 = passed(one7, done[:3] if done else (), "passed_last")
    mine = (four, trio4, one7)
    return (*mine, *[swap(part, grp_perm(1)) for part in mine]), done


def gelu_pair(pre):
    slope = 0.7978845608028654
    inner = slope * (pre + 0.044715 * pre * pre * pre)
    t = jnp.tanh(inner)
    value = 0.5 * pre * (1.0 + t)
    back = 0.5 * (1.0 + t) + 0.5 * pre * (1.0 - t * t) * slope * (1.0 + 3 * 0.044715 * pre * pre)
    return value, back


def place_all(sizes, refs, all6, all7, all8):
    ins, h1, h2, classes, rows6, rows7, rows8 = sizes
    for at in range(16):
        place = at % 8
        ref, q = refs[3 * (at // 8) + (0, 0, 0, 0, 1, 1, 1, 2)[place]], place % 4 % (4 - place // 4)
        half = half_at(place, at < 8)
        all6[pl.ds(pl.multiple_of(half * rows6, 16), rows6), :] = ref[q, :rows6, :]
        region = unfold(ref[q, rows6:, :].astype(F32))
        all7[pl.ds(pl.multiple_of(half * rows7, 8), rows7), :] = region

        @pl.when(half % 2 == 0)
        def _():
            row = pl.multiple_of((half // 2) * rows8, 8)
            all8[pl.ds(row, rows8), :] = region[:rows8, LANE:]


def worker_kernel(sizes, tile, *refs):
    ins, h1, h2, classes, rows6, rows7, rows8 = sizes
    halves, refs = refs[:6], refs[6:]
    count_ref, feat_ref, label_ref, bias_ref, resid6_ref, resid7_ref, resid8_ref = refs[:7]
    acc6_ref, acc7_ref, acc8_ref, stats_ref, w6, w7, w8 = refs[7:]
    first = h2 - LANE

    place_all(sizes, halves, w6, w7, w8)
    w7_low = w7[:, :h2].astype(BF16)
    w8_low = w8[...].astype(BF16)

    rows = feat_ref.shape[0]
    row_mask = (lax.broadcasted_iota(jnp.int32, (rows, 1), 0) < count_ref[:, :1]).astype(F32)
    lanes = lax.broadcasted_iota(jnp.int32, (rows, LANE), 1) - first
    valid = (lanes >= 0) & (lanes < classes)
    labels = jnp.sum(
        jnp.where(shifted_eye(rows, rows, 0, jnp.bool_), label_ref[...], 0), axis=1, keepdims=True
    )
    bias8 = jnp.concatenate(
        [bias_ref[:, h1 + LANE :], jnp.zeros((1, LANE - first - classes), F32)], axis=1
    )

    pre6 = mxu(feat_ref[...], w6[...]) + bias_ref[:, :h1]
    act6, back6 = gelu_pair(pre6)
    act6 = act6.astype(BF16)
    pre7 = mxu(act6, w7_low) + bias_ref[:, h1 : h1 + h2]
    act7, back7 = gelu_pair(pre7)
    act7 = act7.astype(BF16)
    logits = jnp.where(valid, mxu(act7, w8_low) + bias8, -1e30)
    shifted = logits - jnp.max(logits, axis=1, keepdims=True)
    logp = shifted - jnp.log(jnp.sum(jnp.exp(shifted), axis=1, keepdims=True))
    onehot = (labels == lanes).astype(F32)
    target = jnp.where(valid, (1.0 - smoothing) * onehot + smoothing / classes, 0.0)
    loss = jnp.sum(-jnp.sum(target * jnp.where(valid, logp, 0.0), axis=1, keepdims=True) * row_mask)
    weight = jnp.sum(target, axis=1, keepdims=True)
    dlogits = (row_mask * (jnp.exp(logp) * weight - target)).astype(BF16)
    dpre7 = (mxu(dlogits, w8_low, 1, 1) * back7).astype(BF16)
    dpre6 = (mxu(dpre7, w7_low, 1, 1) * back6).astype(BF16)

    square6 = jnp.zeros((8, h1), F32)
    most6 = jnp.zeros((8, h1), F32)
    for t in range(ins // tile):
        part = slice(t * tile, (t + 1) * tile)
        acc = resid6_ref[part, :] + mxu(feat_ref[:, part], dpre6, 0, 0)
        acc6_ref[part, :] = acc
        square6 = square6 + jnp.sum((acc * acc).reshape(tile // 8, 8, h1), axis=0)
        most6 = jnp.maximum(most6, jnp.max(jnp.abs(acc).reshape(tile // 8, 8, h1), axis=0))
    acc7 = mxu(dpre7, act6, 0, 0) + resid7_ref[...]
    acc7_ref[...] = acc7
    acc8 = mxu(dlogits, act7, 0, 0)[first : first + classes, :] + resid8_ref[...]
    acc8_ref[...] = acc8

    bound6 = clip_width * jnp.sqrt(jnp.sum(square6) * (1.0 / (ins * h1)))
    bound7 = clip_width * jnp.sqrt(jnp.sum(acc7 * acc7) * (1.0 / (h1 * h2)))
    bound8 = clip_width * jnp.sqrt(jnp.sum(acc8 * acc8) * (1.0 / (h2 * classes)))
    peak6 = jnp.minimum(jnp.max(most6), bound6)
    peak7 = jnp.minimum(jnp.max(jnp.abs(acc7)), bound7)
    peak8 = jnp.minimum(jnp.max(jnp.abs(acc8)), bound8)
    lane = lax.broadcasted_iota(jnp.int32, (1, LANE), 1) - (first + classes)
    tail = jnp.zeros((1, LANE), F32)
    count = count_ref[:, :1].astype(F32)
    for k, value in enumerate((peak6, peak7, peak8, loss, count, bound6, bound7, bound8)):
        tail = jnp.where(lane == k, value, tail)
    db6 = jnp.sum(dpre6.astype(F32), axis=0, keepdims=True)
    db7 = jnp.sum(dpre7.astype(F32), axis=0, keepdims=True)
    db8 = jnp.sum(dlogits.astype(F32), axis=0, keepdims=True)
    db7 = jnp.concatenate([db7, jnp.zeros((1, 2 * LANE - h2), F32)], axis=1)
    row = jnp.concatenate([db6, db7[:, :LANE], db7[:, LANE:] + db8 + tail], axis=1)
    stats_ref[...] = jnp.broadcast_to(row[None], stats_ref.shape)


def code_of(acc, bound, scale, noise):
    ramp = jnp.minimum(jnp.abs(acc), bound) * scale - (
        noise.astype(F32) * (ramp_slope / noise_levels) + 0.5 * ramp_slope / noise_levels
    )
    ramp = jnp.clip(ramp, 0.0, 1.0)
    return jnp.where(acc < 0, -ramp, ramp)


def lane_of(row_ref, k):
    return row_ref[0:1, k : k + 1]


def write_codes(sizes, places, same_core, head, acc6_ref, noise6_ref, code7, code8, out):
    ins, h1, h2, classes, rows6, rows7, rows8 = sizes
    peak, bound = lane_of(head, 0), lane_of(head, 3)
    scale = (1.0 + ramp_slope) / peak
    for at, place in enumerate(places):
        half = half_at(place, same_core)
        part = pl.ds(pl.multiple_of(half * rows6, 8), rows6)
        code = code_of(acc6_ref[part, :], bound, scale, noise6_ref[part, :])
        out[at, :rows6, :] = code.astype(BF16)
        region = code7[pl.ds(pl.multiple_of(half * rows7, 8), rows7), :]
        lead = (half % 2 == 0).astype(F32)
        region = region + lead * code8[pl.ds(pl.multiple_of((half // 2) * rows8, 8), rows8), :]
        out[at, rows6:, :] = fold(region).astype(BF16)


def first_codes_kernel(sizes, places, stats_ref, mine_ref, acc6_ref, noise6_ref, *refs):
    ins, h1, h2, classes, rows6, rows7, rows8 = sizes
    acc7_ref, noise7_ref, acc8_ref, noise8_ref, out_ref, head_ref, code7, code8 = refs
    at = h1 + h2 + classes
    most = jnp.max(stats_ref[:, :, at : at + 3], axis=0) + 1e-06
    images = jnp.sum(stats_ref[:, :, at + 4 : at + 5], axis=0)
    lane = lax.broadcasted_iota(jnp.int32, (1, LANE), 1)
    head = jnp.zeros((1, LANE), F32)
    for k in range(3):
        head = jnp.where(lane == k, most[:, k : k + 1], head)
        head = jnp.where(lane == 3 + k, mine_ref[0, :, at + 5 + k : at + 6 + k], head)
        head = jnp.where(lane == 6 + k, most[:, k : k + 1] / images, head)
    head_ref[...] = head
    ramp = 1.0 + ramp_slope
    small7 = code_of(acc7_ref[...], lane_of(head, 4), ramp / lane_of(head, 1), noise7_ref[...])
    small8 = code_of(acc8_ref[...], lane_of(head, 5), ramp / lane_of(head, 2), noise8_ref[...])
    code7[...] = upright(small7, 0)
    code8[...] = upright(small8, h2)
    write_codes(sizes, places, False, head, acc6_ref, noise6_ref, code7, code8, out_ref)


def codes_kernel(sizes, places, same_core, head_ref, acc6, noise6, code7, code8, *refs):
    write_codes(sizes, places, same_core, head_ref, acc6, noise6, code7, code8, refs[-1])


def resid_of(head, layer, acc, noise):
    peak = lane_of(head, layer)
    return acc - peak * code_of(acc, lane_of(head, 3 + layer), (1.0 + ramp_slope) / peak, noise)


def resid_kernel(tile, start, after_ref, head_ref, acc6_ref, noise6_ref, *refs):
    out_ref, hold, sems = refs[-3:]
    head = head_ref[...]
    copies = []
    for t in range(hold.shape[0] // tile):
        here, there = pl.ds(t * tile, tile), pl.ds(start + t * tile, tile)
        hold[here, :] = resid_of(head, 0, acc6_ref[there, :], noise6_ref[there, :])
        copies.append(pltpu.make_async_copy(hold.at[here], out_ref.at[there], sems.at[t]))
        copies[-1].start()
    for copy in copies:
        copy.wait()


def new_resid6_part(start, rows, after, head, acc6, noise6, before=None):
    tile = 3 * LANE
    ins = [after, head, acc6, noise6] + ([] if before is None else [before])
    return call(
        functools.partial(resid_kernel, tile, start),
        "new_resid",
        [VMEM] * 4 + [HBM] * (len(ins) - 4),
        HBM,
        shape_of(acc6.shape),
        [pltpu.VMEM((rows, acc6.shape[1]), F32), pltpu.SemaphoreType.DMA((rows // tile,))],
        megabytes=8,
        aliases={} if before is None else {4: 0},
    )(*ins)


def small_resids_kernel(after_ref, head_ref, acc7_ref, noise7_ref, acc8_ref, noise8_ref, *outs):
    head = head_ref[...]
    outs[0][...] = resid_of(head, 1, acc7_ref[...], noise7_ref[...])
    outs[1][...] = resid_of(head, 2, acc8_ref[...], noise8_ref[...])


def totals_kernel(after_ref, stats_ref, bias_ref, first_ref, second_ref, *refs):
    outs, loss_ref, images_ref, rows, sems = refs[:3], refs[3], refs[4], refs[5:8], refs[8]
    width = bias_ref.shape[1]
    total = jnp.sum(stats_ref[...], axis=0)
    images = total[:, width + 4 : width + 5]
    loss_ref[...] = total[:, width + 3 : width + 4]
    images_ref[...] = images
    rows[0][...], rows[1][...], rows[2][...] = adam_biases(
        bias_ref[...], first_ref[...], second_ref[...], total[:, :width] / images
    )
    copies = [
        pltpu.make_async_copy(row.at[0], out, sems.at[k])
        for k, (row, out) in enumerate(zip(rows, outs))
    ]
    for copy in copies:
        copy.start()
    for copy in copies:
        copy.wait()


def hold_kernel(after_ref, m6_ref, m7_ref, m8_ref, out_ref, half7, all8, sems):
    core = own_core()
    rows7, h2 = half7.shape
    rows6 = out_ref.shape[1] - rows7 * 2 // 3
    copies = [
        pltpu.make_async_copy(
            m6_ref.at[pl.ds(pl.multiple_of(core * rows6, 8), rows6)],
            out_ref.at[0, pl.ds(0, rows6)],
            sems.at[0],
        ),
        pltpu.make_async_copy(
            m7_ref.at[pl.ds(pl.multiple_of(core * rows7, 8), rows7)], half7, sems.at[1]
        ),
        pltpu.make_async_copy(m8_ref, all8, sems.at[2]),
    ]
    for copy in copies:
        copy.start()
    for copy in copies:
        copy.wait()
    lead = (core == 0).astype(F32)
    tall = jnp.zeros((rows7, 2 * LANE), F32)
    parts = all8[...]
    for _ in range(3):
        high = parts.astype(BF16)
        tall = tall + upright(high, h2)
        parts = parts - high.astype(F32)
    region = tall * lead + jnp.concatenate(
        [half7[...], jnp.zeros((rows7, 2 * LANE - h2), F32)], axis=1
    )
    out_ref[0, rows6:, :] = fold(region)


def hold_moments(after, moment6, moment7, moment8):
    rows6, h1 = moment6.shape[0] // 2, moment6.shape[1]
    rows7, h2 = moment7.shape[0] // 2, moment7.shape[1]
    return call(
        hold_kernel,
        "hold_moments",
        [VMEM] + [HBM] * 3,
        VMEM,
        shape_of((1, rows6 + rows7 * 2 // 3, h1)),
        [
            pltpu.VMEM((rows7, h2), F32),
            pltpu.VMEM(moment8.shape[::-1], F32),
            pltpu.SemaphoreType.DMA((3,)),
        ],
    )(after, moment6, moment7, moment8.T)


def moment_kernel(sizes, head_ref, held_ref, mine_ref, theirs_ref, out_ref, low_ref):
    ins, h1, h2, classes, rows6, rows7, rows8 = sizes
    codes = mine_ref[0].astype(F32) + theirs_ref[0].astype(F32)
    moment6 = momentum_decay * held_ref[0, :rows6] + lane_of(head_ref, 6) * codes[:rows6]
    column = lax.broadcasted_iota(jnp.int32, (rows7, 2 * LANE), 1)
    rate = fold(jnp.where(column < h2, lane_of(head_ref, 7), lane_of(head_ref, 8)))
    region = momentum_decay * held_ref[0, rows6:] + rate * codes[rows6:]
    out_ref[0, :rows6] = moment6
    out_ref[0, rows6:] = region
    low_ref[0, :rows6] = moment6.astype(BF16)
    low_ref[0, rows6:] = region.astype(BF16)


def schulz_chains(grams, iterates):
    diagonals = [shifted_eye(gram.shape[0], gram.shape[0], 0, F32) for gram in grams]
    for number in range(NS_STEPS):
        lefts = [left_parts(gram) for gram in grams]
        squares = [mxu(left, right_parts(gram)) for left, gram in zip(lefts, grams)]
        mixed = [
            right_parts(coef_a * diagonal + coef_b * gram + coef_c * square)
            for diagonal, gram, square in zip(diagonals, grams, squares)
        ]
        rows = [left_parts(iterate) for iterate in iterates]
        if number == NS_STEPS - 1:
            return [mxu(row, right) for row, right in zip(rows, mixed)]
        both = [
            mxu(jnp.concatenate([left, row], axis=0), right)
            for left, row, right in zip(lefts, rows, mixed)
        ]
        iterates = [value[gram.shape[0] :] for value, gram in zip(both, grams)]
        grams = [
            mxu(left_parts(value[: gram.shape[0]]), right)
            for value, gram, right in zip(both, grams, mixed)
        ]


def grams_of(sizes, ref):
    rows6 = sizes[4]
    places = range(ref.shape[0])
    block = jnp.concatenate([ref[k, :rows6, :] for k in places], axis=0)
    region = [unfold(ref[k, rows6:, :].astype(F32)) for k in places]
    region = jnp.concatenate(region, axis=0).astype(BF16)
    return mxu(block, block, 0, 0), mxu(region, region, 0, 0)


def early_kernel(sizes, trio_ref, one_ref, moment_ref, four_ref, out6_ref, out78_ref, again_ref):
    relay_kernel(trio_ref, one_ref, four_ref)
    again_ref[...] = moment_ref[...]
    out6_ref[...], out78_ref[...] = grams_of(sizes, four_ref)


def late_kernel(sizes, own6_ref, own78_ref, trio_ref, one_ref, theirs_ref, trio2_ref, *outs):
    trio6, trio78 = grams_of(sizes, trio_ref)
    one6, one78 = grams_of(sizes, one_ref)
    outs[0][...] = own6_ref[...] + trio6 + one6
    outs[1][...] = own78_ref[...] + trio78 + one78
    four6, four78 = grams_of(sizes, theirs_ref)
    trio6, trio78 = grams_of(sizes, trio2_ref)
    outs[2][...] = four6 + trio6
    outs[3][...] = four78 + trio78


def momenta_kernel(sizes, mine_ref, theirs_ref, *refs):
    ins, h1, h2, classes, rows6, rows7, rows8 = sizes
    out6_ref, out7_ref, out8_ref, near6_ref, near78_ref, stage7, sems = refs
    core = own_core()
    copies = []
    region8 = None
    for k, (at, ref) in enumerate(((core, mine_ref), (1 - core, theirs_ref))):
        part = pl.ds(pl.multiple_of(at * rows6, 8), rows6)
        near6_ref[part, :] = ref[0, :rows6, :]
        copies.append(
            pltpu.make_async_copy(ref.at[0, pl.ds(0, rows6)], out6_ref.at[part], sems.at[k])
        )
        copies[-1].start()
        region = unfold(ref[0, rows6:, :])
        near78_ref[pl.ds(pl.multiple_of(at * rows7, 8), rows7), :] = region
        region8 = region if region8 is None else jnp.where(core == 0, region8, region)
    column = lax.broadcasted_iota(jnp.int32, (2 * rows7, 2 * LANE), 1)
    near78_ref[: 2 * rows7, :] = jnp.where(column < h2, near78_ref[: 2 * rows7, :], 0.0)
    near78_ref[2 * rows7 :, :] = jnp.where(column[:rows8] < h2, 0.0, region8[:rows8])
    stage7[...] = near78_ref[: 2 * rows7, :h2]
    copies.append(pltpu.make_async_copy(stage7, out7_ref, sems.at[2]))
    copies[-1].start()
    out8_ref[...] = turned(sizes, near78_ref[2 * rows7 :, LANE:])
    for copy in copies:
        copy.wait()


def turned(sizes, rows):
    ins, h1, h2, classes, rows6, rows7, rows8 = sizes
    square = jnp.concatenate([rows, jnp.zeros((LANE - rows8, LANE), F32)], axis=0)
    return square.T[h2 - LANE : h2 - LANE + classes, :rows8]


def update_kernel(sizes, own6, own78, other6, other78, one7_ref, *refs):
    ins, h1, h2, classes, rows6, rows7, rows8 = sizes
    near6_ref, near78_ref, w6_ref, w7_ref, w8_ref, *outs = refs
    new6_ref, new7_ref, new8_ref, low6_ref, low7_ref, low8_ref = outs
    last6, last78 = grams_of(sizes, one7_ref)
    gram6 = own6[...] + (other6[...] + last6)
    gram7 = own78[...] + (other78[...] + last78)

    size = 2 * LANE
    is7_row = lax.broadcasted_iota(jnp.int32, (size, size), 0) < h2
    is7_col = lax.broadcasted_iota(jnp.int32, (size, size), 1) < h2
    diagonal = shifted_eye(size, size, 0, F32)
    inverse6 = 1.0 / (jnp.sqrt(jnp.sum(gram6 * shifted_eye(h1, h1, 0, F32))) + 1e-07)
    trace7 = jnp.sum(jnp.where(is7_col, gram7 * diagonal, 0.0))
    trace8 = jnp.sum(jnp.where(is7_col, 0.0, gram7 * diagonal))
    inverse7 = 1.0 / (jnp.sqrt(trace7) + 1e-07)
    inverse8 = 1.0 / (jnp.sqrt(trace8) + 1e-07)
    inverse = jnp.where(is7_col[:1], inverse7, inverse8)
    gram7 = jnp.where(is7_row == is7_col, gram7 * (inverse * inverse), 0.0)
    iterate6, iterate7 = schulz_chains(
        [gram6 * (inverse6 * inverse6), gram7],
        [near6_ref[...] * inverse6, near78_ref[...] * inverse],
    )
    for iterate, w_ref, new_ref, low_ref in (
        (iterate6, w6_ref, new6_ref, low6_ref),
        (iterate7[: 2 * rows7, :h2], w7_ref, new7_ref, low7_ref),
        (turned(sizes, iterate7[2 * rows7 :, LANE:]), w8_ref, new8_ref, low8_ref),
    ):
        master = w_ref[...]
        value = master - muon_rate * (iterate + decay_rate * master)
        new_ref[...] = value
        low_ref[...] = value.astype(BF16)


def paired_plan(
    features,
    labels,
    counts,
    weight6,
    weight7,
    weight8,
    moment6,
    moment7,
    moment8,
    resid6,
    resid7,
    resid8,
    noise6,
    noise7,
    noise8,
    biases,
    bias_first,
    bias_second,
):
    ins, h1 = resid6.shape
    h2, classes = resid8.shape
    rows6 = weight6.shape[0] // 2
    rows7 = weight7.shape[0] // 2
    rows8 = weight8.shape[0]
    sizes = (ins, h1, h2, classes, rows6, rows7, rows8)
    devices = 32
    half = (rows6 + rows7 * 2 // 3, h1)

    packed = pack_weights(weight6, weight7, weight8)
    staged = stage(
        packed,
        counts,
        features,
        labels,
        biases,
        bias_first,
        bias_second,
        resid6,
        resid7.T,
        resid8.T,
        noise6,
        noise7.T,
        noise8.T,
    )
    features, labels, *bias_rows = staged[:5]
    resid6, resid7, resid8, noise6, noise7, noise8, count_row = staged[5:]
    halves, _ = gather_halves(packed, [(VMEM, count_row)])

    tile = 2 * LANE
    lanes = h1 + 2 * LANE
    acc6, acc7, acc8, stats = call(
        functools.partial(worker_kernel, sizes, tile),
        "worker",
        [VMEM] * 13,
        [VMEM] * 4,
        [
            shape_of((ins, h1)),
            shape_of((h2, h1)),
            shape_of((classes, h2)),
            shape_of((devices, 1, lanes)),
        ],
        [
            pltpu.VMEM((ins, h1), BF16),
            pltpu.VMEM((h1, 2 * LANE), F32),
            pltpu.VMEM((h2, LANE), F32),
        ],
        megabytes=16,
    )(*halves, count_row, features, labels, bias_rows[0], resid6, resid7, resid8)

    all_stats = lax.all_to_all(stats, BOTH, 0, 0, tiled=True)

    def halves_of(count):
        return shape_of((count,) + half, BF16)

    sent7, head, code7, code8 = call(
        functools.partial(first_codes_kernel, sizes, (7,)),
        "codes_first",
        [VMEM] * 8,
        [VMEM] * 4,
        [
            halves_of(1),
            shape_of((1, LANE)),
            shape_of((h1, 2 * LANE)),
            shape_of((h2, 2 * LANE)),
        ],
    )(all_stats, stats, acc6, noise6, acc7, noise7, acc8, noise8)

    def codes(places, same_core, after=()):
        return call(
            functools.partial(codes_kernel, sizes, places, same_core),
            "codes",
            [VMEM] * (5 + len(after)),
            VMEM,
            halves_of(len(places)),
        )(head, acc6, noise6, code7, code8, *after)

    got7 = swap(sent7, grp_perm(1))
    kept7 = codes((7,), True)
    sent456 = codes((4, 5, 6), False, (kept7,))
    got456 = swap(sent456, grp_perm(1))
    out7 = add((0, 0), (kept7, got7), 1, [(VMEM, sent456)])
    near7 = swap(out7, wide_perm(0))
    kept456 = codes((4, 5, 6), True, (out7,))
    out56 = add((1, 1), (kept456, got456), 2)
    near56 = swap(out56, wide_perm(0))
    near4 = swap(add((0, 0), (kept456, got456), 1), wide_perm(0))
    got3 = swap(codes((3,), False, (out56,)), grp_perm(1))
    far3 = add((0, 0, 0), (codes((3,), True, (out56,)), got3, near7), 1)
    near56 = passed(near56, (far3,), "passed_near")
    got012 = swap(codes((0, 1, 2), False, (far3,)), grp_perm(1))
    kept012 = codes((0, 1, 2), True, (far3,))
    totals = call(
        totals_kernel,
        "totals",
        [VMEM] * 5,
        [HBM] * 3 + [RESULT] * 2,
        [shape_of(biases.shape)] * 3 + [shape_of((1, 1))] * 2,
        [pltpu.VMEM((1, biases.shape[0]), F32)] * 3 + [pltpu.SemaphoreType.DMA((3,))],
    )(far3, all_stats, *bias_rows)
    flat = totals[:3]
    far3 = swap(far3, wide_perm(1))
    far2 = add((2, 2, 1), (kept012, got012, near56), 1, name="add_far2")
    far2 = swap(far2, wide_perm(1))
    last = add((1, 1, 0, 0), (kept012, got012, near56, far3), 1, [(HBM, row) for row in flat])
    new_resid6 = new_resid6_part(0, ins // 2, last, head, acc6, noise6)
    last = swap(last, wide_perm(2))
    mine = add((0,) * 5, (kept012, got012, near4, far2, last), 1, [(HBM, new_resid6)])
    held = hold_moments(mine, moment6, moment7, moment8)
    theirs = swap(mine, grp_perm(2))

    moment, moment_low = call(
        functools.partial(moment_kernel, sizes),
        "moment",
        [VMEM] * 4,
        [VMEM] * 2,
        [shape_of((1,) + half), shape_of((1,) + half, BF16)],
    )(head, held, mine, theirs)
    new_resid6 = new_resid6_part(
        ins // 2, ins // 2, moment_low, head, acc6, noise6, new_resid6
    )
    new_resid7, new_resid8 = call(
        small_resids_kernel,
        "small_resids",
        [VMEM] * 6,
        [RESULT] * 2,
        [shape_of(acc7.shape), shape_of(acc8.shape)],
    )(moment_low, head, acc7, noise7, acc8, noise8)
    grams = [shape_of((h1, h1)), shape_of((2 * LANE, 2 * LANE))]

    def beside_last(trio, one3):
        four, *early, again = call(
            functools.partial(early_kernel, sizes),
            "early_grams",
            [VMEM] * 3,
            [VMEM] * 4,
            [halves_of(4), *grams, shape_of((1,) + half)],
            megabytes=8,
        )(trio, one3, moment)
        momenta = call(
            functools.partial(momenta_kernel, sizes),
            "momenta",
            [VMEM] * 2,
            [HBM, HBM, RESULT, VMEM, VMEM],
            [
                shape_of(moment6.shape),
                shape_of(moment7.shape),
                shape_of(moment8.shape[::-1]),
                shape_of(moment6.shape),
                shape_of((2 * rows7 + rows8, 2 * LANE)),
            ],
            [pltpu.VMEM(moment7.shape, F32), pltpu.SemaphoreType.DMA((3,))],
        )(again, swap(again, grp_perm(1)))
        return four, [momenta[3], *early, *momenta]

    moments, done = gather_halves(
        moment_low, [(HBM, new_resid6), (HBM, new_resid8)], beside_last
    )
    early, (mom6, mom7, mom8, near6, near78) = done[1:3], done[3:]
    late = call(
        functools.partial(late_kernel, sizes),
        "late_grams",
        [VMEM] * 6,
        [VMEM] * 4,
        grams * 2,
        megabytes=8,
    )(*early, *moments[1:5])

    updated = call(
        functools.partial(update_kernel, sizes),
        "update",
        [VMEM] * 10,
        [RESULT] * 6,
        [
            shape_of(weight6.shape),
            shape_of(weight7.shape),
            shape_of(weight8.shape[::-1]),
            shape_of(weight6.shape, BF16),
            shape_of(weight7.shape, BF16),
            shape_of(weight8.shape[::-1], BF16),
        ],
        megabytes=16,
    )(*late, moments[5], near6, near78, weight6, weight7, weight8.T)
    new6, new7, new8, low6, low7, low8 = updated
    return (
        new6,
        new7,
        new8.T,
        low6,
        low7,
        low8.T,
        mom6,
        mom7,
        mom8.T,
        new_resid6,
        new_resid7.T,
        new_resid8.T,
        *flat,
        *[array.reshape(()) for array in totals[3:]],
    )


def on_device(*arrays):
    (ins, h1), (_, h2), (_, classes) = [array.shape for array in arrays[9:12]]
    rows6, rows7, rows8 = [array.shape[0] for array in arrays[3:6]]
    paired = (
        (lax.axis_size("grp"), lax.axis_size("wide")) == (4, 8)
        and h1 == 3 * LANE
        and LANE < h2 < 2 * LANE
        and h2 + classes <= 2 * LANE
        and rows6 % 32 == 0
        and rows7 == rows8 * 2
        and rows8 % 24 == 0
        and ins % (2 * LANE) == 0
        and 16 * rows7 // 2 == h1
    )
    return (paired_plan if paired else general_plan)(*arrays)


def solution(mesh):
    split_both = P(BOTH, None)
    split_wide = P("wide", None)
    return jax.shard_map(
        on_device,
        mesh=mesh,
        in_specs=(
            split_both,
            P(BOTH),
            P(BOTH),
            *[split_wide] * 6,
            *[split_both] * 6,
            P(),
            P(),
            P(),
        ),
        out_specs=(*[split_wide] * 9, *[split_both] * 3, P(), P(), P(), P(), P()),
        check_vma=False,
    )
```

```python
import functools

import jax
import jax.numpy as jnp
from jax import lax
from jax.experimental import pallas as pl
from jax.experimental.pallas import tpu as pltpu
from jax.sharding import PartitionSpec as P

NS_STEPS = 5
ADAM_STEP = 10


highest = lax.Precision.HIGHEST
smoothing = 0.1
clip_width = 2.5
noise_levels = 1024.0
ramp_slope = 2.0
momentum_decay = 0.95
muon_rate = 0.6
decay_rate = 0.01
coef_a = 3.4445
coef_b = -4.775
coef_c = 2.0315
beta_first = 0.9
beta_second = 0.999
bias_rate = 0.05
adam_eps = 1e-08

F32 = jnp.float32
BF16 = jnp.bfloat16
LANE = 128
BOTH = ("grp", "wide")


def dithered_code(clipped, peak, noise):
    ratio = jnp.abs(clipped) / peak
    dither = (noise.astype(jnp.float32) + 0.5) / noise_levels
    return jnp.sign(clipped) * jnp.clip(ramp_slope * (ratio - dither) + ratio, 0.0, 1.0)


def gram_of(iterate):
    return jnp.dot(iterate.T, iterate, precision=highest)


def schulz_step(iterate, gram_matrix):
    mixed = coef_b * gram_matrix + coef_c * jnp.dot(gram_matrix, gram_matrix, precision=highest)
    return coef_a * iterate + jnp.dot(iterate, mixed, precision=highest)


def layer_forward(inputs_b, weight_b, bias_part):
    return jnp.dot(inputs_b, weight_b, preferred_element_type=jnp.float32) + bias_part


def layer_backward(inputs_b, weight_b, grad_pre):
    grad_low = grad_pre.astype(jnp.bfloat16)
    weight_grad = jnp.einsum("ri,ro->io", inputs_b, grad_low, preferred_element_type=jnp.float32)
    bias_grad = jnp.sum(grad_low.astype(jnp.float32), axis=0)
    grad_inputs = jnp.einsum("ro,io->ri", grad_low, weight_b, preferred_element_type=jnp.float32)
    return (weight_grad, bias_grad, grad_inputs)


def adam_biases(biases, bias_first, bias_second, bias_grad):
    first_new = beta_first * bias_first + (1.0 - beta_first) * bias_grad
    second_new = beta_second * bias_second + (1.0 - beta_second) * bias_grad * bias_grad
    first_hat = first_new / (1.0 - beta_first**ADAM_STEP)
    second_hat = second_new / (1.0 - beta_second**ADAM_STEP)
    biases_new = biases - bias_rate * (
        first_hat / (jnp.sqrt(second_hat) + adam_eps) + decay_rate * biases
    )
    return biases_new, first_new, second_new


def general_plan(
    features,
    labels,
    counts,
    weight6,
    weight7,
    weight8,
    moment6,
    moment7,
    moment8,
    resid6,
    resid7,
    resid8,
    noise6,
    noise7,
    noise8,
    biases,
    bias_first,
    bias_second,
):
    masters = (weight6, weight7, weight8)
    weights_b = [
        lax.all_gather(weight.astype(jnp.bfloat16), "wide", axis=0, tiled=True)
        for weight in masters
    ]
    widths = [weights_b[0].shape[1], weights_b[1].shape[1], weights_b[2].shape[1]]
    bias_parts = [
        biases[: widths[0]],
        biases[widths[0] : widths[0] + widths[1]],
        biases[widths[0] + widths[1] :],
    ]
    row_mask = (jnp.arange(features.shape[0]) < counts[0]).astype(jnp.float32)
    inputs_list = [features]
    gelu_backs = []
    logits = None
    for which_layer in range(3):
        pre_act = layer_forward(
            inputs_list[which_layer], weights_b[which_layer], bias_parts[which_layer]
        )
        if which_layer < 2:
            activ, gelu_back = jax.vjp(jax.nn.gelu, pre_act)
            inputs_list.append(activ.astype(jnp.bfloat16))
            gelu_backs.append(gelu_back)
        else:
            logits = pre_act
    logp = jax.nn.log_softmax(logits, axis=-1)
    onehot = (labels[:, None] == jnp.arange(widths[2])[None, :]).astype(jnp.float32)
    target = (1.0 - smoothing) * onehot + smoothing / widths[2]
    worker_loss = jnp.sum(-jnp.sum(target * logp, axis=-1) * row_mask)
    upstream = -target * row_mask[:, None]
    grad_pre = upstream - jnp.exp(logp) * jnp.sum(upstream, axis=-1, keepdims=True)
    weight_grads = [None, None, None]
    bias_grads = [None, None, None]
    for which_layer in (2, 1, 0):
        weight_grads[which_layer], bias_grads[which_layer], grad_inputs = layer_backward(
            inputs_list[which_layer], weights_b[which_layer], grad_pre
        )
        if which_layer > 0:
            grad_pre = gelu_backs[which_layer - 1](grad_inputs)[0]
    resids = (resid6, resid7, resid8)
    noises = (noise6, noise7, noise8)
    accs = [weight_grads[k] + resids[k] for k in range(3)]
    clipped_list = []
    for acc in accs:
        bound = clip_width * jnp.sqrt(jnp.mean(acc * acc))
        clipped_list.append(jnp.clip(acc, -bound, bound))
    peak_list = lax.pmax(tuple(jnp.max(jnp.abs(clipped)) for clipped in clipped_list), BOTH)
    peak_list = [p + 1e-06 for p in peak_list]
    code_list = [dithered_code(clipped_list[k], peak_list[k], noises[k]) for k in range(3)]
    new_resids = [accs[k] - peak_list[k] * code_list[k] for k in range(3)]
    loss_total, image_total, bias_total = lax.psum(
        (worker_loss, jnp.sum(row_mask), jnp.concatenate(bias_grads)), BOTH
    )
    code_rows = [
        lax.psum_scatter(code, "wide", scatter_dimension=0, tiled=True) for code in code_list
    ]
    code_sums = lax.psum(tuple(code_rows), "grp")
    moments = (moment6, moment7, moment8)
    new_moments = [
        momentum_decay * moments[k] + peak_list[k] * code_sums[k] / image_total for k in range(3)
    ]
    full_moments = [
        lax.all_gather(moment, "wide", axis=0, tiled=True) for moment in new_moments
    ]
    row_block = lax.axis_index("wide")
    iterates = []
    for k in range(3):
        whole = full_moments[k]
        iterate = whole / (jnp.sqrt(jnp.sum(whole * whole)) + 1e-07)
        for step_num in range(NS_STEPS):
            iterate = schulz_step(iterate, gram_of(iterate))
        row_count = new_moments[k].shape[0]
        iterates.append(lax.dynamic_slice_in_dim(iterate, row_block * row_count, row_count, 0))
    new_weights = [
        masters[k] - muon_rate * (iterates[k] + decay_rate * masters[k]) for k in range(3)
    ]
    new_biases = adam_biases(biases, bias_first, bias_second, bias_total / image_total)
    return (
        *new_weights,
        *[weight.astype(jnp.bfloat16) for weight in new_weights],
        *new_moments,
        *new_resids,
        *new_biases,
        loss_total,
        image_total,
    )


ORDERS = ((2, 1, 4), (1, 2, 4))


def wide_perm(phase):
    return [
        (g * 8 + w, g * 8 + (w ^ ORDERS[g % 2][phase])) for g in range(4) for w in range(8)
    ]


def grp_perm(bit):
    return [(g * 8 + w, (g ^ bit) * 8 + w) for g in range(4) for w in range(8)]


def swap(array, perm):
    return lax.ppermute(array, BOTH, perm)


def own_core():
    return lax.rem(lax.axis_index("grp"), 2)


def half_at(place, same_core):
    core = own_core() if same_core else 1 - own_core()
    masks = [
        sum(order[phase] for phase in range(3) if place & (4 >> phase)) for order in ORDERS
    ]
    return 2 * (lax.axis_index("wide") ^ jnp.where(core == 0, masks[0], masks[1])) + core


def dims(contract_left, contract_right):
    return (((contract_left,), (contract_right,)), ((), ()))


def mxu(left, right, contract_left=1, contract_right=0):
    return lax.dot_general(
        left, right, dims(contract_left, contract_right), preferred_element_type=F32
    )


def split(value):
    high = value.astype(BF16)
    return high, (value - high.astype(F32)).astype(BF16)


def left_parts(value):
    high, rest = split(value)
    return jnp.concatenate([high, high, rest], axis=1)


def right_parts(value):
    high, rest = split(value)
    return jnp.concatenate([high, rest, high], axis=0)


def shifted_eye(rows, cols, shift, dtype):
    at = lax.broadcasted_iota(jnp.int32, (rows, cols), 0) + shift
    return (at == lax.broadcasted_iota(jnp.int32, (rows, cols), 1)).astype(dtype)


def upright(flat, shift, dtype=BF16):
    return mxu(flat.astype(BF16), shifted_eye(flat.shape[0], 2 * LANE, shift, BF16), 0, 0)


def fold(region):
    n = region.shape[0] // 3
    third = jnp.concatenate([region[2 * n :, :LANE], region[2 * n :, LANE:]], axis=0)
    return jnp.concatenate([region[: 2 * n], third], axis=1)


def unfold(folded):
    n = folded.shape[0] // 2
    last = jnp.concatenate([folded[:n, 2 * LANE :], folded[n:, 2 * LANE :]], axis=1)
    return jnp.concatenate([folded[:, : 2 * LANE], last], axis=0)


HBM = pl.BlockSpec(memory_space=pltpu.HBM)
SMEM = pl.BlockSpec(memory_space=pltpu.SMEM)
VMEM = pl.BlockSpec(memory_space=pltpu.VMEM)
RESULT = pl.BlockSpec(memory_space=pltpu.VMEM)


def shape_of(shape, dtype=F32):
    return jax.ShapeDtypeStruct(shape, dtype)


MICROS = {"passed_last": 20.0}


def placed(shape, spec):
    if spec is HBM:
        return pltpu.HBM(shape.shape, shape.dtype)
    return pltpu.VMEM(shape.shape, shape.dtype) if spec is VMEM else shape


def call(kernel, name, in_specs, out_specs, out_shape, scratch=(), megabytes=4, aliases=None):
    many = isinstance(out_shape, list)
    shapes = [
        placed(shape, spec)
        for shape, spec in zip(
            out_shape if many else [out_shape], out_specs if many else [out_specs]
        )
    ]
    kernel_call = pl.pallas_call(
        kernel,
        in_specs=in_specs,
        out_specs=out_specs,
        out_shape=shapes if many else shapes[0],
        scratch_shapes=list(scratch),
        compiler_params=pltpu.CompilerParams(vmem_limit_bytes=megabytes * 1024 * 1024),
        cost_estimate=pl.CostEstimate(
            flops=int(MICROS.get(name, 0.0) * 1.15e9), bytes_accessed=0, transcendentals=0
        ),
        input_output_aliases=aliases or {},
        name=name,
    )

    def run(*arrays):
        return kernel_call(
            *[
                pltpu.with_memory_space_constraint(array, pltpu.HBM) if spec is HBM else array
                for array, spec in zip(arrays, in_specs)
            ]
        )

    return run


def pack_kernel(w6_ref, w7_ref, w8_ref, out_ref, half6, half7, all8, sems):
    core = own_core()
    rows6, rows7 = half6.shape[0], half7.shape[0]
    copies = [
        pltpu.make_async_copy(
            w6_ref.at[pl.ds(pl.multiple_of(core * rows6, 8), rows6)], half6, sems.at[0]
        ),
        pltpu.make_async_copy(
            w7_ref.at[pl.ds(pl.multiple_of(core * rows7, 8), rows7)], half7, sems.at[1]
        ),
        pltpu.make_async_copy(w8_ref, all8, sems.at[2]),
    ]
    for copy in copies:
        copy.start()
    for copy in copies:
        copy.wait()
    out_ref[0, :rows6, :] = half6[...].astype(BF16)
    h2 = half7.shape[1]
    lead = (core == 0).astype(F32)
    region = upright(all8[...], h2) * lead + jnp.concatenate(
        [half7[...], jnp.zeros((rows7, 2 * LANE - h2), F32)], axis=1
    )
    out_ref[0, rows6:, :] = fold(region).astype(BF16)


def pack_weights(weight6, weight7, weight8):
    rows6, h1 = weight6.shape[0] // 2, weight6.shape[1]
    rows7, h2 = weight7.shape[0] // 2, weight7.shape[1]
    return call(
        pack_kernel,
        "pack_weights",
        [HBM] * 3,
        VMEM,
        shape_of((1, rows6 + rows7 * 2 // 3, h1), BF16),
        [
            pltpu.VMEM((rows6, h1), F32),
            pltpu.VMEM((rows7, h2), F32),
            pltpu.VMEM(weight8.shape[::-1], F32),
            pltpu.SemaphoreType.DMA((3,)),
        ],
    )(weight6, weight7, weight8.T)


def stage_kernel(count, after_ref, images_ref, *refs):
    ins, outs, token_ref, sems = refs[:count], refs[count:-2], refs[-2], refs[-1]
    copies = [
        pltpu.make_async_copy(
            source, target if len(source.shape) == len(target.shape) else target.at[0], sems.at[k]
        )
        for k, (source, target) in enumerate(zip(ins, outs))
    ]
    for copy in copies:
        copy.start()
    token_ref[...] = jnp.full(token_ref.shape, images_ref[0], jnp.int32)
    for copy in copies:
        copy.wait()


def stage(after, counts, *arrays):
    count = len(arrays)
    shapes = [(1,) * (2 - array.ndim) + array.shape for array in arrays]
    return call(
        functools.partial(stage_kernel, count),
        "stage",
        [VMEM, SMEM] + [HBM] * count,
        [VMEM] * (count + 1),
        [shape_of(shape, array.dtype) for shape, array in zip(shapes, arrays)]
        + [shape_of((1, LANE), jnp.int32)],
        [pltpu.SemaphoreType.DMA((count,))],
    )(after, counts, *arrays)


def add_kernel(picks, size, *refs):
    for k in range(size):
        total = None
        for ref, pick in zip(refs, picks):
            part = ref[pick + k].astype(F32)
            total = part if total is None else total + part
        refs[-1][k] = total.astype(BF16)


def add(picks, arrays, size, after=(), name="add"):
    shape = shape_of((size,) + arrays[0].shape[1:], BF16)
    specs = [VMEM] * len(arrays) + [spec for spec, _ in after]
    return call(functools.partial(add_kernel, picks, size), name, specs, VMEM, shape)(
        *arrays, *[array for _, array in after]
    )


def pass_kernel(in_ref, *refs):
    refs[-1][...] = in_ref[...]


def passed(array, after, name="passed"):
    specs = [VMEM] * (1 + len(after))
    shape = shape_of(array.shape, array.dtype)
    return call(pass_kernel, name, specs, VMEM, shape)(array, *after)


def first_join_kernel(own_ref, far_ref, mid_ref, *refs):
    trio_ref, again_ref = refs[-2:]
    for k, ref in enumerate((own_ref, far_ref, mid_ref)):
        trio_ref[k] = ref[0]
    again_ref[...] = far_ref[...]


def relay_kernel(trio_ref, one_ref, *refs):
    outs = refs[len(refs) // 2 :]
    count = trio_ref.shape[0]
    outs[0][:count] = trio_ref[...]
    outs[0][count:] = one_ref[...]
    if len(refs) > 1:
        outs[1][...] = refs[0][...]


def relay(trio, one, beside=()):
    joined = shape_of((trio.shape[0] + one.shape[0],) + one.shape[1:], one.dtype)
    shapes = [joined] + [shape_of(array.shape, array.dtype) for array in beside]
    ins = [trio, one, *beside]
    return call(relay_kernel, "relay", [VMEM] * len(ins), [VMEM] * len(shapes), shapes)(*ins)


def gather_halves(own, after=(), work=None):
    far = swap(own, wide_perm(2))
    mid = swap(own, wide_perm(1))
    trio, far = call(
        first_join_kernel,
        "first_join",
        [VMEM] * 3 + [spec for spec, _ in after],
        [VMEM] * 2,
        [shape_of((3,) + own.shape[1:], BF16), shape_of(own.shape, BF16)],
    )(own, far, mid, *[array for _, array in after])
    trio4 = swap(trio, wide_perm(0))
    one3 = swap(far, wide_perm(1))
    one7 = swap(one3, wide_perm(0))
    four, done = (relay(trio, one3)[0], None) if work is None else work(trio, one3)
    trio4 = passed(trio4, (four,))
    one7 = passed(one7, done[:3] if done else (four,), "passed_last")
    mine = (four, trio4, one7)
    return (*mine, *[swap(part, grp_perm(1)) for part in mine]), done


def gelu_pair(pre):
    slope = 0.7978845608028654
    inner = slope * (pre + 0.044715 * pre * pre * pre)
    t = jnp.tanh(inner)
    value = 0.5 * pre * (1.0 + t)
    back = 0.5 * (1.0 + t) + 0.5 * pre * (1.0 - t * t) * slope * (1.0 + 3 * 0.044715 * pre * pre)
    return value, back


def place_all(sizes, refs, all6, all7, all8):
    ins, h1, h2, classes, rows6, rows7, rows8 = sizes
    for at in range(16):
        place = at % 8
        ref, q = refs[3 * (at // 8) + (0, 0, 0, 0, 1, 1, 1, 2)[place]], place % 4 % (4 - place // 4)
        half = half_at(place, at < 8)
        all6[pl.ds(pl.multiple_of(half * rows6, 16), rows6), :] = ref[q, :rows6, :]
        region = unfold(ref[q, rows6:, :].astype(F32))
        all7[pl.ds(pl.multiple_of(half * rows7, 8), rows7), :] = region

        @pl.when(half % 2 == 0)
        def _():
            row = pl.multiple_of((half // 2) * rows8, 8)
            all8[pl.ds(row, rows8), :] = region[:rows8, LANE:]


def worker_kernel(sizes, tile, *refs):
    ins, h1, h2, classes, rows6, rows7, rows8 = sizes
    halves, refs = refs[:6], refs[6:]
    count_ref, feat_ref, label_ref, bias_ref, resid6_ref, resid7_ref, resid8_ref = refs[:7]
    acc6_ref, acc7_ref, acc8_ref, stats_ref, w6, w7, w8 = refs[7:]
    first = h2 - LANE

    place_all(sizes, halves, w6, w7, w8)
    w7_low = w7[:, :h2].astype(BF16)
    w8_low = w8[...].astype(BF16)

    rows = feat_ref.shape[0]
    row_mask = (lax.broadcasted_iota(jnp.int32, (rows, 1), 0) < count_ref[:, :1]).astype(F32)
    lanes = lax.broadcasted_iota(jnp.int32, (rows, LANE), 1) - first
    valid = (lanes >= 0) & (lanes < classes)
    labels = jnp.sum(
        jnp.where(shifted_eye(rows, rows, 0, jnp.bool_), label_ref[...], 0), axis=1, keepdims=True
    )
    bias8 = jnp.concatenate(
        [bias_ref[:, h1 + LANE :], jnp.zeros((1, LANE - first - classes), F32)], axis=1
    )

    pre6 = mxu(feat_ref[...], w6[...]) + bias_ref[:, :h1]
    act6, back6 = gelu_pair(pre6)
    act6 = act6.astype(BF16)
    pre7 = mxu(act6, w7_low) + bias_ref[:, h1 : h1 + h2]
    act7, back7 = gelu_pair(pre7)
    act7 = act7.astype(BF16)
    logits = jnp.where(valid, mxu(act7, w8_low) + bias8, -1e30)
    shifted = logits - jnp.max(logits, axis=1, keepdims=True)
    logp = shifted - jnp.log(jnp.sum(jnp.exp(shifted), axis=1, keepdims=True))
    onehot = (labels == lanes).astype(F32)
    target = jnp.where(valid, (1.0 - smoothing) * onehot + smoothing / classes, 0.0)
    loss = jnp.sum(-jnp.sum(target * jnp.where(valid, logp, 0.0), axis=1, keepdims=True) * row_mask)
    weight = jnp.sum(target, axis=1, keepdims=True)
    dlogits = (row_mask * (jnp.exp(logp) * weight - target)).astype(BF16)
    dpre7 = (mxu(dlogits, w8_low, 1, 1) * back7).astype(BF16)
    dpre6 = (mxu(dpre7, w7_low, 1, 1) * back6).astype(BF16)

    square6 = jnp.zeros((8, h1), F32)
    most6 = jnp.zeros((8, h1), F32)
    for t in range(ins // tile):
        part = slice(t * tile, (t + 1) * tile)
        acc = resid6_ref[part, :] + mxu(feat_ref[:, part], dpre6, 0, 0)
        acc6_ref[part, :] = acc
        square6 = square6 + jnp.sum((acc * acc).reshape(tile // 8, 8, h1), axis=0)
        most6 = jnp.maximum(most6, jnp.max(jnp.abs(acc).reshape(tile // 8, 8, h1), axis=0))
    acc7 = mxu(dpre7, act6, 0, 0) + resid7_ref[...]
    acc7_ref[...] = acc7
    acc8 = mxu(dlogits, act7, 0, 0)[first : first + classes, :] + resid8_ref[...]
    acc8_ref[...] = acc8

    bound6 = clip_width * jnp.sqrt(jnp.sum(square6) * (1.0 / (ins * h1)))
    bound7 = clip_width * jnp.sqrt(jnp.sum(acc7 * acc7) * (1.0 / (h1 * h2)))
    bound8 = clip_width * jnp.sqrt(jnp.sum(acc8 * acc8) * (1.0 / (h2 * classes)))
    peak6 = jnp.minimum(jnp.max(most6), bound6)
    peak7 = jnp.minimum(jnp.max(jnp.abs(acc7)), bound7)
    peak8 = jnp.minimum(jnp.max(jnp.abs(acc8)), bound8)
    lane = lax.broadcasted_iota(jnp.int32, (1, LANE), 1) - (first + classes)
    tail = jnp.zeros((1, LANE), F32)
    count = count_ref[:, :1].astype(F32)
    for k, value in enumerate((peak6, peak7, peak8, loss, count, bound6, bound7, bound8)):
        tail = jnp.where(lane == k, value, tail)
    db6 = jnp.sum(dpre6.astype(F32), axis=0, keepdims=True)
    db7 = jnp.sum(dpre7.astype(F32), axis=0, keepdims=True)
    db8 = jnp.sum(dlogits.astype(F32), axis=0, keepdims=True)
    db7 = jnp.concatenate([db7, jnp.zeros((1, 2 * LANE - h2), F32)], axis=1)
    row = jnp.concatenate([db6, db7[:, :LANE], db7[:, LANE:] + db8 + tail], axis=1)
    stats_ref[...] = jnp.broadcast_to(row[None], stats_ref.shape)


def code_of(acc, bound, scale, noise):
    ramp = jnp.minimum(jnp.abs(acc), bound) * scale - (
        noise.astype(F32) * (ramp_slope / noise_levels) + 0.5 * ramp_slope / noise_levels
    )
    ramp = jnp.clip(ramp, 0.0, 1.0)
    return jnp.where(acc < 0, -ramp, ramp)


def lane_of(row_ref, k):
    return row_ref[0:1, k : k + 1]


def write_codes(sizes, places, same_core, head, acc6_ref, noise6_ref, code7, code8, out):
    ins, h1, h2, classes, rows6, rows7, rows8 = sizes
    peak, bound = lane_of(head, 0), lane_of(head, 3)
    scale = (1.0 + ramp_slope) / peak
    for at, place in enumerate(places):
        half = half_at(place, same_core)
        part = pl.ds(pl.multiple_of(half * rows6, 8), rows6)
        code = code_of(acc6_ref[part, :], bound, scale, noise6_ref[part, :])
        out[at, :rows6, :] = code.astype(BF16)
        region = code7[pl.ds(pl.multiple_of(half * rows7, 8), rows7), :]
        lead = (half % 2 == 0).astype(F32)
        region = region + lead * code8[pl.ds(pl.multiple_of((half // 2) * rows8, 8), rows8), :]
        out[at, rows6:, :] = fold(region).astype(BF16)


def first_codes_kernel(sizes, places, stats_ref, mine_ref, acc6_ref, noise6_ref, *refs):
    ins, h1, h2, classes, rows6, rows7, rows8 = sizes
    acc7_ref, noise7_ref, acc8_ref, noise8_ref, out_ref, head_ref, code7, code8 = refs
    at = h1 + h2 + classes
    most = jnp.max(stats_ref[:, :, at : at + 3], axis=0) + 1e-06
    images = jnp.sum(stats_ref[:, :, at + 4 : at + 5], axis=0)
    lane = lax.broadcasted_iota(jnp.int32, (1, LANE), 1)
    head = jnp.zeros((1, LANE), F32)
    for k in range(3):
        head = jnp.where(lane == k, most[:, k : k + 1], head)
        head = jnp.where(lane == 3 + k, mine_ref[0, :, at + 5 + k : at + 6 + k], head)
        head = jnp.where(lane == 6 + k, most[:, k : k + 1] / images, head)
    head_ref[...] = head
    ramp = 1.0 + ramp_slope
    small7 = code_of(acc7_ref[...], lane_of(head, 4), ramp / lane_of(head, 1), noise7_ref[...])
    small8 = code_of(acc8_ref[...], lane_of(head, 5), ramp / lane_of(head, 2), noise8_ref[...])
    code7[...] = upright(small7, 0)
    code8[...] = upright(small8, h2)
    write_codes(sizes, places, False, head, acc6_ref, noise6_ref, code7, code8, out_ref)


def codes_kernel(sizes, places, same_core, head_ref, acc6, noise6, code7, code8, *refs):
    write_codes(sizes, places, same_core, head_ref, acc6, noise6, code7, code8, refs[-1])


def resid_of(head, layer, acc, noise):
    peak = lane_of(head, layer)
    return acc - peak * code_of(acc, lane_of(head, 3 + layer), (1.0 + ramp_slope) / peak, noise)


def resid_kernel(tile, start, after_ref, head_ref, acc6_ref, noise6_ref, *refs):
    out_ref, hold, sems = refs[-3:]
    head = head_ref[...]
    copies = []
    for t in range(hold.shape[0] // tile):
        here, there = pl.ds(t * tile, tile), pl.ds(start + t * tile, tile)
        hold[here, :] = resid_of(head, 0, acc6_ref[there, :], noise6_ref[there, :])
        copies.append(pltpu.make_async_copy(hold.at[here], out_ref.at[there], sems.at[t]))
        copies[-1].start()
    for copy in copies:
        copy.wait()


def new_resid6_part(start, rows, after, head, acc6, noise6, before=None):
    tile = 3 * LANE
    ins = [after, head, acc6, noise6] + ([] if before is None else [before])
    return call(
        functools.partial(resid_kernel, tile, start),
        "new_resid",
        [VMEM] * 4 + [HBM] * (len(ins) - 4),
        HBM,
        shape_of(acc6.shape),
        [pltpu.VMEM((rows, acc6.shape[1]), F32), pltpu.SemaphoreType.DMA((rows // tile,))],
        megabytes=8,
        aliases={} if before is None else {4: 0},
    )(*ins)


def small_resids_kernel(after_ref, head_ref, acc7_ref, noise7_ref, acc8_ref, noise8_ref, *outs):
    head = head_ref[...]
    outs[0][...] = resid_of(head, 1, acc7_ref[...], noise7_ref[...])
    outs[1][...] = resid_of(head, 2, acc8_ref[...], noise8_ref[...])


def totals_kernel(after_ref, stats_ref, bias_ref, first_ref, second_ref, *refs):
    outs, loss_ref, images_ref, rows, sems = refs[:3], refs[3], refs[4], refs[5:8], refs[8]
    width = bias_ref.shape[1]
    total = jnp.sum(stats_ref[...], axis=0)
    images = total[:, width + 4 : width + 5]
    loss_ref[...] = total[:, width + 3 : width + 4]
    images_ref[...] = images
    rows[0][...], rows[1][...], rows[2][...] = adam_biases(
        bias_ref[...], first_ref[...], second_ref[...], total[:, :width] / images
    )
    copies = [
        pltpu.make_async_copy(row.at[0], out, sems.at[k])
        for k, (row, out) in enumerate(zip(rows, outs))
    ]
    for copy in copies:
        copy.start()
    for copy in copies:
        copy.wait()


def hold_kernel(after_ref, m6_ref, m7_ref, m8_ref, out_ref, half7, all8, sems):
    core = own_core()
    rows7, h2 = half7.shape
    rows6 = out_ref.shape[1] - rows7 * 2 // 3
    copies = [
        pltpu.make_async_copy(
            m6_ref.at[pl.ds(pl.multiple_of(core * rows6, 8), rows6)],
            out_ref.at[0, pl.ds(0, rows6)],
            sems.at[0],
        ),
        pltpu.make_async_copy(
            m7_ref.at[pl.ds(pl.multiple_of(core * rows7, 8), rows7)], half7, sems.at[1]
        ),
        pltpu.make_async_copy(m8_ref, all8, sems.at[2]),
    ]
    for copy in copies:
        copy.start()
    for copy in copies:
        copy.wait()
    lead = (core == 0).astype(F32)
    tall = jnp.zeros((rows7, 2 * LANE), F32)
    parts = all8[...]
    for _ in range(3):
        high = parts.astype(BF16)
        tall = tall + upright(high, h2)
        parts = parts - high.astype(F32)
    region = tall * lead + jnp.concatenate(
        [half7[...], jnp.zeros((rows7, 2 * LANE - h2), F32)], axis=1
    )
    out_ref[0, rows6:, :] = fold(region)


def hold_moments(after, moment6, moment7, moment8):
    rows6, h1 = moment6.shape[0] // 2, moment6.shape[1]
    rows7, h2 = moment7.shape[0] // 2, moment7.shape[1]
    return call(
        hold_kernel,
        "hold_moments",
        [VMEM] + [HBM] * 3,
        VMEM,
        shape_of((1, rows6 + rows7 * 2 // 3, h1)),
        [
            pltpu.VMEM((rows7, h2), F32),
            pltpu.VMEM(moment8.shape[::-1], F32),
            pltpu.SemaphoreType.DMA((3,)),
        ],
    )(after, moment6, moment7, moment8.T)


def moment_kernel(sizes, head_ref, held_ref, mine_ref, theirs_ref, out_ref, low_ref):
    ins, h1, h2, classes, rows6, rows7, rows8 = sizes
    codes = mine_ref[0].astype(F32) + theirs_ref[0].astype(F32)
    moment6 = momentum_decay * held_ref[0, :rows6] + lane_of(head_ref, 6) * codes[:rows6]
    column = lax.broadcasted_iota(jnp.int32, (rows7, 2 * LANE), 1)
    rate = fold(jnp.where(column < h2, lane_of(head_ref, 7), lane_of(head_ref, 8)))
    region = momentum_decay * held_ref[0, rows6:] + rate * codes[rows6:]
    out_ref[0, :rows6] = moment6
    out_ref[0, rows6:] = region
    low_ref[0, :rows6] = moment6.astype(BF16)
    low_ref[0, rows6:] = region.astype(BF16)


def schulz_chains(grams, iterates):
    diagonals = [shifted_eye(gram.shape[0], gram.shape[0], 0, F32) for gram in grams]
    for number in range(NS_STEPS):
        lefts = [left_parts(gram) for gram in grams]
        squares = [mxu(left, right_parts(gram)) for left, gram in zip(lefts, grams)]
        mixed = [
            right_parts(coef_a * diagonal + coef_b * gram + coef_c * square)
            for diagonal, gram, square in zip(diagonals, grams, squares)
        ]
        rows = [left_parts(iterate) for iterate in iterates]
        if number == NS_STEPS - 1:
            return [mxu(row, right) for row, right in zip(rows, mixed)]
        both = [
            mxu(jnp.concatenate([left, row], axis=0), right)
            for left, row, right in zip(lefts, rows, mixed)
        ]
        iterates = [value[gram.shape[0] :] for value, gram in zip(both, grams)]
        grams = [
            mxu(left_parts(value[: gram.shape[0]]), right)
            for value, gram, right in zip(both, grams, mixed)
        ]


def grams_of(sizes, ref):
    rows6 = sizes[4]
    places = range(ref.shape[0])
    block = jnp.concatenate([ref[k, :rows6, :] for k in places], axis=0)
    region = [unfold(ref[k, rows6:, :].astype(F32)) for k in places]
    region = jnp.concatenate(region, axis=0).astype(BF16)
    return mxu(block, block, 0, 0), mxu(region, region, 0, 0)


def early_kernel(sizes, four_ref, out6_ref, out78_ref):
    out6_ref[...], out78_ref[...] = grams_of(sizes, four_ref)


def late_kernel(sizes, own6_ref, own78_ref, trio_ref, one_ref, theirs_ref, trio2_ref, *outs):
    trio6, trio78 = grams_of(sizes, trio_ref)
    one6, one78 = grams_of(sizes, one_ref)
    outs[0][...] = own6_ref[...] + trio6 + one6
    outs[1][...] = own78_ref[...] + trio78 + one78
    four6, four78 = grams_of(sizes, theirs_ref)
    trio6, trio78 = grams_of(sizes, trio2_ref)
    outs[2][...] = four6 + trio6
    outs[3][...] = four78 + trio78


def momenta_kernel(sizes, mine_ref, theirs_ref, *refs):
    ins, h1, h2, classes, rows6, rows7, rows8 = sizes
    out6_ref, out7_ref, out8_ref, near6_ref, near78_ref, stage7, sems = refs
    core = own_core()
    copies = []
    region8 = None
    for k, (at, ref) in enumerate(((core, mine_ref), (1 - core, theirs_ref))):
        part = pl.ds(pl.multiple_of(at * rows6, 8), rows6)
        near6_ref[part, :] = ref[0, :rows6, :]
        copies.append(
            pltpu.make_async_copy(ref.at[0, pl.ds(0, rows6)], out6_ref.at[part], sems.at[k])
        )
        copies[-1].start()
        region = unfold(ref[0, rows6:, :])
        near78_ref[pl.ds(pl.multiple_of(at * rows7, 8), rows7), :] = region
        region8 = region if region8 is None else jnp.where(core == 0, region8, region)
    column = lax.broadcasted_iota(jnp.int32, (2 * rows7, 2 * LANE), 1)
    near78_ref[: 2 * rows7, :] = jnp.where(column < h2, near78_ref[: 2 * rows7, :], 0.0)
    near78_ref[2 * rows7 :, :] = jnp.where(column[:rows8] < h2, 0.0, region8[:rows8])
    stage7[...] = near78_ref[: 2 * rows7, :h2]
    copies.append(pltpu.make_async_copy(stage7, out7_ref, sems.at[2]))
    copies[-1].start()
    out8_ref[...] = turned(sizes, near78_ref[2 * rows7 :, LANE:])
    for copy in copies:
        copy.wait()


def turned(sizes, rows):
    ins, h1, h2, classes, rows6, rows7, rows8 = sizes
    square = jnp.concatenate([rows, jnp.zeros((LANE - rows8, LANE), F32)], axis=0)
    return square.T[h2 - LANE : h2 - LANE + classes, :rows8]


def update_kernel(sizes, own6, own78, other6, other78, one7_ref, *refs):
    ins, h1, h2, classes, rows6, rows7, rows8 = sizes
    near6_ref, near78_ref, w6_ref, w7_ref, w8_ref, *outs = refs
    new6_ref, new7_ref, new8_ref, low6_ref, low7_ref, low8_ref = outs
    last6, last78 = grams_of(sizes, one7_ref)
    gram6 = own6[...] + (other6[...] + last6)
    gram7 = own78[...] + (other78[...] + last78)

    size = 2 * LANE
    is7_row = lax.broadcasted_iota(jnp.int32, (size, size), 0) < h2
    is7_col = lax.broadcasted_iota(jnp.int32, (size, size), 1) < h2
    diagonal = shifted_eye(size, size, 0, F32)
    inverse6 = 1.0 / (jnp.sqrt(jnp.sum(gram6 * shifted_eye(h1, h1, 0, F32))) + 1e-07)
    trace7 = jnp.sum(jnp.where(is7_col, gram7 * diagonal, 0.0))
    trace8 = jnp.sum(jnp.where(is7_col, 0.0, gram7 * diagonal))
    inverse7 = 1.0 / (jnp.sqrt(trace7) + 1e-07)
    inverse8 = 1.0 / (jnp.sqrt(trace8) + 1e-07)
    inverse = jnp.where(is7_col[:1], inverse7, inverse8)
    gram7 = jnp.where(is7_row == is7_col, gram7 * (inverse * inverse), 0.0)
    iterate6, iterate7 = schulz_chains(
        [gram6 * (inverse6 * inverse6), gram7],
        [near6_ref[...] * inverse6, near78_ref[...] * inverse],
    )
    for iterate, w_ref, new_ref, low_ref in (
        (iterate6, w6_ref, new6_ref, low6_ref),
        (iterate7[: 2 * rows7, :h2], w7_ref, new7_ref, low7_ref),
        (turned(sizes, iterate7[2 * rows7 :, LANE:]), w8_ref, new8_ref, low8_ref),
    ):
        master = w_ref[...]
        value = master - muon_rate * (iterate + decay_rate * master)
        new_ref[...] = value
        low_ref[...] = value.astype(BF16)


def paired_plan(
    features,
    labels,
    counts,
    weight6,
    weight7,
    weight8,
    moment6,
    moment7,
    moment8,
    resid6,
    resid7,
    resid8,
    noise6,
    noise7,
    noise8,
    biases,
    bias_first,
    bias_second,
):
    ins, h1 = resid6.shape
    h2, classes = resid8.shape
    rows6 = weight6.shape[0] // 2
    rows7 = weight7.shape[0] // 2
    rows8 = weight8.shape[0]
    sizes = (ins, h1, h2, classes, rows6, rows7, rows8)
    devices = 32
    half = (rows6 + rows7 * 2 // 3, h1)

    packed = pack_weights(weight6, weight7, weight8)
    staged = stage(
        packed,
        counts,
        features,
        labels,
        biases,
        bias_first,
        bias_second,
        resid6,
        resid7.T,
        resid8.T,
        noise6,
        noise7.T,
        noise8.T,
    )
    features, labels, *bias_rows = staged[:5]
    resid6, resid7, resid8, noise6, noise7, noise8, count_row = staged[5:]
    halves, _ = gather_halves(packed, [(VMEM, count_row)])

    tile = 2 * LANE
    lanes = h1 + 2 * LANE
    acc6, acc7, acc8, stats = call(
        functools.partial(worker_kernel, sizes, tile),
        "worker",
        [VMEM] * 13,
        [VMEM] * 4,
        [
            shape_of((ins, h1)),
            shape_of((h2, h1)),
            shape_of((classes, h2)),
            shape_of((devices, 1, lanes)),
        ],
        [
            pltpu.VMEM((ins, h1), BF16),
            pltpu.VMEM((h1, 2 * LANE), F32),
            pltpu.VMEM((h2, LANE), F32),
        ],
        megabytes=16,
    )(*halves, count_row, features, labels, bias_rows[0], resid6, resid7, resid8)

    all_stats = lax.all_to_all(stats, BOTH, 0, 0, tiled=True)

    def halves_of(count):
        return shape_of((count,) + half, BF16)

    sent7, head, code7, code8 = call(
        functools.partial(first_codes_kernel, sizes, (7,)),
        "codes_first",
        [VMEM] * 8,
        [VMEM] * 4,
        [
            halves_of(1),
            shape_of((1, LANE)),
            shape_of((h1, 2 * LANE)),
            shape_of((h2, 2 * LANE)),
        ],
    )(all_stats, stats, acc6, noise6, acc7, noise7, acc8, noise8)

    def codes(places, same_core, after=()):
        return call(
            functools.partial(codes_kernel, sizes, places, same_core),
            "codes",
            [VMEM] * (5 + len(after)),
            VMEM,
            halves_of(len(places)),
        )(head, acc6, noise6, code7, code8, *after)

    got7 = swap(sent7, grp_perm(1))
    out7 = add((0, 0), (codes((7,), True), got7), 1)
    near7 = swap(out7, wide_perm(0))
    rest = tuple(range(7))
    got = swap(codes(rest, False, (out7,)), grp_perm(1))
    kept = codes(rest, True, (out7,))
    near56 = swap(add((5, 5), (kept, got), 2), wide_perm(0))
    near4 = swap(add((4, 4), (kept, got), 1), wide_perm(0))
    far3 = add((3, 3, 0), (kept, got, near7), 1)
    near56 = passed(near56, (far3,), "passed_near")
    totals = call(
        totals_kernel,
        "totals",
        [VMEM] * 5,
        [HBM] * 3 + [RESULT] * 2,
        [shape_of(biases.shape)] * 3 + [shape_of((1, 1))] * 2,
        [pltpu.VMEM((1, biases.shape[0]), F32)] * 3 + [pltpu.SemaphoreType.DMA((3,))],
    )(far3, all_stats, *bias_rows)
    flat = totals[:3]
    far3 = swap(far3, wide_perm(1))
    far2 = add((2, 2, 1), (kept, got, near56), 1, name="add_far2")
    far2 = swap(far2, wide_perm(1))
    last = add((1, 1, 0, 0), (kept, got, near56, far3), 1, [(HBM, row) for row in flat])
    new_resid6 = new_resid6_part(0, ins // 2, last, head, acc6, noise6)
    last = swap(last, wide_perm(2))
    mine = add((0,) * 5, (kept, got, near4, far2, last), 1, [(HBM, new_resid6)])
    held = hold_moments(mine, moment6, moment7, moment8)
    theirs = swap(mine, grp_perm(2))

    moment, moment_low = call(
        functools.partial(moment_kernel, sizes),
        "moment",
        [VMEM] * 4,
        [VMEM] * 2,
        [shape_of((1,) + half), shape_of((1,) + half, BF16)],
    )(head, held, mine, theirs)
    new_resid6 = new_resid6_part(
        ins // 2, ins // 2, moment_low, head, acc6, noise6, new_resid6
    )
    new_resid7, new_resid8 = call(
        small_resids_kernel,
        "small_resids",
        [VMEM] * 6,
        [RESULT] * 2,
        [shape_of(acc7.shape), shape_of(acc8.shape)],
    )(moment_low, head, acc7, noise7, acc8, noise8)
    grams = [shape_of((h1, h1)), shape_of((2 * LANE, 2 * LANE))]

    def beside_last(trio, one3):
        four, again = relay(trio, one3, (moment,))
        early = call(
            functools.partial(early_kernel, sizes),
            "early_grams",
            [VMEM],
            [VMEM] * 2,
            grams,
            megabytes=8,
        )(four)
        momenta = call(
            functools.partial(momenta_kernel, sizes),
            "momenta",
            [VMEM] * 2,
            [HBM, HBM, RESULT, VMEM, VMEM],
            [
                shape_of(moment6.shape),
                shape_of(moment7.shape),
                shape_of(moment8.shape[::-1]),
                shape_of(moment6.shape),
                shape_of((2 * rows7 + rows8, 2 * LANE)),
            ],
            [pltpu.VMEM(moment7.shape, F32), pltpu.SemaphoreType.DMA((3,))],
        )(again, swap(again, grp_perm(1)))
        return four, [momenta[3], *early, *momenta]

    moments, done = gather_halves(
        moment_low, [(HBM, new_resid6), (HBM, new_resid8)], beside_last
    )
    early, (mom6, mom7, mom8, near6, near78) = done[1:3], done[3:]
    late = call(
        functools.partial(late_kernel, sizes),
        "late_grams",
        [VMEM] * 6,
        [VMEM] * 4,
        grams * 2,
        megabytes=8,
    )(*early, *moments[1:5])

    updated = call(
        functools.partial(update_kernel, sizes),
        "update",
        [VMEM] * 10,
        [RESULT] * 6,
        [
            shape_of(weight6.shape),
            shape_of(weight7.shape),
            shape_of(weight8.shape[::-1]),
            shape_of(weight6.shape, BF16),
            shape_of(weight7.shape, BF16),
            shape_of(weight8.shape[::-1], BF16),
        ],
        megabytes=16,
    )(*late, moments[5], near6, near78, weight6, weight7, weight8.T)
    new6, new7, new8, low6, low7, low8 = updated
    return (
        new6,
        new7,
        new8.T,
        low6,
        low7,
        low8.T,
        mom6,
        mom7,
        mom8.T,
        new_resid6,
        new_resid7.T,
        new_resid8.T,
        *flat,
        *[array.reshape(()) for array in totals[3:]],
    )


def on_device(*arrays):
    (ins, h1), (_, h2), (_, classes) = [array.shape for array in arrays[9:12]]
    rows6, rows7, rows8 = [array.shape[0] for array in arrays[3:6]]
    paired = (
        (lax.axis_size("grp"), lax.axis_size("wide")) == (4, 8)
        and h1 == 3 * LANE
        and LANE < h2 < 2 * LANE
        and h2 + classes <= 2 * LANE
        and rows6 % 32 == 0
        and rows7 == rows8 * 2
        and rows8 % 24 == 0
        and ins % (2 * LANE) == 0
        and 16 * rows7 // 2 == h1
    )
    return (paired_plan if paired else general_plan)(*arrays)


def solution(mesh):
    split_both = P(BOTH, None)
    split_wide = P("wide", None)
    return jax.shard_map(
        on_device,
        mesh=mesh,
        in_specs=(
            split_both,
            P(BOTH),
            P(BOTH),
            *[split_wide] * 6,
            *[split_both] * 6,
            P(),
            P(),
            P(),
        ),
        out_specs=(*[split_wide] * 9, *[split_both] * 3, P(), P(), P(), P(), P()),
        check_vma=False,
    )
```

```python
import functools

import jax
import jax.numpy as jnp
from jax import lax
from jax.experimental import pallas as pl
from jax.experimental.pallas import tpu as pltpu
from jax.sharding import PartitionSpec as P

NS_STEPS = 5
ADAM_STEP = 10


highest = lax.Precision.HIGHEST
smoothing = 0.1
clip_width = 2.5
noise_levels = 1024.0
ramp_slope = 2.0
momentum_decay = 0.95
muon_rate = 0.6
decay_rate = 0.01
coef_a = 3.4445
coef_b = -4.775
coef_c = 2.0315
beta_first = 0.9
beta_second = 0.999
bias_rate = 0.05
adam_eps = 1e-08

F32 = jnp.float32
BF16 = jnp.bfloat16
LANE = 128
BOTH = ("grp", "wide")


def dithered_code(clipped, peak, noise):
    ratio = jnp.abs(clipped) / peak
    dither = (noise.astype(jnp.float32) + 0.5) / noise_levels
    return jnp.sign(clipped) * jnp.clip(ramp_slope * (ratio - dither) + ratio, 0.0, 1.0)


def gram_of(iterate):
    return jnp.dot(iterate.T, iterate, precision=highest)


def schulz_step(iterate, gram_matrix):
    mixed = coef_b * gram_matrix + coef_c * jnp.dot(gram_matrix, gram_matrix, precision=highest)
    return coef_a * iterate + jnp.dot(iterate, mixed, precision=highest)


def layer_forward(inputs_b, weight_b, bias_part):
    return jnp.dot(inputs_b, weight_b, preferred_element_type=jnp.float32) + bias_part


def layer_backward(inputs_b, weight_b, grad_pre):
    grad_low = grad_pre.astype(jnp.bfloat16)
    weight_grad = jnp.einsum("ri,ro->io", inputs_b, grad_low, preferred_element_type=jnp.float32)
    bias_grad = jnp.sum(grad_low.astype(jnp.float32), axis=0)
    grad_inputs = jnp.einsum("ro,io->ri", grad_low, weight_b, preferred_element_type=jnp.float32)
    return (weight_grad, bias_grad, grad_inputs)


def adam_biases(biases, bias_first, bias_second, bias_grad):
    first_new = beta_first * bias_first + (1.0 - beta_first) * bias_grad
    second_new = beta_second * bias_second + (1.0 - beta_second) * bias_grad * bias_grad
    first_hat = first_new / (1.0 - beta_first**ADAM_STEP)
    second_hat = second_new / (1.0 - beta_second**ADAM_STEP)
    biases_new = biases - bias_rate * (
        first_hat / (jnp.sqrt(second_hat) + adam_eps) + decay_rate * biases
    )
    return biases_new, first_new, second_new


def general_plan(
    features,
    labels,
    counts,
    weight6,
    weight7,
    weight8,
    moment6,
    moment7,
    moment8,
    resid6,
    resid7,
    resid8,
    noise6,
    noise7,
    noise8,
    biases,
    bias_first,
    bias_second,
):
    masters = (weight6, weight7, weight8)
    weights_b = [
        lax.all_gather(weight.astype(jnp.bfloat16), "wide", axis=0, tiled=True)
        for weight in masters
    ]
    widths = [weights_b[0].shape[1], weights_b[1].shape[1], weights_b[2].shape[1]]
    bias_parts = [
        biases[: widths[0]],
        biases[widths[0] : widths[0] + widths[1]],
        biases[widths[0] + widths[1] :],
    ]
    row_mask = (jnp.arange(features.shape[0]) < counts[0]).astype(jnp.float32)
    inputs_list = [features]
    gelu_backs = []
    logits = None
    for which_layer in range(3):
        pre_act = layer_forward(
            inputs_list[which_layer], weights_b[which_layer], bias_parts[which_layer]
        )
        if which_layer < 2:
            activ, gelu_back = jax.vjp(jax.nn.gelu, pre_act)
            inputs_list.append(activ.astype(jnp.bfloat16))
            gelu_backs.append(gelu_back)
        else:
            logits = pre_act
    logp = jax.nn.log_softmax(logits, axis=-1)
    onehot = (labels[:, None] == jnp.arange(widths[2])[None, :]).astype(jnp.float32)
    target = (1.0 - smoothing) * onehot + smoothing / widths[2]
    worker_loss = jnp.sum(-jnp.sum(target * logp, axis=-1) * row_mask)
    upstream = -target * row_mask[:, None]
    grad_pre = upstream - jnp.exp(logp) * jnp.sum(upstream, axis=-1, keepdims=True)
    weight_grads = [None, None, None]
    bias_grads = [None, None, None]
    for which_layer in (2, 1, 0):
        weight_grads[which_layer], bias_grads[which_layer], grad_inputs = layer_backward(
            inputs_list[which_layer], weights_b[which_layer], grad_pre
        )
        if which_layer > 0:
            grad_pre = gelu_backs[which_layer - 1](grad_inputs)[0]
    resids = (resid6, resid7, resid8)
    noises = (noise6, noise7, noise8)
    accs = [weight_grads[k] + resids[k] for k in range(3)]
    clipped_list = []
    for acc in accs:
        bound = clip_width * jnp.sqrt(jnp.mean(acc * acc))
        clipped_list.append(jnp.clip(acc, -bound, bound))
    peak_list = lax.pmax(tuple(jnp.max(jnp.abs(clipped)) for clipped in clipped_list), BOTH)
    peak_list = [p + 1e-06 for p in peak_list]
    code_list = [dithered_code(clipped_list[k], peak_list[k], noises[k]) for k in range(3)]
    new_resids = [accs[k] - peak_list[k] * code_list[k] for k in range(3)]
    loss_total, image_total, bias_total = lax.psum(
        (worker_loss, jnp.sum(row_mask), jnp.concatenate(bias_grads)), BOTH
    )
    code_rows = [
        lax.psum_scatter(code, "wide", scatter_dimension=0, tiled=True) for code in code_list
    ]
    code_sums = lax.psum(tuple(code_rows), "grp")
    moments = (moment6, moment7, moment8)
    new_moments = [
        momentum_decay * moments[k] + peak_list[k] * code_sums[k] / image_total for k in range(3)
    ]
    full_moments = [
        lax.all_gather(moment, "wide", axis=0, tiled=True) for moment in new_moments
    ]
    row_block = lax.axis_index("wide")
    iterates = []
    for k in range(3):
        whole = full_moments[k]
        iterate = whole / (jnp.sqrt(jnp.sum(whole * whole)) + 1e-07)
        for step_num in range(NS_STEPS):
            iterate = schulz_step(iterate, gram_of(iterate))
        row_count = new_moments[k].shape[0]
        iterates.append(lax.dynamic_slice_in_dim(iterate, row_block * row_count, row_count, 0))
    new_weights = [
        masters[k] - muon_rate * (iterates[k] + decay_rate * masters[k]) for k in range(3)
    ]
    new_biases = adam_biases(biases, bias_first, bias_second, bias_total / image_total)
    return (
        *new_weights,
        *[weight.astype(jnp.bfloat16) for weight in new_weights],
        *new_moments,
        *new_resids,
        *new_biases,
        loss_total,
        image_total,
    )


ORDERS = ((2, 1, 4), (1, 2, 4))


def half_of(grp, wide):
    return (grp + wide + (wide >> 1)) & 1


def wide_perm(phase):
    pairs = []
    for g in range(4):
        for w in range(8):
            bit = ORDERS[half_of(g, w)][phase]
            pairs.append((g * 8 + w, (g ^ (bit < 4)) * 8 + (w ^ bit)))
    return pairs


def grp_perm(bit):
    return [(g * 8 + w, (g ^ bit) * 8 + w) for g in range(4) for w in range(8)]


def swap(array, perm):
    return lax.ppermute(array, BOTH, perm)


def own_half():
    return half_of(lax.axis_index("grp"), lax.axis_index("wide"))


def half_at(place, same_core):
    core = own_half() if same_core else 1 - own_half()
    masks = [
        sum(order[phase] for phase in range(3) if place & (4 >> phase)) for order in ORDERS
    ]
    return 2 * (lax.axis_index("wide") ^ jnp.where(core == 0, masks[0], masks[1])) + core


def dims(contract_left, contract_right):
    return (((contract_left,), (contract_right,)), ((), ()))


def mxu(left, right, contract_left=1, contract_right=0):
    return lax.dot_general(
        left, right, dims(contract_left, contract_right), preferred_element_type=F32
    )


def split(value):
    high = value.astype(BF16)
    return high, (value - high.astype(F32)).astype(BF16)


def left_parts(value):
    high, rest = split(value)
    return jnp.concatenate([high, high, rest], axis=1)


def right_parts(value):
    high, rest = split(value)
    return jnp.concatenate([high, rest, high], axis=0)


def shifted_eye(rows, cols, shift, dtype):
    at = lax.broadcasted_iota(jnp.int32, (rows, cols), 0) + shift
    return (at == lax.broadcasted_iota(jnp.int32, (rows, cols), 1)).astype(dtype)


def upright(flat, shift, dtype=BF16):
    return mxu(flat.astype(BF16), shifted_eye(flat.shape[0], 2 * LANE, shift, BF16), 0, 0)


def fold(region):
    n = region.shape[0] // 3
    third = jnp.concatenate([region[2 * n :, :LANE], region[2 * n :, LANE:]], axis=0)
    return jnp.concatenate([region[: 2 * n], third], axis=1)


def unfold(folded):
    n = folded.shape[0] // 2
    last = jnp.concatenate([folded[:n, 2 * LANE :], folded[n:, 2 * LANE :]], axis=1)
    return jnp.concatenate([folded[:, : 2 * LANE], last], axis=0)


HBM = pl.BlockSpec(memory_space=pltpu.HBM)
SMEM = pl.BlockSpec(memory_space=pltpu.SMEM)
VMEM = pl.BlockSpec(memory_space=pltpu.VMEM)
RESULT = pl.BlockSpec(memory_space=pltpu.VMEM)


def shape_of(shape, dtype=F32):
    return jax.ShapeDtypeStruct(shape, dtype)


MICROS = {"passed": 5.0, "passed_last": 20.0, "passed_one": 20.0, "add_far3": 20.0}


def placed(shape, spec):
    if spec is HBM:
        return pltpu.HBM(shape.shape, shape.dtype)
    return pltpu.VMEM(shape.shape, shape.dtype) if spec is VMEM else shape


def call(kernel, name, in_specs, out_specs, out_shape, scratch=(), megabytes=4, aliases=None):
    many = isinstance(out_shape, list)
    shapes = [
        placed(shape, spec)
        for shape, spec in zip(
            out_shape if many else [out_shape], out_specs if many else [out_specs]
        )
    ]
    kernel_call = pl.pallas_call(
        kernel,
        in_specs=in_specs,
        out_specs=out_specs,
        out_shape=shapes if many else shapes[0],
        scratch_shapes=list(scratch),
        compiler_params=pltpu.CompilerParams(vmem_limit_bytes=megabytes * 1024 * 1024),
        cost_estimate=pl.CostEstimate(
            flops=int(MICROS.get(name, 0.0) * 1.15e9), bytes_accessed=0, transcendentals=0
        ),
        input_output_aliases=aliases or {},
        name=name,
    )

    def run(*arrays):
        return kernel_call(
            *[
                pltpu.with_memory_space_constraint(array, pltpu.HBM) if spec is HBM else array
                for array, spec in zip(arrays, in_specs)
            ]
        )

    return run


def pack_kernel(w6_ref, w7_ref, w8_ref, out_ref, half6, half7, all8, sems):
    core = own_half()
    rows6, rows7 = half6.shape[0], half7.shape[0]
    copies = [
        pltpu.make_async_copy(
            w6_ref.at[pl.ds(pl.multiple_of(core * rows6, 8), rows6)], half6, sems.at[0]
        ),
        pltpu.make_async_copy(
            w7_ref.at[pl.ds(pl.multiple_of(core * rows7, 8), rows7)], half7, sems.at[1]
        ),
        pltpu.make_async_copy(w8_ref, all8, sems.at[2]),
    ]
    for copy in copies:
        copy.start()
    for copy in copies:
        copy.wait()
    out_ref[0, :rows6, :] = half6[...].astype(BF16)
    h2 = half7.shape[1]
    lead = (core == 0).astype(F32)
    region = upright(all8[...], h2) * lead + jnp.concatenate(
        [half7[...], jnp.zeros((rows7, 2 * LANE - h2), F32)], axis=1
    )
    out_ref[0, rows6:, :] = fold(region).astype(BF16)


def pack_weights(weight6, weight7, weight8):
    rows6, h1 = weight6.shape[0] // 2, weight6.shape[1]
    rows7, h2 = weight7.shape[0] // 2, weight7.shape[1]
    return call(
        pack_kernel,
        "pack_weights",
        [HBM] * 3,
        VMEM,
        shape_of((1, rows6 + rows7 * 2 // 3, h1), BF16),
        [
            pltpu.VMEM((rows6, h1), F32),
            pltpu.VMEM((rows7, h2), F32),
            pltpu.VMEM(weight8.shape[::-1], F32),
            pltpu.SemaphoreType.DMA((3,)),
        ],
    )(weight6, weight7, weight8.T)


def stage_kernel(count, after_ref, images_ref, *refs):
    ins, outs, token_ref, sems = refs[:count], refs[count:-2], refs[-2], refs[-1]
    copies = [
        pltpu.make_async_copy(
            source, target if len(source.shape) == len(target.shape) else target.at[0], sems.at[k]
        )
        for k, (source, target) in enumerate(zip(ins, outs))
    ]
    for copy in copies:
        copy.start()
    token_ref[...] = jnp.full(token_ref.shape, images_ref[0], jnp.int32)
    for copy in copies:
        copy.wait()


def stage(after, counts, *arrays):
    count = len(arrays)
    shapes = [(1,) * (2 - array.ndim) + array.shape for array in arrays]
    return call(
        functools.partial(stage_kernel, count),
        "stage",
        [VMEM, SMEM] + [HBM] * count,
        [VMEM] * (count + 1),
        [shape_of(shape, array.dtype) for shape, array in zip(shapes, arrays)]
        + [shape_of((1, LANE), jnp.int32)],
        [pltpu.SemaphoreType.DMA((count,))],
    )(after, counts, *arrays)


def add_kernel(picks, size, *refs):
    for k in range(size):
        total = None
        for ref, pick in zip(refs, picks):
            part = ref[pick + k].astype(F32)
            total = part if total is None else total + part
        refs[-1][k] = total.astype(BF16)


def add(picks, arrays, size, after=(), name="add"):
    shape = shape_of((size,) + arrays[0].shape[1:], BF16)
    specs = [VMEM] * len(arrays) + [spec for spec, _ in after]
    return call(functools.partial(add_kernel, picks, size), name, specs, VMEM, shape)(
        *arrays, *[array for _, array in after]
    )


def pass_kernel(in_ref, *refs):
    refs[-1][...] = in_ref[...]


def passed(array, after, name="passed"):
    specs = [VMEM] * (1 + len(after))
    shape = shape_of(array.shape, array.dtype)
    return call(pass_kernel, name, specs, VMEM, shape)(array, *after)


def first_join_kernel(own_ref, far_ref, mid_ref, *refs):
    trio_ref, again_ref = refs[-2:]
    for k, ref in enumerate((own_ref, far_ref, mid_ref)):
        trio_ref[k] = ref[0]
    again_ref[...] = far_ref[...]


def relay_kernel(trio_ref, one_ref, *refs):
    outs = refs[len(refs) // 2 :]
    count = trio_ref.shape[0]
    outs[0][:count] = trio_ref[...]
    outs[0][count:] = one_ref[...]
    if len(refs) > 1:
        outs[1][...] = refs[0][...]


def relay(trio, one, beside=()):
    joined = shape_of((trio.shape[0] + one.shape[0],) + one.shape[1:], one.dtype)
    shapes = [joined] + [shape_of(array.shape, array.dtype) for array in beside]
    ins = [trio, one, *beside]
    return call(relay_kernel, "relay", [VMEM] * len(ins), [VMEM] * len(shapes), shapes)(*ins)


def gather_halves(own, after=(), work=None):
    far = swap(own, wide_perm(2))
    mid = swap(own, wide_perm(1))
    trio, far = call(
        first_join_kernel,
        "first_join",
        [VMEM] * 3 + [spec for spec, _ in after],
        [VMEM] * 2,
        [shape_of((3,) + own.shape[1:], BF16), shape_of(own.shape, BF16)],
    )(own, far, mid, *[array for _, array in after])
    trio4 = swap(trio, wide_perm(0))
    one3 = swap(far, wide_perm(1))
    one3 = passed(one3, (), "passed_one")
    one7 = swap(one3, wide_perm(0))
    four, begun = (relay(trio, one3)[0], None) if work is None else work(trio, one3)
    trio4 = passed(trio4, (four,))
    other_four = swap(four, grp_perm(1))
    done = (four,) if work is None else begun(trio4, other_four)
    one7 = passed(one7, done[:3], "passed_last")
    others = (other_four, swap(trio4, grp_perm(1)), swap(one7, grp_perm(1)))
    return (four, trio4, one7, *others), done


def gelu_pair(pre):
    slope = 0.7978845608028654
    inner = slope * (pre + 0.044715 * pre * pre * pre)
    t = jnp.tanh(inner)
    value = 0.5 * pre * (1.0 + t)
    back = 0.5 * (1.0 + t) + 0.5 * pre * (1.0 - t * t) * slope * (1.0 + 3 * 0.044715 * pre * pre)
    return value, back


def place_all(sizes, refs, all6, all7, all8):
    ins, h1, h2, classes, rows6, rows7, rows8 = sizes
    for at in range(16):
        place = at % 8
        ref, q = refs[3 * (at // 8) + (0, 0, 0, 0, 1, 1, 1, 2)[place]], place % 4 % (4 - place // 4)
        half = half_at(place, at < 8)
        all6[pl.ds(pl.multiple_of(half * rows6, 16), rows6), :] = ref[q, :rows6, :]
        region = unfold(ref[q, rows6:, :].astype(F32))
        all7[pl.ds(pl.multiple_of(half * rows7, 8), rows7), :] = region

        @pl.when(half % 2 == 0)
        def _():
            row = pl.multiple_of((half // 2) * rows8, 8)
            all8[pl.ds(row, rows8), :] = region[:rows8, LANE:]


def worker_kernel(sizes, tile, *refs):
    ins, h1, h2, classes, rows6, rows7, rows8 = sizes
    halves, refs = refs[:6], refs[6:]
    count_ref, feat_ref, label_ref, bias_ref, resid6_ref, resid7_ref, resid8_ref = refs[:7]
    acc6_ref, acc7_ref, acc8_ref, stats_ref, w6, w7, w8 = refs[7:]
    first = h2 - LANE

    place_all(sizes, halves, w6, w7, w8)
    w7_low = w7[:, :h2].astype(BF16)
    w8_low = w8[...].astype(BF16)

    rows = feat_ref.shape[0]
    row_mask = (lax.broadcasted_iota(jnp.int32, (rows, 1), 0) < count_ref[:, :1]).astype(F32)
    lanes = lax.broadcasted_iota(jnp.int32, (rows, LANE), 1) - first
    valid = (lanes >= 0) & (lanes < classes)
    labels = jnp.sum(
        jnp.where(shifted_eye(rows, rows, 0, jnp.bool_), label_ref[...], 0), axis=1, keepdims=True
    )
    bias8 = jnp.concatenate(
        [bias_ref[:, h1 + LANE :], jnp.zeros((1, LANE - first - classes), F32)], axis=1
    )

    pre6 = mxu(feat_ref[...], w6[...]) + bias_ref[:, :h1]
    act6, back6 = gelu_pair(pre6)
    act6 = act6.astype(BF16)
    pre7 = mxu(act6, w7_low) + bias_ref[:, h1 : h1 + h2]
    act7, back7 = gelu_pair(pre7)
    act7 = act7.astype(BF16)
    logits = jnp.where(valid, mxu(act7, w8_low) + bias8, -1e30)
    shifted = logits - jnp.max(logits, axis=1, keepdims=True)
    logp = shifted - jnp.log(jnp.sum(jnp.exp(shifted), axis=1, keepdims=True))
    onehot = (labels == lanes).astype(F32)
    target = jnp.where(valid, (1.0 - smoothing) * onehot + smoothing / classes, 0.0)
    loss = jnp.sum(-jnp.sum(target * jnp.where(valid, logp, 0.0), axis=1, keepdims=True) * row_mask)
    weight = jnp.sum(target, axis=1, keepdims=True)
    dlogits = (row_mask * (jnp.exp(logp) * weight - target)).astype(BF16)
    dpre7 = (mxu(dlogits, w8_low, 1, 1) * back7).astype(BF16)
    dpre6 = (mxu(dpre7, w7_low, 1, 1) * back6).astype(BF16)

    square6 = jnp.zeros((8, h1), F32)
    most6 = jnp.zeros((8, h1), F32)
    for t in range(ins // tile):
        part = slice(t * tile, (t + 1) * tile)
        acc = resid6_ref[part, :] + mxu(feat_ref[:, part], dpre6, 0, 0)
        acc6_ref[part, :] = acc
        square6 = square6 + jnp.sum((acc * acc).reshape(tile // 8, 8, h1), axis=0)
        most6 = jnp.maximum(most6, jnp.max(jnp.abs(acc).reshape(tile // 8, 8, h1), axis=0))
    acc7 = mxu(dpre7, act6, 0, 0) + resid7_ref[...]
    acc7_ref[...] = acc7
    acc8 = mxu(dlogits, act7, 0, 0)[first : first + classes, :] + resid8_ref[...]
    acc8_ref[...] = acc8

    bound6 = clip_width * jnp.sqrt(jnp.sum(square6) * (1.0 / (ins * h1)))
    bound7 = clip_width * jnp.sqrt(jnp.sum(acc7 * acc7) * (1.0 / (h1 * h2)))
    bound8 = clip_width * jnp.sqrt(jnp.sum(acc8 * acc8) * (1.0 / (h2 * classes)))
    peak6 = jnp.minimum(jnp.max(most6), bound6)
    peak7 = jnp.minimum(jnp.max(jnp.abs(acc7)), bound7)
    peak8 = jnp.minimum(jnp.max(jnp.abs(acc8)), bound8)
    lane = lax.broadcasted_iota(jnp.int32, (1, LANE), 1) - (first + classes)
    tail = jnp.zeros((1, LANE), F32)
    count = count_ref[:, :1].astype(F32)
    for k, value in enumerate((peak6, peak7, peak8, loss, count, bound6, bound7, bound8)):
        tail = jnp.where(lane == k, value, tail)
    db6 = jnp.sum(dpre6.astype(F32), axis=0, keepdims=True)
    db7 = jnp.sum(dpre7.astype(F32), axis=0, keepdims=True)
    db8 = jnp.sum(dlogits.astype(F32), axis=0, keepdims=True)
    db7 = jnp.concatenate([db7, jnp.zeros((1, 2 * LANE - h2), F32)], axis=1)
    row = jnp.concatenate([db6, db7[:, :LANE], db7[:, LANE:] + db8 + tail], axis=1)
    stats_ref[...] = jnp.broadcast_to(row[None], stats_ref.shape)


def code_of(acc, bound, scale, noise):
    ramp = jnp.minimum(jnp.abs(acc), bound) * scale - (
        noise.astype(F32) * (ramp_slope / noise_levels) + 0.5 * ramp_slope / noise_levels
    )
    ramp = jnp.clip(ramp, 0.0, 1.0)
    return jnp.where(acc < 0, -ramp, ramp)


def lane_of(row_ref, k):
    return row_ref[0:1, k : k + 1]


def write_codes(sizes, places, same_core, head, acc6_ref, noise6_ref, code7, code8, out):
    ins, h1, h2, classes, rows6, rows7, rows8 = sizes
    peak, bound = lane_of(head, 0), lane_of(head, 3)
    scale = (1.0 + ramp_slope) / peak
    for at, place in enumerate(places):
        half = half_at(place, same_core)
        part = pl.ds(pl.multiple_of(half * rows6, 8), rows6)
        code = code_of(acc6_ref[part, :], bound, scale, noise6_ref[part, :])
        out[at, :rows6, :] = code.astype(BF16)
        region = code7[pl.ds(pl.multiple_of(half * rows7, 8), rows7), :]
        lead = (half % 2 == 0).astype(F32)
        region = region + lead * code8[pl.ds(pl.multiple_of((half // 2) * rows8, 8), rows8), :]
        out[at, rows6:, :] = fold(region).astype(BF16)


def first_codes_kernel(sizes, places, stats_ref, mine_ref, acc6_ref, noise6_ref, *refs):
    ins, h1, h2, classes, rows6, rows7, rows8 = sizes
    acc7_ref, noise7_ref, acc8_ref, noise8_ref, out_ref, head_ref, code7, code8 = refs
    at = h1 + h2 + classes
    most = jnp.max(stats_ref[:, :, at : at + 3], axis=0) + 1e-06
    images = jnp.sum(stats_ref[:, :, at + 4 : at + 5], axis=0)
    lane = lax.broadcasted_iota(jnp.int32, (1, LANE), 1)
    head = jnp.zeros((1, LANE), F32)
    for k in range(3):
        head = jnp.where(lane == k, most[:, k : k + 1], head)
        head = jnp.where(lane == 3 + k, mine_ref[0, :, at + 5 + k : at + 6 + k], head)
        head = jnp.where(lane == 6 + k, most[:, k : k + 1] / images, head)
    head_ref[...] = head
    ramp = 1.0 + ramp_slope
    small7 = code_of(acc7_ref[...], lane_of(head, 4), ramp / lane_of(head, 1), noise7_ref[...])
    small8 = code_of(acc8_ref[...], lane_of(head, 5), ramp / lane_of(head, 2), noise8_ref[...])
    code7[...] = upright(small7, 0)
    code8[...] = upright(small8, h2)
    write_codes(sizes, places, False, head, acc6_ref, noise6_ref, code7, code8, out_ref)


def codes_kernel(sizes, places, same_core, head_ref, acc6, noise6, code7, code8, *refs):
    write_codes(sizes, places, same_core, head_ref, acc6, noise6, code7, code8, refs[-1])


def resid_of(head, layer, acc, noise):
    peak = lane_of(head, layer)
    return acc - peak * code_of(acc, lane_of(head, 3 + layer), (1.0 + ramp_slope) / peak, noise)


def resid_kernel(tile, start, after_ref, head_ref, acc6_ref, noise6_ref, *refs):
    out_ref, hold, sems = refs[-3:]
    head = head_ref[...]
    copies = []
    for t in range(hold.shape[0] // tile):
        here, there = pl.ds(t * tile, tile), pl.ds(start + t * tile, tile)
        hold[here, :] = resid_of(head, 0, acc6_ref[there, :], noise6_ref[there, :])
        copies.append(pltpu.make_async_copy(hold.at[here], out_ref.at[there], sems.at[t]))
        copies[-1].start()
    for copy in copies:
        copy.wait()


def new_resid6_part(start, rows, after, head, acc6, noise6, before=None):
    tile = 3 * LANE
    ins = [after, head, acc6, noise6] + ([] if before is None else [before])
    return call(
        functools.partial(resid_kernel, tile, start),
        "new_resid",
        [VMEM] * 4 + [HBM] * (len(ins) - 4),
        HBM,
        shape_of(acc6.shape),
        [pltpu.VMEM((rows, acc6.shape[1]), F32), pltpu.SemaphoreType.DMA((rows // tile,))],
        megabytes=8,
        aliases={} if before is None else {4: 0},
    )(*ins)


def small_resids_kernel(after_ref, head_ref, acc7_ref, noise7_ref, acc8_ref, noise8_ref, *outs):
    head = head_ref[...]
    outs[0][...] = resid_of(head, 1, acc7_ref[...], noise7_ref[...])
    outs[1][...] = resid_of(head, 2, acc8_ref[...], noise8_ref[...])


def totals_kernel(after_ref, stats_ref, bias_ref, first_ref, second_ref, *refs):
    outs, loss_ref, images_ref, rows, sems = refs[:3], refs[3], refs[4], refs[5:8], refs[8]
    width = bias_ref.shape[1]
    total = jnp.sum(stats_ref[...], axis=0)
    images = total[:, width + 4 : width + 5]
    loss_ref[...] = total[:, width + 3 : width + 4]
    images_ref[...] = images
    rows[0][...], rows[1][...], rows[2][...] = adam_biases(
        bias_ref[...], first_ref[...], second_ref[...], total[:, :width] / images
    )
    copies = [
        pltpu.make_async_copy(row.at[0], out, sems.at[k])
        for k, (row, out) in enumerate(zip(rows, outs))
    ]
    for copy in copies:
        copy.start()
    for copy in copies:
        copy.wait()


def hold_kernel(after_ref, m6_ref, m7_ref, m8_ref, out_ref, half7, all8, sems):
    core = own_half()
    rows7, h2 = half7.shape
    rows6 = out_ref.shape[1] - rows7 * 2 // 3
    copies = [
        pltpu.make_async_copy(
            m6_ref.at[pl.ds(pl.multiple_of(core * rows6, 8), rows6)],
            out_ref.at[0, pl.ds(0, rows6)],
            sems.at[0],
        ),
        pltpu.make_async_copy(
            m7_ref.at[pl.ds(pl.multiple_of(core * rows7, 8), rows7)], half7, sems.at[1]
        ),
        pltpu.make_async_copy(m8_ref, all8, sems.at[2]),
    ]
    for copy in copies:
        copy.start()
    for copy in copies:
        copy.wait()
    lead = (core == 0).astype(F32)
    tall = jnp.zeros((rows7, 2 * LANE), F32)
    parts = all8[...]
    for _ in range(3):
        high = parts.astype(BF16)
        tall = tall + upright(high, h2)
        parts = parts - high.astype(F32)
    region = tall * lead + jnp.concatenate(
        [half7[...], jnp.zeros((rows7, 2 * LANE - h2), F32)], axis=1
    )
    out_ref[0, rows6:, :] = fold(region)


def hold_moments(after, moment6, moment7, moment8):
    rows6, h1 = moment6.shape[0] // 2, moment6.shape[1]
    rows7, h2 = moment7.shape[0] // 2, moment7.shape[1]
    return call(
        hold_kernel,
        "hold_moments",
        [VMEM] + [HBM] * 3,
        VMEM,
        shape_of((1, rows6 + rows7 * 2 // 3, h1)),
        [
            pltpu.VMEM((rows7, h2), F32),
            pltpu.VMEM(moment8.shape[::-1], F32),
            pltpu.SemaphoreType.DMA((3,)),
        ],
    )(after, moment6, moment7, moment8.T)


def moment_kernel(sizes, head_ref, held_ref, mine_ref, theirs_ref, out_ref, low_ref):
    ins, h1, h2, classes, rows6, rows7, rows8 = sizes
    codes = mine_ref[0].astype(F32) + theirs_ref[0].astype(F32)
    moment6 = momentum_decay * held_ref[0, :rows6] + lane_of(head_ref, 6) * codes[:rows6]
    column = lax.broadcasted_iota(jnp.int32, (rows7, 2 * LANE), 1)
    rate = fold(jnp.where(column < h2, lane_of(head_ref, 7), lane_of(head_ref, 8)))
    region = momentum_decay * held_ref[0, rows6:] + rate * codes[rows6:]
    out_ref[0, :rows6] = moment6
    out_ref[0, rows6:] = region
    low_ref[0, :rows6] = moment6.astype(BF16)
    low_ref[0, rows6:] = region.astype(BF16)


def schulz_chains(grams, iterates, inverses):
    diagonals = [shifted_eye(gram.shape[0], gram.shape[0], 0, F32) for gram in grams]
    for number in range(NS_STEPS):
        lefts = [left_parts(gram) for gram in grams]
        squares = [mxu(left, right_parts(gram)) for left, gram in zip(lefts, grams)]
        if number == 0:
            scales = [inverse * inverse for inverse in inverses]
            squares = [square * (scale * scale) for square, scale in zip(squares, scales)]
            grams = [gram * scale for gram, scale in zip(grams, scales)]
        mixed = [
            right_parts(coef_a * diagonal + coef_b * gram + coef_c * square)
            for diagonal, gram, square in zip(diagonals, grams, squares)
        ]
        rows = [left_parts(iterate) for iterate in iterates]
        if number == NS_STEPS - 1:
            return [mxu(row, right) for row, right in zip(rows, mixed)]
        both = [
            mxu(jnp.concatenate([left, row], axis=0), right)
            for left, row, right in zip(lefts, rows, mixed)
        ]
        iterates = [value[gram.shape[0] :] for value, gram in zip(both, grams)]
        products = [value[: gram.shape[0]] for value, gram in zip(both, grams)]
        if number == 0:
            iterates = [iterate * inverse for iterate, inverse in zip(iterates, inverses)]
            products = [product * scale for product, scale in zip(products, scales)]
        grams = [mxu(left_parts(product), right) for product, right in zip(products, mixed)]


def grams_of(sizes, ref):
    rows6 = sizes[4]
    places = range(ref.shape[0])
    block = jnp.concatenate([ref[k, :rows6, :] for k in places], axis=0)
    region = [unfold(ref[k, rows6:, :].astype(F32)) for k in places]
    region = jnp.concatenate(region, axis=0).astype(BF16)
    return mxu(block, block, 0, 0), mxu(region, region, 0, 0)


def early_kernel(sizes, four_ref, out6_ref, out78_ref):
    out6_ref[...], out78_ref[...] = grams_of(sizes, four_ref)


def middle_kernel(sizes, own6_ref, own78_ref, trio_ref, theirs_ref, *outs):
    trio6, trio78 = grams_of(sizes, trio_ref)
    outs[0][...] = own6_ref[...] + trio6
    outs[1][...] = own78_ref[...] + trio78
    outs[2][...], outs[3][...] = grams_of(sizes, theirs_ref)


def late_kernel(sizes, own6_ref, own78_ref, other6_ref, other78_ref, one_ref, trio_ref, *outs):
    one6, one78 = grams_of(sizes, one_ref)
    outs[0][...] = own6_ref[...] + one6
    outs[1][...] = own78_ref[...] + one78
    trio6, trio78 = grams_of(sizes, trio_ref)
    outs[2][...] = other6_ref[...] + trio6
    outs[3][...] = other78_ref[...] + trio78


def momenta_kernel(sizes, mine_ref, theirs_ref, *refs):
    ins, h1, h2, classes, rows6, rows7, rows8 = sizes
    out6_ref, out7_ref, out8_ref, near6_ref, near78_ref, stage7, sems = refs
    core = own_half()
    copies = []
    region8 = None
    for k, (at, ref) in enumerate(((core, mine_ref), (1 - core, theirs_ref))):
        part = pl.ds(pl.multiple_of(at * rows6, 8), rows6)
        near6_ref[part, :] = ref[0, :rows6, :]
        copies.append(
            pltpu.make_async_copy(ref.at[0, pl.ds(0, rows6)], out6_ref.at[part], sems.at[k])
        )
        copies[-1].start()
        region = unfold(ref[0, rows6:, :])
        near78_ref[pl.ds(pl.multiple_of(at * rows7, 8), rows7), :] = region
        region8 = region if region8 is None else jnp.where(core == 0, region8, region)
    column = lax.broadcasted_iota(jnp.int32, (2 * rows7, 2 * LANE), 1)
    near78_ref[: 2 * rows7, :] = jnp.where(column < h2, near78_ref[: 2 * rows7, :], 0.0)
    near78_ref[2 * rows7 :, :] = jnp.where(column[:rows8] < h2, 0.0, region8[:rows8])
    stage7[...] = near78_ref[: 2 * rows7, :h2]
    copies.append(pltpu.make_async_copy(stage7, out7_ref, sems.at[2]))
    copies[-1].start()
    out8_ref[...] = turned(sizes, near78_ref[2 * rows7 :, LANE:])
    for copy in copies:
        copy.wait()


def turned(sizes, rows):
    ins, h1, h2, classes, rows6, rows7, rows8 = sizes
    square = jnp.concatenate([rows, jnp.zeros((LANE - rows8, LANE), F32)], axis=0)
    return square.T[h2 - LANE : h2 - LANE + classes, :rows8]


def update_kernel(sizes, own6, own78, other6, other78, one7_ref, *refs):
    ins, h1, h2, classes, rows6, rows7, rows8 = sizes
    near6_ref, near78_ref, w6_ref, w7_ref, w8_ref, *outs = refs
    new6_ref, new7_ref, new8_ref, low6_ref, low7_ref, low8_ref = outs
    last6, last78 = grams_of(sizes, one7_ref)
    gram6 = own6[...] + (other6[...] + last6)
    gram7 = own78[...] + (other78[...] + last78)

    size = 2 * LANE
    is7_row = lax.broadcasted_iota(jnp.int32, (size, size), 0) < h2
    is7_col = lax.broadcasted_iota(jnp.int32, (size, size), 1) < h2
    diagonal = shifted_eye(size, size, 0, F32)
    inverse6 = 1.0 / (jnp.sqrt(jnp.sum(gram6 * shifted_eye(h1, h1, 0, F32))) + 1e-07)
    trace7 = jnp.sum(jnp.where(is7_col, gram7 * diagonal, 0.0))
    trace8 = jnp.sum(jnp.where(is7_col, 0.0, gram7 * diagonal))
    inverse7 = 1.0 / (jnp.sqrt(trace7) + 1e-07)
    inverse8 = 1.0 / (jnp.sqrt(trace8) + 1e-07)
    inverse = jnp.where(is7_col[:1], inverse7, inverse8)
    gram7 = jnp.where(is7_row == is7_col, gram7, 0.0)
    iterate6, iterate7 = schulz_chains(
        [gram6, gram7], [near6_ref[...], near78_ref[...]], [inverse6, inverse]
    )
    for iterate, w_ref, new_ref, low_ref in (
        (iterate6, w6_ref, new6_ref, low6_ref),
        (iterate7[: 2 * rows7, :h2], w7_ref, new7_ref, low7_ref),
        (turned(sizes, iterate7[2 * rows7 :, LANE:]), w8_ref, new8_ref, low8_ref),
    ):
        master = w_ref[...]
        value = master - muon_rate * (iterate + decay_rate * master)
        new_ref[...] = value
        low_ref[...] = value.astype(BF16)


def paired_plan(
    features,
    labels,
    counts,
    weight6,
    weight7,
    weight8,
    moment6,
    moment7,
    moment8,
    resid6,
    resid7,
    resid8,
    noise6,
    noise7,
    noise8,
    biases,
    bias_first,
    bias_second,
):
    ins, h1 = resid6.shape
    h2, classes = resid8.shape
    rows6 = weight6.shape[0] // 2
    rows7 = weight7.shape[0] // 2
    rows8 = weight8.shape[0]
    sizes = (ins, h1, h2, classes, rows6, rows7, rows8)
    devices = 32
    half = (rows6 + rows7 * 2 // 3, h1)

    packed = pack_weights(weight6, weight7, weight8)
    staged = stage(
        packed,
        counts,
        features,
        labels,
        biases,
        bias_first,
        bias_second,
        resid6,
        resid7.T,
        resid8.T,
        noise6,
        noise7.T,
        noise8.T,
    )
    features, labels, *bias_rows = staged[:5]
    resid6, resid7, resid8, noise6, noise7, noise8, count_row = staged[5:]
    halves, _ = gather_halves(packed, [(VMEM, count_row)])

    tile = 2 * LANE
    lanes = h1 + 2 * LANE
    acc6, acc7, acc8, stats = call(
        functools.partial(worker_kernel, sizes, tile),
        "worker",
        [VMEM] * 13,
        [VMEM] * 4,
        [
            shape_of((ins, h1)),
            shape_of((h2, h1)),
            shape_of((classes, h2)),
            shape_of((devices, 1, lanes)),
        ],
        [
            pltpu.VMEM((ins, h1), BF16),
            pltpu.VMEM((h1, 2 * LANE), F32),
            pltpu.VMEM((h2, LANE), F32),
        ],
        megabytes=16,
    )(*halves, count_row, features, labels, bias_rows[0], resid6, resid7, resid8)

    all_stats = lax.all_to_all(stats, BOTH, 0, 0, tiled=True)

    def halves_of(count):
        return shape_of((count,) + half, BF16)

    sent7, head, code7, code8 = call(
        functools.partial(first_codes_kernel, sizes, (7,)),
        "codes_first",
        [VMEM] * 8,
        [VMEM] * 4,
        [
            halves_of(1),
            shape_of((1, LANE)),
            shape_of((h1, 2 * LANE)),
            shape_of((h2, 2 * LANE)),
        ],
    )(all_stats, stats, acc6, noise6, acc7, noise7, acc8, noise8)

    def codes(places, same_core, after=()):
        return call(
            functools.partial(codes_kernel, sizes, places, same_core),
            "codes",
            [VMEM] * (5 + len(after)),
            VMEM,
            halves_of(len(places)),
        )(head, acc6, noise6, code7, code8, *after)

    got7 = swap(sent7, grp_perm(1))
    out7 = add((0, 0), (codes((7,), True), got7), 1)
    near7 = swap(out7, wide_perm(0))
    rest = tuple(range(7))
    got = swap(codes(rest, False, (out7,)), grp_perm(1))
    kept = codes(rest, True, (out7,))
    near56 = swap(add((5, 5), (kept, got), 2), wide_perm(0))
    near4 = swap(add((4, 4), (kept, got), 1), wide_perm(0))
    far3 = add((3, 3, 0), (kept, got, near7), 1, name="add_far3")
    near56 = passed(near56, (far3,), "passed_near")
    totals = call(
        totals_kernel,
        "totals",
        [VMEM] * 5,
        [HBM] * 3 + [RESULT] * 2,
        [shape_of(biases.shape)] * 3 + [shape_of((1, 1))] * 2,
        [pltpu.VMEM((1, biases.shape[0]), F32)] * 3 + [pltpu.SemaphoreType.DMA((3,))],
    )(far3, all_stats, *bias_rows)
    flat = totals[:3]
    far3 = swap(far3, wide_perm(1))
    far2 = add((2, 2, 1), (kept, got, near56), 1, name="add_far2")
    far2 = swap(far2, wide_perm(1))
    last = add(
        (1, 1, 0, 0),
        (kept, got, near56, far3),
        1,
        [(HBM, row) for row in flat],
        name="add_last",
    )
    new_resid6 = new_resid6_part(0, ins // 2, last, head, acc6, noise6)
    last = swap(last, wide_perm(2))
    mine = add(
        (0,) * 5, (kept, got, near4, far2, last), 1, [(HBM, new_resid6)], name="add_mine"
    )
    held = hold_moments(mine, moment6, moment7, moment8)
    theirs = swap(mine, grp_perm(2))

    moment, moment_low = call(
        functools.partial(moment_kernel, sizes),
        "moment",
        [VMEM] * 4,
        [VMEM] * 2,
        [shape_of((1,) + half), shape_of((1,) + half, BF16)],
    )(head, held, mine, theirs)
    new_resid6 = new_resid6_part(
        ins // 2, ins // 2, moment_low, head, acc6, noise6, new_resid6
    )
    new_resid7, new_resid8 = call(
        small_resids_kernel,
        "small_resids",
        [VMEM] * 6,
        [RESULT] * 2,
        [shape_of(acc7.shape), shape_of(acc8.shape)],
    )(moment_low, head, acc7, noise7, acc8, noise8)
    grams = [shape_of((h1, h1)), shape_of((2 * LANE, 2 * LANE))]

    def beside_last(trio, one3):
        four, again = relay(trio, one3, (moment,))
        early = call(
            functools.partial(early_kernel, sizes),
            "early_grams",
            [VMEM],
            [VMEM] * 2,
            grams,
            megabytes=8,
        )(four)
        momenta = call(
            functools.partial(momenta_kernel, sizes),
            "momenta",
            [VMEM] * 2,
            [HBM, HBM, RESULT, VMEM, VMEM],
            [
                shape_of(moment6.shape),
                shape_of(moment7.shape),
                shape_of(moment8.shape[::-1]),
                shape_of(moment6.shape),
                shape_of((2 * rows7 + rows8, 2 * LANE)),
            ],
            [pltpu.VMEM(moment7.shape, F32), pltpu.SemaphoreType.DMA((3,))],
        )(again, swap(again, grp_perm(1)))

        def begun(trio4, other_four):
            middle = call(
                functools.partial(middle_kernel, sizes),
                "middle_grams",
                [VMEM] * 4,
                [VMEM] * 4,
                grams * 2,
                megabytes=8,
            )(*early, trio4, other_four)
            return [momenta[3], middle[0], middle[2], *middle, *momenta]

        return four, begun

    moments, done = gather_halves(
        moment_low, [(HBM, new_resid6), (HBM, new_resid8)], beside_last
    )
    middle, (mom6, mom7, mom8, near6, near78) = done[3:7], done[7:]
    late = call(
        functools.partial(late_kernel, sizes),
        "late_grams",
        [VMEM] * 6,
        [VMEM] * 4,
        grams * 2,
        megabytes=8,
    )(*middle, moments[2], moments[4])

    updated = call(
        functools.partial(update_kernel, sizes),
        "update",
        [VMEM] * 10,
        [RESULT] * 6,
        [
            shape_of(weight6.shape),
            shape_of(weight7.shape),
            shape_of(weight8.shape[::-1]),
            shape_of(weight6.shape, BF16),
            shape_of(weight7.shape, BF16),
            shape_of(weight8.shape[::-1], BF16),
        ],
        megabytes=16,
    )(*late, moments[5], near6, near78, weight6, weight7, weight8.T)
    new6, new7, new8, low6, low7, low8 = updated
    return (
        new6,
        new7,
        new8.T,
        low6,
        low7,
        low8.T,
        mom6,
        mom7,
        mom8.T,
        new_resid6,
        new_resid7.T,
        new_resid8.T,
        *flat,
        *[array.reshape(()) for array in totals[3:]],
    )


def on_device(*arrays):
    (ins, h1), (_, h2), (_, classes) = [array.shape for array in arrays[9:12]]
    rows6, rows7, rows8 = [array.shape[0] for array in arrays[3:6]]
    paired = (
        (lax.axis_size("grp"), lax.axis_size("wide")) == (4, 8)
        and h1 == 3 * LANE
        and LANE < h2 < 2 * LANE
        and h2 + classes <= 2 * LANE
        and rows6 % 32 == 0
        and rows7 == rows8 * 2
        and rows8 % 24 == 0
        and ins % (2 * LANE) == 0
        and 16 * rows7 // 2 == h1
    )
    return (paired_plan if paired else general_plan)(*arrays)


def solution(mesh):
    split_both = P(BOTH, None)
    split_wide = P("wide", None)
    return jax.shard_map(
        on_device,
        mesh=mesh,
        in_specs=(
            split_both,
            P(BOTH),
            P(BOTH),
            *[split_wide] * 6,
            *[split_both] * 6,
            P(),
            P(),
            P(),
        ),
        out_specs=(*[split_wide] * 9, *[split_both] * 3, P(), P(), P(), P(), P()),
        check_vma=False,
    )
```

```python
import functools

import jax
import jax.numpy as jnp
from jax import lax
from jax.experimental import pallas as pl
from jax.experimental.pallas import tpu as pltpu
from jax.sharding import PartitionSpec as P

NS_STEPS = 5
ADAM_STEP = 10


highest = lax.Precision.HIGHEST
smoothing = 0.1
clip_width = 2.5
noise_levels = 1024.0
ramp_slope = 2.0
momentum_decay = 0.95
muon_rate = 0.6
decay_rate = 0.01
coef_a = 3.4445
coef_b = -4.775
coef_c = 2.0315
beta_first = 0.9
beta_second = 0.999
bias_rate = 0.05
adam_eps = 1e-08

F32 = jnp.float32
BF16 = jnp.bfloat16
LANE = 128
BOTH = ("grp", "wide")


def dithered_code(clipped, peak, noise):
    ratio = jnp.abs(clipped) / peak
    dither = (noise.astype(jnp.float32) + 0.5) / noise_levels
    return jnp.sign(clipped) * jnp.clip(ramp_slope * (ratio - dither) + ratio, 0.0, 1.0)


def gram_of(iterate):
    return jnp.dot(iterate.T, iterate, precision=highest)


def schulz_step(iterate, gram_matrix):
    mixed = coef_b * gram_matrix + coef_c * jnp.dot(gram_matrix, gram_matrix, precision=highest)
    return coef_a * iterate + jnp.dot(iterate, mixed, precision=highest)


def layer_forward(inputs_b, weight_b, bias_part):
    return jnp.dot(inputs_b, weight_b, preferred_element_type=jnp.float32) + bias_part


def layer_backward(inputs_b, weight_b, grad_pre):
    grad_low = grad_pre.astype(jnp.bfloat16)
    weight_grad = jnp.einsum("ri,ro->io", inputs_b, grad_low, preferred_element_type=jnp.float32)
    bias_grad = jnp.sum(grad_low.astype(jnp.float32), axis=0)
    grad_inputs = jnp.einsum("ro,io->ri", grad_low, weight_b, preferred_element_type=jnp.float32)
    return (weight_grad, bias_grad, grad_inputs)


def adam_biases(biases, bias_first, bias_second, bias_grad):
    first_new = beta_first * bias_first + (1.0 - beta_first) * bias_grad
    second_new = beta_second * bias_second + (1.0 - beta_second) * bias_grad * bias_grad
    first_hat = first_new / (1.0 - beta_first**ADAM_STEP)
    second_hat = second_new / (1.0 - beta_second**ADAM_STEP)
    biases_new = biases - bias_rate * (
        first_hat / (jnp.sqrt(second_hat) + adam_eps) + decay_rate * biases
    )
    return biases_new, first_new, second_new


def general_plan(
    features,
    labels,
    counts,
    weight6,
    weight7,
    weight8,
    moment6,
    moment7,
    moment8,
    resid6,
    resid7,
    resid8,
    noise6,
    noise7,
    noise8,
    biases,
    bias_first,
    bias_second,
):
    masters = (weight6, weight7, weight8)
    weights_b = [
        lax.all_gather(weight.astype(jnp.bfloat16), "wide", axis=0, tiled=True)
        for weight in masters
    ]
    widths = [weights_b[0].shape[1], weights_b[1].shape[1], weights_b[2].shape[1]]
    bias_parts = [
        biases[: widths[0]],
        biases[widths[0] : widths[0] + widths[1]],
        biases[widths[0] + widths[1] :],
    ]
    row_mask = (jnp.arange(features.shape[0]) < counts[0]).astype(jnp.float32)
    inputs_list = [features]
    gelu_backs = []
    logits = None
    for which_layer in range(3):
        pre_act = layer_forward(
            inputs_list[which_layer], weights_b[which_layer], bias_parts[which_layer]
        )
        if which_layer < 2:
            activ, gelu_back = jax.vjp(jax.nn.gelu, pre_act)
            inputs_list.append(activ.astype(jnp.bfloat16))
            gelu_backs.append(gelu_back)
        else:
            logits = pre_act
    logp = jax.nn.log_softmax(logits, axis=-1)
    onehot = (labels[:, None] == jnp.arange(widths[2])[None, :]).astype(jnp.float32)
    target = (1.0 - smoothing) * onehot + smoothing / widths[2]
    worker_loss = jnp.sum(-jnp.sum(target * logp, axis=-1) * row_mask)
    upstream = -target * row_mask[:, None]
    grad_pre = upstream - jnp.exp(logp) * jnp.sum(upstream, axis=-1, keepdims=True)
    weight_grads = [None, None, None]
    bias_grads = [None, None, None]
    for which_layer in (2, 1, 0):
        weight_grads[which_layer], bias_grads[which_layer], grad_inputs = layer_backward(
            inputs_list[which_layer], weights_b[which_layer], grad_pre
        )
        if which_layer > 0:
            grad_pre = gelu_backs[which_layer - 1](grad_inputs)[0]
    resids = (resid6, resid7, resid8)
    noises = (noise6, noise7, noise8)
    accs = [weight_grads[k] + resids[k] for k in range(3)]
    clipped_list = []
    for acc in accs:
        bound = clip_width * jnp.sqrt(jnp.mean(acc * acc))
        clipped_list.append(jnp.clip(acc, -bound, bound))
    peak_list = lax.pmax(tuple(jnp.max(jnp.abs(clipped)) for clipped in clipped_list), BOTH)
    peak_list = [p + 1e-06 for p in peak_list]
    code_list = [dithered_code(clipped_list[k], peak_list[k], noises[k]) for k in range(3)]
    new_resids = [accs[k] - peak_list[k] * code_list[k] for k in range(3)]
    loss_total, image_total, bias_total = lax.psum(
        (worker_loss, jnp.sum(row_mask), jnp.concatenate(bias_grads)), BOTH
    )
    code_rows = [
        lax.psum_scatter(code, "wide", scatter_dimension=0, tiled=True) for code in code_list
    ]
    code_sums = lax.psum(tuple(code_rows), "grp")
    moments = (moment6, moment7, moment8)
    new_moments = [
        momentum_decay * moments[k] + peak_list[k] * code_sums[k] / image_total for k in range(3)
    ]
    full_moments = [
        lax.all_gather(moment, "wide", axis=0, tiled=True) for moment in new_moments
    ]
    row_block = lax.axis_index("wide")
    iterates = []
    for k in range(3):
        whole = full_moments[k]
        iterate = whole / (jnp.sqrt(jnp.sum(whole * whole)) + 1e-07)
        for step_num in range(NS_STEPS):
            iterate = schulz_step(iterate, gram_of(iterate))
        row_count = new_moments[k].shape[0]
        iterates.append(lax.dynamic_slice_in_dim(iterate, row_block * row_count, row_count, 0))
    new_weights = [
        masters[k] - muon_rate * (iterates[k] + decay_rate * masters[k]) for k in range(3)
    ]
    new_biases = adam_biases(biases, bias_first, bias_second, bias_total / image_total)
    return (
        *new_weights,
        *[weight.astype(jnp.bfloat16) for weight in new_weights],
        *new_moments,
        *new_resids,
        *new_biases,
        loss_total,
        image_total,
    )


ORDERS = ((2, 1, 4), (1, 2, 4))


def half_of(grp, wide):
    return (grp + wide + (wide >> 1)) & 1


def wide_perm(phase):
    pairs = []
    for g in range(4):
        for w in range(8):
            bit = ORDERS[half_of(g, w)][phase]
            pairs.append((g * 8 + w, (g ^ (bit < 4)) * 8 + (w ^ bit)))
    return pairs


def grp_perm(bit):
    return [(g * 8 + w, (g ^ bit) * 8 + w) for g in range(4) for w in range(8)]


def swap(array, perm):
    return lax.ppermute(array, BOTH, perm)


def own_half():
    return half_of(lax.axis_index("grp"), lax.axis_index("wide"))


def half_at(place, same_core):
    core = own_half() if same_core else 1 - own_half()
    masks = [
        sum(order[phase] for phase in range(3) if place & (4 >> phase)) for order in ORDERS
    ]
    return 2 * (lax.axis_index("wide") ^ jnp.where(core == 0, masks[0], masks[1])) + core


def dims(contract_left, contract_right):
    return (((contract_left,), (contract_right,)), ((), ()))


def mxu(left, right, contract_left=1, contract_right=0):
    return lax.dot_general(
        left, right, dims(contract_left, contract_right), preferred_element_type=F32
    )


def split(value):
    high = value.astype(BF16)
    return high, (value - high.astype(F32)).astype(BF16)


def left_parts(value):
    high, rest = split(value)
    return jnp.concatenate([high, high, rest], axis=1)


def right_parts(value):
    high, rest = split(value)
    return jnp.concatenate([high, rest, high], axis=0)


def shifted_eye(rows, cols, shift, dtype):
    at = lax.broadcasted_iota(jnp.int32, (rows, cols), 0) + shift
    return (at == lax.broadcasted_iota(jnp.int32, (rows, cols), 1)).astype(dtype)


def upright(flat, shift, dtype=BF16):
    return mxu(flat.astype(BF16), shifted_eye(flat.shape[0], 2 * LANE, shift, BF16), 0, 0)


def fold(region):
    n = region.shape[0] // 3
    third = jnp.concatenate([region[2 * n :, :LANE], region[2 * n :, LANE:]], axis=0)
    return jnp.concatenate([region[: 2 * n], third], axis=1)


def unfold(folded):
    n = folded.shape[0] // 2
    last = jnp.concatenate([folded[:n, 2 * LANE :], folded[n:, 2 * LANE :]], axis=1)
    return jnp.concatenate([folded[:, : 2 * LANE], last], axis=0)


HBM = pl.BlockSpec(memory_space=pltpu.HBM)
SMEM = pl.BlockSpec(memory_space=pltpu.SMEM)
VMEM = pl.BlockSpec(memory_space=pltpu.VMEM)
RESULT = pl.BlockSpec(memory_space=pltpu.VMEM)


def shape_of(shape, dtype=F32):
    return jax.ShapeDtypeStruct(shape, dtype)


MICROS = {"passed": 5.0, "passed_last": 20.0, "passed_one": 20.0, "add_far3": 20.0, "relay": 10.0, "first_join": 20.0}


def placed(shape, spec):
    if spec is HBM:
        return pltpu.HBM(shape.shape, shape.dtype)
    return pltpu.VMEM(shape.shape, shape.dtype) if spec is VMEM else shape


def call(kernel, name, in_specs, out_specs, out_shape, scratch=(), megabytes=4, aliases=None):
    many = isinstance(out_shape, list)
    shapes = [
        placed(shape, spec)
        for shape, spec in zip(
            out_shape if many else [out_shape], out_specs if many else [out_specs]
        )
    ]
    kernel_call = pl.pallas_call(
        kernel,
        in_specs=in_specs,
        out_specs=out_specs,
        out_shape=shapes if many else shapes[0],
        scratch_shapes=list(scratch),
        compiler_params=pltpu.CompilerParams(vmem_limit_bytes=megabytes * 1024 * 1024),
        cost_estimate=pl.CostEstimate(
            flops=int(MICROS.get(name, 0.0) * 1.15e9), bytes_accessed=0, transcendentals=0
        ),
        input_output_aliases=aliases or {},
        name=name,
    )

    def run(*arrays):
        return kernel_call(
            *[
                pltpu.with_memory_space_constraint(array, pltpu.HBM) if spec is HBM else array
                for array, spec in zip(arrays, in_specs)
            ]
        )

    return run


def pack_kernel(w6_ref, w7_ref, w8_ref, out_ref, half6, half7, all8, sems):
    core = own_half()
    rows6, rows7 = half6.shape[0], half7.shape[0]
    copies = [
        pltpu.make_async_copy(
            w6_ref.at[pl.ds(pl.multiple_of(core * rows6, 8), rows6)], half6, sems.at[0]
        ),
        pltpu.make_async_copy(
            w7_ref.at[pl.ds(pl.multiple_of(core * rows7, 8), rows7)], half7, sems.at[1]
        ),
        pltpu.make_async_copy(w8_ref, all8, sems.at[2]),
    ]
    for copy in copies:
        copy.start()
    for copy in copies:
        copy.wait()
    out_ref[0, :rows6, :] = half6[...].astype(BF16)
    h2 = half7.shape[1]
    lead = (core == 0).astype(F32)
    region = upright(all8[...], h2) * lead + jnp.concatenate(
        [half7[...], jnp.zeros((rows7, 2 * LANE - h2), F32)], axis=1
    )
    out_ref[0, rows6:, :] = fold(region).astype(BF16)


def pack_weights(weight6, weight7, weight8):
    rows6, h1 = weight6.shape[0] // 2, weight6.shape[1]
    rows7, h2 = weight7.shape[0] // 2, weight7.shape[1]
    return call(
        pack_kernel,
        "pack_weights",
        [HBM] * 3,
        VMEM,
        shape_of((1, rows6 + rows7 * 2 // 3, h1), BF16),
        [
            pltpu.VMEM((rows6, h1), F32),
            pltpu.VMEM((rows7, h2), F32),
            pltpu.VMEM(weight8.shape[::-1], F32),
            pltpu.SemaphoreType.DMA((3,)),
        ],
    )(weight6, weight7, weight8.T)


def stage_kernel(count, after_ref, images_ref, *refs):
    ins, outs, token_ref, sems = refs[:count], refs[count:-2], refs[-2], refs[-1]
    copies = [
        pltpu.make_async_copy(
            source, target if len(source.shape) == len(target.shape) else target.at[0], sems.at[k]
        )
        for k, (source, target) in enumerate(zip(ins, outs))
    ]
    for copy in copies:
        copy.start()
    token_ref[...] = jnp.full(token_ref.shape, images_ref[0], jnp.int32)
    for copy in copies:
        copy.wait()


def stage(after, counts, *arrays):
    count = len(arrays)
    shapes = [(1,) * (2 - array.ndim) + array.shape for array in arrays]
    return call(
        functools.partial(stage_kernel, count),
        "stage",
        [VMEM, SMEM] + [HBM] * count,
        [VMEM] * (count + 1),
        [shape_of(shape, array.dtype) for shape, array in zip(shapes, arrays)]
        + [shape_of((1, LANE), jnp.int32)],
        [pltpu.SemaphoreType.DMA((count,))],
    )(after, counts, *arrays)


def add_kernel(picks, size, *refs):
    for k in range(size):
        total = None
        for ref, pick in zip(refs, picks):
            part = ref[pick + k].astype(F32)
            total = part if total is None else total + part
        refs[-1][k] = total.astype(BF16)


def add(picks, arrays, size, after=(), name="add"):
    shape = shape_of((size,) + arrays[0].shape[1:], BF16)
    specs = [VMEM] * len(arrays) + [spec for spec, _ in after]
    return call(functools.partial(add_kernel, picks, size), name, specs, VMEM, shape)(
        *arrays, *[array for _, array in after]
    )


def pass_kernel(in_ref, *refs):
    refs[-1][...] = in_ref[...]


def passed(array, after, name="passed"):
    specs = [VMEM] * (1 + len(after))
    shape = shape_of(array.shape, array.dtype)
    return call(pass_kernel, name, specs, VMEM, shape)(array, *after)


def first_join_kernel(own_ref, far_ref, mid_ref, *refs):
    trio_ref, again_ref = refs[-2:]
    for k, ref in enumerate((own_ref, far_ref, mid_ref)):
        trio_ref[k] = ref[0]
    again_ref[...] = far_ref[...]


def relay_kernel(trio_ref, one_ref, *refs):
    outs = refs[len(refs) // 2 :]
    count = trio_ref.shape[0]
    outs[0][:count] = trio_ref[...]
    outs[0][count:] = one_ref[...]
    if len(refs) > 1:
        outs[1][...] = refs[0][...]


def relay(trio, one, beside=()):
    joined = shape_of((trio.shape[0] + one.shape[0],) + one.shape[1:], one.dtype)
    shapes = [joined] + [shape_of(array.shape, array.dtype) for array in beside]
    ins = [trio, one, *beside]
    return call(relay_kernel, "relay", [VMEM] * len(ins), [VMEM] * len(shapes), shapes)(*ins)


def gather_halves(own, after=(), work=None):
    far = swap(own, wide_perm(2))
    mid = swap(own, wide_perm(1))
    trio, far = call(
        first_join_kernel,
        "first_join",
        [VMEM] * 3 + [spec for spec, _ in after],
        [VMEM] * 2,
        [shape_of((3,) + own.shape[1:], BF16), shape_of(own.shape, BF16)],
    )(own, far, mid, *[array for _, array in after])
    trio4 = swap(trio, wide_perm(0))
    one3 = swap(far, wide_perm(1))
    one3 = passed(one3, (), "passed_one")
    one7 = swap(one3, wide_perm(0))
    four, begun = (relay(trio, one3)[0], None) if work is None else work(trio, one3)
    trio4 = passed(trio4, (four,))
    other_four = swap(four, grp_perm(1))
    done = (four,) if work is None else begun(trio4, other_four)
    one7 = passed(one7, done[:3], "passed_last")
    others = (other_four, swap(trio4, grp_perm(1)), swap(one7, grp_perm(1)))
    return (four, trio4, one7, *others), done


def gelu_pair(pre):
    slope = 0.7978845608028654
    inner = slope * (pre + 0.044715 * pre * pre * pre)
    t = jnp.tanh(inner)
    value = 0.5 * pre * (1.0 + t)
    back = 0.5 * (1.0 + t) + 0.5 * pre * (1.0 - t * t) * slope * (1.0 + 3 * 0.044715 * pre * pre)
    return value, back


def place_all(sizes, refs, all6, all7, all8):
    ins, h1, h2, classes, rows6, rows7, rows8 = sizes
    for at in range(16):
        place = at % 8
        ref, q = refs[3 * (at // 8) + (0, 0, 0, 0, 1, 1, 1, 2)[place]], place % 4 % (4 - place // 4)
        half = half_at(place, at < 8)
        all6[pl.ds(pl.multiple_of(half * rows6, 16), rows6), :] = ref[q, :rows6, :]
        region = unfold(ref[q, rows6:, :].astype(F32))
        all7[pl.ds(pl.multiple_of(half * rows7, 8), rows7), :] = region

        @pl.when(half % 2 == 0)
        def _():
            row = pl.multiple_of((half // 2) * rows8, 8)
            all8[pl.ds(row, rows8), :] = region[:rows8, LANE:]


def worker_kernel(sizes, tile, *refs):
    ins, h1, h2, classes, rows6, rows7, rows8 = sizes
    halves, refs = refs[:6], refs[6:]
    count_ref, feat_ref, label_ref, bias_ref, resid6_ref, resid7_ref, resid8_ref = refs[:7]
    acc6_ref, acc7_ref, acc8_ref, stats_ref, w6, w7, w8 = refs[7:]
    first = h2 - LANE

    place_all(sizes, halves, w6, w7, w8)
    w7_low = w7[:, :h2].astype(BF16)
    w8_low = w8[...].astype(BF16)

    rows = feat_ref.shape[0]
    row_mask = (lax.broadcasted_iota(jnp.int32, (rows, 1), 0) < count_ref[:, :1]).astype(F32)
    lanes = lax.broadcasted_iota(jnp.int32, (rows, LANE), 1) - first
    valid = (lanes >= 0) & (lanes < classes)
    labels = jnp.sum(
        jnp.where(shifted_eye(rows, rows, 0, jnp.bool_), label_ref[...], 0), axis=1, keepdims=True
    )
    bias8 = jnp.concatenate(
        [bias_ref[:, h1 + LANE :], jnp.zeros((1, LANE - first - classes), F32)], axis=1
    )

    pre6 = mxu(feat_ref[...], w6[...]) + bias_ref[:, :h1]
    act6, back6 = gelu_pair(pre6)
    act6 = act6.astype(BF16)
    pre7 = mxu(act6, w7_low) + bias_ref[:, h1 : h1 + h2]
    act7, back7 = gelu_pair(pre7)
    act7 = act7.astype(BF16)
    logits = jnp.where(valid, mxu(act7, w8_low) + bias8, -1e30)
    shifted = logits - jnp.max(logits, axis=1, keepdims=True)
    logp = shifted - jnp.log(jnp.sum(jnp.exp(shifted), axis=1, keepdims=True))
    onehot = (labels == lanes).astype(F32)
    target = jnp.where(valid, (1.0 - smoothing) * onehot + smoothing / classes, 0.0)
    loss = jnp.sum(-jnp.sum(target * jnp.where(valid, logp, 0.0), axis=1, keepdims=True) * row_mask)
    weight = jnp.sum(target, axis=1, keepdims=True)
    dlogits = (row_mask * (jnp.exp(logp) * weight - target)).astype(BF16)
    dpre7 = (mxu(dlogits, w8_low, 1, 1) * back7).astype(BF16)
    dpre6 = (mxu(dpre7, w7_low, 1, 1) * back6).astype(BF16)

    square6 = jnp.zeros((8, h1), F32)
    most6 = jnp.zeros((8, h1), F32)
    for t in range(ins // tile):
        part = slice(t * tile, (t + 1) * tile)
        acc = resid6_ref[part, :] + mxu(feat_ref[:, part], dpre6, 0, 0)
        acc6_ref[part, :] = acc
        square6 = square6 + jnp.sum((acc * acc).reshape(tile // 8, 8, h1), axis=0)
        most6 = jnp.maximum(most6, jnp.max(jnp.abs(acc).reshape(tile // 8, 8, h1), axis=0))
    acc7 = mxu(dpre7, act6, 0, 0) + resid7_ref[...]
    acc7_ref[...] = acc7
    acc8 = mxu(dlogits, act7, 0, 0)[first : first + classes, :] + resid8_ref[...]
    acc8_ref[...] = acc8

    bound6 = clip_width * jnp.sqrt(jnp.sum(square6) * (1.0 / (ins * h1)))
    bound7 = clip_width * jnp.sqrt(jnp.sum(acc7 * acc7) * (1.0 / (h1 * h2)))
    bound8 = clip_width * jnp.sqrt(jnp.sum(acc8 * acc8) * (1.0 / (h2 * classes)))
    peak6 = jnp.minimum(jnp.max(most6), bound6)
    peak7 = jnp.minimum(jnp.max(jnp.abs(acc7)), bound7)
    peak8 = jnp.minimum(jnp.max(jnp.abs(acc8)), bound8)
    lane = lax.broadcasted_iota(jnp.int32, (1, LANE), 1) - (first + classes)
    tail = jnp.zeros((1, LANE), F32)
    count = count_ref[:, :1].astype(F32)
    for k, value in enumerate((peak6, peak7, peak8, loss, count, bound6, bound7, bound8)):
        tail = jnp.where(lane == k, value, tail)
    db6 = jnp.sum(dpre6.astype(F32), axis=0, keepdims=True)
    db7 = jnp.sum(dpre7.astype(F32), axis=0, keepdims=True)
    db8 = jnp.sum(dlogits.astype(F32), axis=0, keepdims=True)
    db7 = jnp.concatenate([db7, jnp.zeros((1, 2 * LANE - h2), F32)], axis=1)
    row = jnp.concatenate([db6, db7[:, :LANE], db7[:, LANE:] + db8 + tail], axis=1)
    stats_ref[...] = jnp.broadcast_to(row[None], stats_ref.shape)


def code_of(acc, bound, scale, noise):
    ramp = jnp.minimum(jnp.abs(acc), bound) * scale - (
        noise.astype(F32) * (ramp_slope / noise_levels) + 0.5 * ramp_slope / noise_levels
    )
    ramp = jnp.clip(ramp, 0.0, 1.0)
    return jnp.where(acc < 0, -ramp, ramp)


def lane_of(row_ref, k):
    return row_ref[0:1, k : k + 1]


def write_codes(sizes, places, same_core, head, acc6_ref, noise6_ref, code7, code8, out):
    ins, h1, h2, classes, rows6, rows7, rows8 = sizes
    peak, bound = lane_of(head, 0), lane_of(head, 3)
    scale = (1.0 + ramp_slope) / peak
    for at, place in enumerate(places):
        half = half_at(place, same_core)
        part = pl.ds(pl.multiple_of(half * rows6, 8), rows6)
        code = code_of(acc6_ref[part, :], bound, scale, noise6_ref[part, :])
        out[at, :rows6, :] = code.astype(BF16)
        region = code7[pl.ds(pl.multiple_of(half * rows7, 8), rows7), :]
        lead = (half % 2 == 0).astype(F32)
        region = region + lead * code8[pl.ds(pl.multiple_of((half // 2) * rows8, 8), rows8), :]
        out[at, rows6:, :] = fold(region).astype(BF16)


def first_codes_kernel(sizes, places, stats_ref, mine_ref, acc6_ref, noise6_ref, *refs):
    ins, h1, h2, classes, rows6, rows7, rows8 = sizes
    acc7_ref, noise7_ref, acc8_ref, noise8_ref, out_ref, head_ref, code7, code8 = refs
    at = h1 + h2 + classes
    most = jnp.max(stats_ref[:, :, at : at + 3], axis=0) + 1e-06
    images = jnp.sum(stats_ref[:, :, at + 4 : at + 5], axis=0)
    lane = lax.broadcasted_iota(jnp.int32, (1, LANE), 1)
    head = jnp.zeros((1, LANE), F32)
    for k in range(3):
        head = jnp.where(lane == k, most[:, k : k + 1], head)
        head = jnp.where(lane == 3 + k, mine_ref[0, :, at + 5 + k : at + 6 + k], head)
        head = jnp.where(lane == 6 + k, most[:, k : k + 1] / images, head)
    head_ref[...] = head
    ramp = 1.0 + ramp_slope
    small7 = code_of(acc7_ref[...], lane_of(head, 4), ramp / lane_of(head, 1), noise7_ref[...])
    small8 = code_of(acc8_ref[...], lane_of(head, 5), ramp / lane_of(head, 2), noise8_ref[...])
    code7[...] = upright(small7, 0)
    code8[...] = upright(small8, h2)
    write_codes(sizes, places, False, head, acc6_ref, noise6_ref, code7, code8, out_ref)


def codes_kernel(sizes, places, same_core, head_ref, acc6, noise6, code7, code8, *refs):
    write_codes(sizes, places, same_core, head_ref, acc6, noise6, code7, code8, refs[-1])


def resid_of(head, layer, acc, noise):
    peak = lane_of(head, layer)
    return acc - peak * code_of(acc, lane_of(head, 3 + layer), (1.0 + ramp_slope) / peak, noise)


def resid_kernel(tile, start, after_ref, head_ref, acc6_ref, noise6_ref, *refs):
    out_ref, hold, sems = refs[-3:]
    head = head_ref[...]
    copies = []
    for t in range(hold.shape[0] // tile):
        here, there = pl.ds(t * tile, tile), pl.ds(start + t * tile, tile)
        hold[here, :] = resid_of(head, 0, acc6_ref[there, :], noise6_ref[there, :])
        copies.append(pltpu.make_async_copy(hold.at[here], out_ref.at[there], sems.at[t]))
        copies[-1].start()
    for copy in copies:
        copy.wait()


def new_resid6_part(start, rows, after, head, acc6, noise6, before=None):
    tile = 3 * LANE
    ins = [after, head, acc6, noise6] + ([] if before is None else [before])
    return call(
        functools.partial(resid_kernel, tile, start),
        "new_resid",
        [VMEM] * 4 + [HBM] * (len(ins) - 4),
        HBM,
        shape_of(acc6.shape),
        [pltpu.VMEM((rows, acc6.shape[1]), F32), pltpu.SemaphoreType.DMA((rows // tile,))],
        megabytes=8,
        aliases={} if before is None else {4: 0},
    )(*ins)


def small_resids_kernel(after_ref, head_ref, acc7_ref, noise7_ref, acc8_ref, noise8_ref, *outs):
    head = head_ref[...]
    outs[0][...] = resid_of(head, 1, acc7_ref[...], noise7_ref[...])
    outs[1][...] = resid_of(head, 2, acc8_ref[...], noise8_ref[...])


def totals_kernel(after_ref, stats_ref, bias_ref, first_ref, second_ref, *refs):
    outs, loss_ref, images_ref, rows, sems = refs[:3], refs[3], refs[4], refs[5:8], refs[8]
    width = bias_ref.shape[1]
    total = jnp.sum(stats_ref[...], axis=0)
    images = total[:, width + 4 : width + 5]
    loss_ref[...] = total[:, width + 3 : width + 4]
    images_ref[...] = images
    rows[0][...], rows[1][...], rows[2][...] = adam_biases(
        bias_ref[...], first_ref[...], second_ref[...], total[:, :width] / images
    )
    copies = [
        pltpu.make_async_copy(row.at[0], out, sems.at[k])
        for k, (row, out) in enumerate(zip(rows, outs))
    ]
    for copy in copies:
        copy.start()
    for copy in copies:
        copy.wait()


def hold_kernel(after_ref, m6_ref, m7_ref, m8_ref, out_ref, half7, all8, sems):
    core = own_half()
    rows7, h2 = half7.shape
    rows6 = out_ref.shape[1] - rows7 * 2 // 3
    copies = [
        pltpu.make_async_copy(
            m6_ref.at[pl.ds(pl.multiple_of(core * rows6, 8), rows6)],
            out_ref.at[0, pl.ds(0, rows6)],
            sems.at[0],
        ),
        pltpu.make_async_copy(
            m7_ref.at[pl.ds(pl.multiple_of(core * rows7, 8), rows7)], half7, sems.at[1]
        ),
        pltpu.make_async_copy(m8_ref, all8, sems.at[2]),
    ]
    for copy in copies:
        copy.start()
    for copy in copies:
        copy.wait()
    lead = (core == 0).astype(F32)
    tall = jnp.zeros((rows7, 2 * LANE), F32)
    parts = all8[...]
    for _ in range(3):
        high = parts.astype(BF16)
        tall = tall + upright(high, h2)
        parts = parts - high.astype(F32)
    region = tall * lead + jnp.concatenate(
        [half7[...], jnp.zeros((rows7, 2 * LANE - h2), F32)], axis=1
    )
    out_ref[0, rows6:, :] = fold(region)


def hold_moments(after, moment6, moment7, moment8):
    rows6, h1 = moment6.shape[0] // 2, moment6.shape[1]
    rows7, h2 = moment7.shape[0] // 2, moment7.shape[1]
    return call(
        hold_kernel,
        "hold_moments",
        [VMEM] + [HBM] * 3,
        VMEM,
        shape_of((1, rows6 + rows7 * 2 // 3, h1)),
        [
            pltpu.VMEM((rows7, h2), F32),
            pltpu.VMEM(moment8.shape[::-1], F32),
            pltpu.SemaphoreType.DMA((3,)),
        ],
    )(after, moment6, moment7, moment8.T)


def moment_kernel(sizes, head_ref, held_ref, mine_ref, theirs_ref, out_ref, low_ref):
    ins, h1, h2, classes, rows6, rows7, rows8 = sizes
    codes = mine_ref[0].astype(F32) + theirs_ref[0].astype(F32)
    moment6 = momentum_decay * held_ref[0, :rows6] + lane_of(head_ref, 6) * codes[:rows6]
    column = lax.broadcasted_iota(jnp.int32, (rows7, 2 * LANE), 1)
    rate = fold(jnp.where(column < h2, lane_of(head_ref, 7), lane_of(head_ref, 8)))
    region = momentum_decay * held_ref[0, rows6:] + rate * codes[rows6:]
    out_ref[0, :rows6] = moment6
    out_ref[0, rows6:] = region
    low_ref[0, :rows6] = moment6.astype(BF16)
    low_ref[0, rows6:] = region.astype(BF16)


def schulz_chains(grams, iterates, inverses):
    diagonals = [shifted_eye(gram.shape[0], gram.shape[0], 0, F32) for gram in grams]
    for number in range(NS_STEPS):
        lefts = [left_parts(gram) for gram in grams]
        squares = [mxu(left, right_parts(gram)) for left, gram in zip(lefts, grams)]
        if number == 0:
            scales = [inverse * inverse for inverse in inverses]
            squares = [square * (scale * scale) for square, scale in zip(squares, scales)]
            grams = [gram * scale for gram, scale in zip(grams, scales)]
        mixed = [
            right_parts(coef_a * diagonal + coef_b * gram + coef_c * square)
            for diagonal, gram, square in zip(diagonals, grams, squares)
        ]
        rows = [left_parts(iterate) for iterate in iterates]
        if number == NS_STEPS - 1:
            return [mxu(row, right) for row, right in zip(rows, mixed)]
        both = [
            mxu(jnp.concatenate([left, row], axis=0), right)
            for left, row, right in zip(lefts, rows, mixed)
        ]
        iterates = [value[gram.shape[0] :] for value, gram in zip(both, grams)]
        products = [value[: gram.shape[0]] for value, gram in zip(both, grams)]
        if number == 0:
            iterates = [iterate * inverse for iterate, inverse in zip(iterates, inverses)]
            products = [product * scale for product, scale in zip(products, scales)]
        grams = [mxu(left_parts(product), right) for product, right in zip(products, mixed)]


def grams_of(sizes, ref):
    rows6 = sizes[4]
    places = range(ref.shape[0])
    block = jnp.concatenate([ref[k, :rows6, :] for k in places], axis=0)
    region = [unfold(ref[k, rows6:, :].astype(F32)) for k in places]
    region = jnp.concatenate(region, axis=0).astype(BF16)
    return mxu(block, block, 0, 0), mxu(region, region, 0, 0)


def early_kernel(sizes, four_ref, out6_ref, out78_ref):
    out6_ref[...], out78_ref[...] = grams_of(sizes, four_ref)


def middle_kernel(sizes, own6_ref, own78_ref, trio_ref, theirs_ref, *outs):
    trio6, trio78 = grams_of(sizes, trio_ref)
    outs[0][...] = own6_ref[...] + trio6
    outs[1][...] = own78_ref[...] + trio78
    outs[2][...], outs[3][...] = grams_of(sizes, theirs_ref)


def late_kernel(sizes, own6_ref, own78_ref, other6_ref, other78_ref, one_ref, trio_ref, *outs):
    one6, one78 = grams_of(sizes, one_ref)
    outs[0][...] = own6_ref[...] + one6
    outs[1][...] = own78_ref[...] + one78
    trio6, trio78 = grams_of(sizes, trio_ref)
    outs[2][...] = other6_ref[...] + trio6
    outs[3][...] = other78_ref[...] + trio78


def momenta_kernel(sizes, mine_ref, theirs_ref, *refs):
    ins, h1, h2, classes, rows6, rows7, rows8 = sizes
    out6_ref, out7_ref, out8_ref, near6_ref, near78_ref, stage7, sems = refs
    core = own_half()
    copies = []
    region8 = None
    for k, (at, ref) in enumerate(((core, mine_ref), (1 - core, theirs_ref))):
        part = pl.ds(pl.multiple_of(at * rows6, 8), rows6)
        near6_ref[part, :] = ref[0, :rows6, :]
        copies.append(
            pltpu.make_async_copy(ref.at[0, pl.ds(0, rows6)], out6_ref.at[part], sems.at[k])
        )
        copies[-1].start()
        region = unfold(ref[0, rows6:, :])
        near78_ref[pl.ds(pl.multiple_of(at * rows7, 8), rows7), :] = region
        region8 = region if region8 is None else jnp.where(core == 0, region8, region)
    column = lax.broadcasted_iota(jnp.int32, (2 * rows7, 2 * LANE), 1)
    near78_ref[: 2 * rows7, :] = jnp.where(column < h2, near78_ref[: 2 * rows7, :], 0.0)
    near78_ref[2 * rows7 :, :] = jnp.where(column[:rows8] < h2, 0.0, region8[:rows8])
    stage7[...] = near78_ref[: 2 * rows7, :h2]
    copies.append(pltpu.make_async_copy(stage7, out7_ref, sems.at[2]))
    copies[-1].start()
    out8_ref[...] = turned(sizes, near78_ref[2 * rows7 :, LANE:])
    for copy in copies:
        copy.wait()


def turned(sizes, rows):
    ins, h1, h2, classes, rows6, rows7, rows8 = sizes
    square = jnp.concatenate([rows, jnp.zeros((LANE - rows8, LANE), F32)], axis=0)
    return square.T[h2 - LANE : h2 - LANE + classes, :rows8]


def update_kernel(sizes, own6, own78, other6, other78, one7_ref, *refs):
    ins, h1, h2, classes, rows6, rows7, rows8 = sizes
    near6_ref, near78_ref, w6_ref, w7_ref, w8_ref, *outs = refs
    new6_ref, new7_ref, new8_ref, low6_ref, low7_ref, low8_ref = outs
    last6, last78 = grams_of(sizes, one7_ref)
    gram6 = own6[...] + (other6[...] + last6)
    gram7 = own78[...] + (other78[...] + last78)

    size = 2 * LANE
    is7_row = lax.broadcasted_iota(jnp.int32, (size, size), 0) < h2
    is7_col = lax.broadcasted_iota(jnp.int32, (size, size), 1) < h2
    diagonal = shifted_eye(size, size, 0, F32)
    inverse6 = 1.0 / (jnp.sqrt(jnp.sum(gram6 * shifted_eye(h1, h1, 0, F32))) + 1e-07)
    trace7 = jnp.sum(jnp.where(is7_col, gram7 * diagonal, 0.0))
    trace8 = jnp.sum(jnp.where(is7_col, 0.0, gram7 * diagonal))
    inverse7 = 1.0 / (jnp.sqrt(trace7) + 1e-07)
    inverse8 = 1.0 / (jnp.sqrt(trace8) + 1e-07)
    inverse = jnp.where(is7_col[:1], inverse7, inverse8)
    gram7 = jnp.where(is7_row == is7_col, gram7, 0.0)
    iterate6, iterate7 = schulz_chains(
        [gram6, gram7], [near6_ref[...], near78_ref[...]], [inverse6, inverse]
    )
    for iterate, w_ref, new_ref, low_ref in (
        (iterate6, w6_ref, new6_ref, low6_ref),
        (iterate7[: 2 * rows7, :h2], w7_ref, new7_ref, low7_ref),
        (turned(sizes, iterate7[2 * rows7 :, LANE:]), w8_ref, new8_ref, low8_ref),
    ):
        master = w_ref[...]
        value = master - muon_rate * (iterate + decay_rate * master)
        new_ref[...] = value
        low_ref[...] = value.astype(BF16)


def paired_plan(
    features,
    labels,
    counts,
    weight6,
    weight7,
    weight8,
    moment6,
    moment7,
    moment8,
    resid6,
    resid7,
    resid8,
    noise6,
    noise7,
    noise8,
    biases,
    bias_first,
    bias_second,
):
    ins, h1 = resid6.shape
    h2, classes = resid8.shape
    rows6 = weight6.shape[0] // 2
    rows7 = weight7.shape[0] // 2
    rows8 = weight8.shape[0]
    sizes = (ins, h1, h2, classes, rows6, rows7, rows8)
    devices = 32
    half = (rows6 + rows7 * 2 // 3, h1)

    packed = pack_weights(weight6, weight7, weight8)
    staged = stage(
        packed,
        counts,
        features,
        labels,
        biases,
        bias_first,
        bias_second,
        resid6,
        resid7.T,
        resid8.T,
        noise6,
        noise7.T,
        noise8.T,
    )
    features, labels, *bias_rows = staged[:5]
    resid6, resid7, resid8, noise6, noise7, noise8, count_row = staged[5:]
    halves, _ = gather_halves(packed, [(VMEM, count_row)])

    tile = 2 * LANE
    lanes = h1 + 2 * LANE
    acc6, acc7, acc8, stats = call(
        functools.partial(worker_kernel, sizes, tile),
        "worker",
        [VMEM] * 13,
        [VMEM] * 4,
        [
            shape_of((ins, h1)),
            shape_of((h2, h1)),
            shape_of((classes, h2)),
            shape_of((devices, 1, lanes)),
        ],
        [
            pltpu.VMEM((ins, h1), BF16),
            pltpu.VMEM((h1, 2 * LANE), F32),
            pltpu.VMEM((h2, LANE), F32),
        ],
        megabytes=16,
    )(*halves, count_row, features, labels, bias_rows[0], resid6, resid7, resid8)

    all_stats = lax.all_to_all(stats, BOTH, 0, 0, tiled=True)

    def halves_of(count):
        return shape_of((count,) + half, BF16)

    sent7, head, code7, code8 = call(
        functools.partial(first_codes_kernel, sizes, (7,)),
        "codes_first",
        [VMEM] * 8,
        [VMEM] * 4,
        [
            halves_of(1),
            shape_of((1, LANE)),
            shape_of((h1, 2 * LANE)),
            shape_of((h2, 2 * LANE)),
        ],
    )(all_stats, stats, acc6, noise6, acc7, noise7, acc8, noise8)

    def codes(places, same_core, after=()):
        return call(
            functools.partial(codes_kernel, sizes, places, same_core),
            "codes",
            [VMEM] * (5 + len(after)),
            VMEM,
            halves_of(len(places)),
        )(head, acc6, noise6, code7, code8, *after)

    got7 = swap(sent7, grp_perm(1))
    out7 = add((0, 0), (codes((7,), True), got7), 1)
    near7 = swap(out7, wide_perm(0))
    rest = tuple(range(7))
    got = swap(codes(rest, False, (out7,)), grp_perm(1))
    kept = codes(rest, True, (out7,))
    near56 = swap(add((5, 5), (kept, got), 2), wide_perm(0))
    near4 = swap(add((4, 4), (kept, got), 1), wide_perm(0))
    far3 = add((3, 3, 0), (kept, got, near7), 1, name="add_far3")
    near56 = passed(near56, (far3,), "passed_near")
    totals = call(
        totals_kernel,
        "totals",
        [VMEM] * 5,
        [HBM] * 3 + [RESULT] * 2,
        [shape_of(biases.shape)] * 3 + [shape_of((1, 1))] * 2,
        [pltpu.VMEM((1, biases.shape[0]), F32)] * 3 + [pltpu.SemaphoreType.DMA((3,))],
    )(far3, all_stats, *bias_rows)
    flat = totals[:3]
    far3 = swap(far3, wide_perm(1))
    far2 = add((2, 2, 1), (kept, got, near56), 1, name="add_far2")
    far2 = swap(far2, wide_perm(1))
    last = add(
        (1, 1, 0, 0),
        (kept, got, near56, far3),
        1,
        [(HBM, row) for row in flat],
        name="add_last",
    )
    new_resid6 = new_resid6_part(0, ins // 2, last, head, acc6, noise6)
    last = swap(last, wide_perm(2))
    mine = add(
        (0,) * 5, (kept, got, near4, far2, last), 1, [(HBM, new_resid6)], name="add_mine"
    )
    held = hold_moments(mine, moment6, moment7, moment8)
    theirs = swap(mine, grp_perm(2))

    moment, moment_low = call(
        functools.partial(moment_kernel, sizes),
        "moment",
        [VMEM] * 4,
        [VMEM] * 2,
        [shape_of((1,) + half), shape_of((1,) + half, BF16)],
    )(head, held, mine, theirs)
    new_resid6 = new_resid6_part(
        ins // 2, ins // 2, moment_low, head, acc6, noise6, new_resid6
    )
    new_resid7, new_resid8 = call(
        small_resids_kernel,
        "small_resids",
        [VMEM] * 6,
        [RESULT] * 2,
        [shape_of(acc7.shape), shape_of(acc8.shape)],
    )(moment_low, head, acc7, noise7, acc8, noise8)
    grams = [shape_of((h1, h1)), shape_of((2 * LANE, 2 * LANE))]

    def beside_last(trio, one3):
        four, again = relay(trio, one3, (moment,))
        early = call(
            functools.partial(early_kernel, sizes),
            "early_grams",
            [VMEM],
            [VMEM] * 2,
            grams,
            megabytes=8,
        )(four)
        momenta = call(
            functools.partial(momenta_kernel, sizes),
            "momenta",
            [VMEM] * 2,
            [HBM, HBM, RESULT, VMEM, VMEM],
            [
                shape_of(moment6.shape),
                shape_of(moment7.shape),
                shape_of(moment8.shape[::-1]),
                shape_of(moment6.shape),
                shape_of((2 * rows7 + rows8, 2 * LANE)),
            ],
            [pltpu.VMEM(moment7.shape, F32), pltpu.SemaphoreType.DMA((3,))],
        )(again, swap(again, grp_perm(1)))

        def begun(trio4, other_four):
            middle = call(
                functools.partial(middle_kernel, sizes),
                "middle_grams",
                [VMEM] * 4,
                [VMEM] * 4,
                grams * 2,
                megabytes=8,
            )(*early, trio4, other_four)
            return [momenta[3], middle[0], middle[2], *middle, *momenta]

        return four, begun

    moments, done = gather_halves(
        moment_low, [(HBM, new_resid6), (HBM, new_resid8)], beside_last
    )
    middle, (mom6, mom7, mom8, near6, near78) = done[3:7], done[7:]
    late = call(
        functools.partial(late_kernel, sizes),
        "late_grams",
        [VMEM] * 6,
        [VMEM] * 4,
        grams * 2,
        megabytes=8,
    )(*middle, moments[2], moments[4])

    updated = call(
        functools.partial(update_kernel, sizes),
        "update",
        [VMEM] * 10,
        [RESULT] * 6,
        [
            shape_of(weight6.shape),
            shape_of(weight7.shape),
            shape_of(weight8.shape[::-1]),
            shape_of(weight6.shape, BF16),
            shape_of(weight7.shape, BF16),
            shape_of(weight8.shape[::-1], BF16),
        ],
        megabytes=16,
    )(*late, moments[5], near6, near78, weight6, weight7, weight8.T)
    new6, new7, new8, low6, low7, low8 = updated
    return (
        new6,
        new7,
        new8.T,
        low6,
        low7,
        low8.T,
        mom6,
        mom7,
        mom8.T,
        new_resid6,
        new_resid7.T,
        new_resid8.T,
        *flat,
        *[array.reshape(()) for array in totals[3:]],
    )


def on_device(*arrays):
    (ins, h1), (_, h2), (_, classes) = [array.shape for array in arrays[9:12]]
    rows6, rows7, rows8 = [array.shape[0] for array in arrays[3:6]]
    paired = (
        (lax.axis_size("grp"), lax.axis_size("wide")) == (4, 8)
        and h1 == 3 * LANE
        and LANE < h2 < 2 * LANE
        and h2 + classes <= 2 * LANE
        and rows6 % 32 == 0
        and rows7 == rows8 * 2
        and rows8 % 24 == 0
        and ins % (2 * LANE) == 0
        and 16 * rows7 // 2 == h1
    )
    return (paired_plan if paired else general_plan)(*arrays)


def solution(mesh):
    split_both = P(BOTH, None)
    split_wide = P("wide", None)
    return jax.shard_map(
        on_device,
        mesh=mesh,
        in_specs=(
            split_both,
            P(BOTH),
            P(BOTH),
            *[split_wide] * 6,
            *[split_both] * 6,
            P(),
            P(),
            P(),
        ),
        out_specs=(*[split_wide] * 9, *[split_both] * 3, P(), P(), P(), P(), P()),
        check_vma=False,
    )
```
